32 devices in a mesh: seq: 4 (over y, x), head: 8 (over z, core).
Axes of the slice: x: 2, y: 2, z: 4, core: 2. Of those that a mesh axis runs over, the one named last changes fastest.
Arguments:
- pre_x: bfloat16 [4096, 8192], P('seq', 'head'), may hold values from -6 to 6
- pre_bc: bfloat16 [4096, 256], P('seq'), may hold values from -6 to 6
- conv_x: float32 [4, 8192], P(None, 'head'), may hold values from -3 to 3
- conv_bc: float32 [4, 256], replicated, may hold values from -3 to 3
- log_decay: float32 [128, 4096], P('head', 'seq'), may hold values from -1.5 to 0
- lengths: int32 [4], replicated, may hold values from 1 to 2048, 4096 in all
- grad_out: bfloat16 [4096, 8192], P('seq', 'head'), may hold values from -0.119628906 to 0.119628906
Outputs:
- grad_pre_x: float32 [4096, 8192], P('seq', 'head')
- grad_pre_bc: float32 [4096, 256], P(('seq', 'head'))
- grad_log_decay: float32 [128, 4096], P('head', 'seq')
The draws below stay inside these ranges and needn't reach their ends.
Inputs may be any that keep to these rules, and one draw needn't show every extreme that they name: `lengths`: the 4 counts sum to 4096.
All inputs are finite; a program needn't handle non-finite values.
Results may differ from the reference program's by a relative error of at most 0.0003.
Values may be sent and summed in bfloat16 or wider, within the bound.
No kernel may reach another device: no remote copies, remote signals or barrier semaphores. Data moves between devices by JAX's collectives and lax.ppermute only.
A program may use at most 192 MiB of HBM per device.

```python
import math
import jax
import jax.numpy as jnp
import numpy as np
from jax import lax

HEAD_COUNT_TOTAL = 128
P_SIZE = 64
N = 128
K = 4
NOTES = 4
BLOCK = 256
PACKED_LENGTH = 4096
HP = 8192


def draw_log_decay(key, part):
    random_keys = jax.random.split(jax.random.fold_in(key, 7), 6)
    slow_share = 0.5
    slow = jax.random.uniform(random_keys[0], (HEAD_COUNT_TOTAL,)) < slow_share
    slow_rate = jnp.exp(jax.random.uniform(random_keys[1], (HEAD_COUNT_TOTAL,), jnp.float32, jnp.log(0.1), jnp.log(1.0))) / PACKED_LENGTH
    fast_rate = jnp.exp(jax.random.uniform(random_keys[2], (HEAD_COUNT_TOTAL,), jnp.float32, jnp.log(1.0 / 50.0), jnp.log(1.0 / 30.0)))
    decay_speed = jnp.where(slow, slow_rate, fast_rate)
    coarse_value = jnp.exp(jax.random.uniform(random_keys[3], (HEAD_COUNT_TOTAL, PACKED_LENGTH), jnp.float32, jnp.log(0.5), jnp.log(2.0)))
    cluster_locations = jax.random.randint(random_keys[4], (6,), 0, PACKED_LENGTH)
    cluster_loss = jax.random.uniform(random_keys[5], (HEAD_COUNT_TOTAL, 6), jnp.float32, 0.2, 0.5)
    locations = jnp.arange(PACKED_LENGTH)
    cluster_groups = jnp.zeros((HEAD_COUNT_TOTAL, PACKED_LENGTH), jnp.float32)
    for token_index in range(6):
        matched = (locations == cluster_locations[token_index]).astype(jnp.float32)
        cluster_groups = cluster_groups + jnp.log(1.0 - cluster_loss[:, token_index])[:, None] * matched[None, :]
    return (-(decay_speed[:, None] * coarse_value) + cluster_groups).astype(jnp.float32)


def strengthened(array, stream_key, source, target, blocks, factor):
    def block_of(position):
        return (jnp.arange(array.shape[position]) // (array.shape[position] // blocks)).reshape((-1,) + (1,) * (array.ndim - 1 - position))

    one_side = jax.random.permutation(stream_key, blocks)[block_of(target)]
    second = (block_of(target) + blocks // 2) % blocks
    return jnp.where((block_of(source) == one_side) | (block_of(source) == second), factor * array, array)


def level_of(stream_key, shape, shards, smallest, top_value):
    loudness, own = 1.0, jax.random.fold_in(stream_key, 6)
    for position, blocks in shards:
        heights = jnp.exp(jax.random.uniform(jax.random.fold_in(own, position), (blocks,), jnp.float32, smallest / len(shards), top_value / len(shards)))
        loudness = loudness * jnp.repeat(heights, shape[position] // blocks).reshape([-1 if axis == position else 1 for axis in range(len(shape))])
    return loudness


def profile(count, total, most, skew):
    weights = [(1 << 20) // math.isqrt(rank ** skew) + 1 for rank in range(2, count + 1)]
    spare, counts = total - most - (count - 1), [1] * (count - 1)
    while spare > 0:
        candidates = [i for i in range(count - 1) if counts[i] < most]
        whole, left = sum([weights[i] for i in candidates]), spare
        for i in candidates:
            addition = min(most - counts[i], max(1, left * weights[i] // whole), spare)
            counts[i] = counts[i] + addition
            spare = spare - addition
    return np.array([most] + counts)


def ragged(stream_key, number_of, total, most, slope):
    if number_of == 2:
        one = jax.random.randint(stream_key, (), max(1, total - most), min(most, total - 1) + 1)
        return jnp.stack([one, total - one])
    tallies = jnp.asarray(profile(number_of, total, most, slope), jnp.int32)
    couples = (number_of - 1) // 2
    donor, receiver = tallies[1:1 + 2 * couples:2], tallies[2:2 + 2 * couples:2]
    slack = jnp.minimum(donor - 1, most - receiver)
    moved = jax.random.randint(jax.random.fold_in(stream_key, 1), (couples,), 0, 1 << 20) % (slack + 1)
    tallies = tallies.at[1:1 + 2 * couples:2].set(donor - moved).at[2:2 + 2 * couples:2].set(receiver + moved)
    return tallies[jax.random.permutation(jax.random.fold_in(stream_key, 2), number_of)]


def normal_values(own_key, shape, scale, most, cuts=(), held_as=jnp.bfloat16):
    values = jax.random.normal(own_key, shape, jnp.float32) * scale
    if len(cuts) > 0:
        values = level_of(own_key, shape, cuts, -0.22, 0.18) * values
    return jnp.clip(values, min=-most, max=most).astype(held_as)


def bell_draw_with(stream_key, dims, spread, reach, cuts, heavy, held_as=jnp.bfloat16):
    values = spread * jax.random.normal(stream_key, dims, jnp.float32)
    if cuts:
        values = values * level_of(stream_key, dims, cuts, -0.22, 0.18)
    return jnp.clip(strengthened(values, jax.random.fold_in(stream_key, 3), *heavy), -reach, reach).astype(held_as)


def setup_inputs(seed: int = 0) -> dict:
    arg_keys = jax.random.split(jax.random.key(seed), 8)
    return {
        "pre_x": normal_values(arg_keys[0], (PACKED_LENGTH, HP), 1.0, 6.0, ((0, 4), (1, 8))),
        "pre_bc": normal_values(arg_keys[1], (PACKED_LENGTH, 2 * N), 1.0, 6.0, ((0, 4),)),
        "conv_x": normal_values(arg_keys[2], (K, HP), 0.5, 3.0, ((1, 8),), jnp.float32),
        "conv_bc": normal_values(arg_keys[3], (K, 2 * N), 0.5, 3.0, (), jnp.float32),
        "log_decay": draw_log_decay(jax.random.fold_in(arg_keys[7], 71), 0),
        "lengths": ragged(arg_keys[5], NOTES, PACKED_LENGTH, PACKED_LENGTH // 2, 2).astype(jnp.int32),
        "grad_out": bell_draw_with(arg_keys[6], (PACKED_LENGTH, HP), 0.02, 0.119628906, ((0, 4), (1, 8)), (1, 0, 8, 2.0)),
    }


precise = lax.Precision.HIGHEST

def matmul(left, right):
    return jnp.dot(left, right, precision=precise, preferred_element_type=jnp.float32)

def note_index(positions, lengths):
    starts = jnp.cumsum(lengths) - lengths
    hits = (positions[:, None] >= starts[None, :]).astype(jnp.int32)
    return (lax.optimization_barrier(jnp.sum(hits, axis=1)) - 1).astype(jnp.int32)

def block_edges(log_block, note_block, note_before):
    cumul = jnp.cumsum(log_block)
    entry = jnp.exp(cumul) * (note_block == note_before)
    leave = jnp.exp(cumul[-1] - cumul) * (note_block == note_block[-1])
    through = jnp.exp(cumul[-1]) * (note_block[-1] == note_before)
    return (cumul, entry, leave, through)

def block_forward(state, x_block, b_block, c_block, log_block, note_block, note_before):
    cumul, entry, leave, through = block_edges(log_block, note_block, note_before)
    length = note_block.shape[0]
    lower = jnp.arange(length)[:, None] >= jnp.arange(length)[None, :]
    linked = lower & (note_block[:, None] == note_block[None, :])
    decay_matrix = jnp.exp(jnp.where(linked, cumul[:, None] - cumul[None, :], 0.0)) * linked
    scores = matmul(c_block, b_block.T) * decay_matrix
    output = matmul(scores, x_block) + entry[:, None] * matmul(c_block, state.T)
    updated = through * state + matmul((x_block * leave[:, None]).T, b_block)
    return (output, updated)

def head_forward(state, x_head, b_blocks, c_blocks, log_head, note_blocks, befores):

    def advance(carry, block):
        output, updated = block_forward(carry, *block)
        return (updated, output)
    final, outputs = lax.scan(advance, state, (x_head, b_blocks, c_blocks, log_head, note_blocks, befores))
    return (outputs, final)

def conv_forward(extended, weights, note_ext):
    width = weights.shape[0]
    count = extended.shape[0] - width + 1
    result = jnp.zeros((count, extended.shape[1]), jnp.float32)
    for k in range(width):
        linked = note_ext[k:k + count] == note_ext[width - 1:width - 1 + count]
        result = result + weights[k][None, :] * extended[k:k + count] * linked[:, None]
    return result

def reference(pre_x, pre_bc, conv_x, conv_bc, log_decay, lengths, grad_out):
    rim_width = K - 1
    note_ext = note_index(jnp.arange(-rim_width, PACKED_LENGTH).astype(jnp.int32), lengths)
    note_ids = note_ext[rim_width:]
    block_count = PACKED_LENGTH // BLOCK
    note_blocks = note_ids.reshape(block_count, BLOCK)
    befores = jnp.concatenate([jnp.full((1,), -1, jnp.int32), note_blocks[:-1, -1]])

    def forward(in_x, in_bc, log_rates):
        pad_x = jnp.zeros((rim_width, in_x.shape[1]), jnp.float32)
        pad_bc = jnp.zeros((rim_width, in_bc.shape[1]), jnp.float32)
        u_x = conv_forward(jnp.concatenate([pad_x, in_x]), conv_x, note_ext)
        u_bc = conv_forward(jnp.concatenate([pad_bc, in_bc]), conv_bc, note_ext)
        v_x = jax.nn.silu(u_x)
        v_bc = jax.nn.silu(u_bc)
        x_heads = v_x.reshape(block_count, BLOCK, HEAD_COUNT_TOTAL, P_SIZE).transpose(2, 0, 1, 3)
        b_blocks = v_bc[:, :N].reshape(block_count, BLOCK, N)
        c_blocks = v_bc[:, N:].reshape(block_count, BLOCK, N)
        log_blocks = log_rates.reshape(HEAD_COUNT_TOTAL, block_count, BLOCK)

        def one_head(paired):
            start_state = jnp.zeros((P_SIZE, N), jnp.float32)
            return head_forward(start_state, paired[0], b_blocks, c_blocks, paired[1], note_blocks, befores)[0]
        outputs = lax.map(jax.checkpoint(one_head), (x_heads, log_blocks))
        return outputs.transpose(1, 2, 0, 3).reshape(PACKED_LENGTH, HEAD_COUNT_TOTAL * P_SIZE)
    _, pull = jax.vjp(forward, pre_x.astype(jnp.float32), pre_bc.astype(jnp.float32), log_decay)
    grad_x, grad_bc, grad_log = pull(grad_out.astype(jnp.float32))
    return (grad_x, grad_bc, grad_log)
```

```python
import functools
import jax
import jax.numpy as jnp
from jax import lax
from jax.experimental import pallas as pl
from jax.experimental.pallas import tpu as pltpu
from jax.sharding import PartitionSpec as P

P_SIZE = 64
N = 128
K = 4
CHUNK = 64
LANES = 128
f32 = jnp.float32
bf16 = jnp.bfloat16
NN = (((1,), (0,)), ((), ()))
NT = (((1,), (1,)), ((), ()))
TN = (((0,), (0,)), ((), ()))
VMEM_LIMIT = 56 * 1024 * 1024


def split(value):
    high = value.astype(bf16)
    return high, (value - high.astype(f32)).astype(bf16)


def dot(left, right, dims=NN):
    return lax.dot_general(left, right, dims, preferred_element_type=f32)


def thirds(value):
    high, low = split(value)
    return high, low, (value - high.astype(f32) - low.astype(f32)).astype(bf16)


def exact(left, right, dims=NN):
    if isinstance(left, tuple):
        return dot(left[0], right, dims) + dot(left[1], right, dims) + dot(left[2], right, dims)
    return dot(left, right[0], dims) + dot(left, right[1], dims) + dot(left, right[2], dims)


def dot3(left, right, dims=NN):
    return (
        dot(left[0], right[0], dims) + dot(left[0], right[1], dims) + dot(left[1], right[0], dims)
    )


def rows_iota(shape):
    return lax.broadcasted_iota(jnp.int32, shape, 0)


def cols_iota(shape):
    return lax.broadcasted_iota(jnp.int32, shape, 1)


def note_of(position, lens_ref):
    first = lens_ref[0]
    second = first + lens_ref[1]
    third = second + lens_ref[2]
    one = lambda flag: jnp.where(flag, 1, 0)
    return one(position >= 0) + one(position >= first) + one(position >= second) + one(
        position >= third
    )


def widen(block, width):
    return block if width == LANES else jnp.concatenate([block] * (width // LANES), axis=1)


def conv_ahead(ext_ref, taps_ref, rows, start, lens_ref, width):
    position = start + rows_iota((rows, LANES))
    here = note_of(position, lens_ref)
    total = ext_ref[8 : 8 + rows, :] * taps_ref[K - 1 : K, :]
    for lag in range(1, K):
        linked = jnp.where(note_of(position - lag, lens_ref) == here, 1.0, 0.0)
        total = total + ext_ref[8 - lag : 8 - lag + rows, :] * taps_ref[K - 1 - lag : K - lag, :] * widen(linked, width)
    return total


def conv_back(ext_ref, taps_ref, rows, start, lens_ref, width):
    position = start + rows_iota((rows, LANES))
    here = note_of(position, lens_ref)
    total = ext_ref[0:rows, :] * taps_ref[K - 1 : K, :]
    for lag in range(1, K):
        linked = jnp.where(note_of(position + lag, lens_ref) == here, 1.0, 0.0)
        total = total + ext_ref[lag : lag + rows, :] * taps_ref[K - 1 - lag : K - lag, :] * widen(linked, width)
    return total


def silu_and_slope(u):
    sigma = 1.0 / (1.0 + jnp.exp(-u))
    value = u * sigma
    return value, sigma + value * (1.0 - sigma)


def expander(width, heads, channels, group):
    row = rows_iota((width, channels)) - group * 3 * heads
    own = cols_iota((width, channels)) // P_SIZE
    inside = (row >= 0) & (row < 3 * heads)
    return jnp.where(inside & (row % heads == own), 1.0, 0.0).astype(bf16)


def head_summer(channels):
    same = rows_iota((channels, LANES)) // P_SIZE == cols_iota((channels, LANES))
    return jnp.where(same, 1.0, 0.0).astype(bf16)


def prep_kernel(
    lens_ref, start_ref, pre_ref, halo_ref, taps_ref, log_ref,
    hi_ref, lo_ref, slope_ref, scale_ref, kappa_ref, through_ref,
    ext, padded,
):
    tokens = pre_ref.shape[0]
    heads = log_ref.shape[0]
    channels = kappa_ref.shape[1]
    chunks = tokens // CHUNK
    start = start_ref[0]
    ext[0:8, :] = halo_ref[8:16, :].astype(f32)
    ext[8:, :] = pre_ref[...].astype(f32)
    value, slope = silu_and_slope(conv_ahead(ext, taps_ref, tokens, start, lens_ref, 2 * N))
    high, low = split(value)
    hi_ref[...] = high
    lo_ref[...] = low
    slope_ref[...] = slope

    padded[...] = jnp.zeros_like(padded)
    padded[0:heads, :] = log_ref[...]
    square = (LANES, LANES)
    row, col = rows_iota(square), cols_iota(square)
    same = row // CHUNK == col // CHUNK
    one = lambda flag: jnp.where(flag, 1.0, 0.0)
    inner = one(same & (col <= row)) - one(same & (col % CHUNK < CHUNK // 2))
    sums = jnp.concatenate(
        [inner, one(col <= row), one(col > row), jnp.ones(square, f32)], axis=0
    ).astype(bf16)
    blocks = tokens // LANES
    parts = thirds(padded[...])
    tables = [
        exact(sums, tuple(part[:, b * LANES : (b + 1) * LANES] for part in parts), NT)
        for b in range(blocks)
    ]
    inners, aheads, behinds, totals = (
        [table[i * LANES : (i + 1) * LANES, :] for table in tables] for i in range(4)
    )
    before = jnp.zeros(square, f32)
    offsets = []
    for b in range(blocks):
        offsets.append(before)
        before = before + totals[b]
    after = jnp.zeros(square, f32)
    note_before = note_of(start - 1, lens_ref)
    note_last = note_of(start + tokens - 1, lens_ref)
    scale_ref[...] = jnp.zeros_like(scale_ref)
    for b in reversed(range(blocks)):
        note = note_of(start + b * LANES + row, lens_ref)
        entry = jnp.exp(aheads[b] + offsets[b]) * one(note == note_before)
        leave = jnp.exp(behinds[b] + after) * one(note == note_last)
        after = after + totals[b]
        rows = slice(b * LANES, (b + 1) * LANES)
        for group, scale in enumerate((jnp.exp(inners[b]), jnp.exp(-inners[b]), entry, leave)):
            for place, part in enumerate(thirds(scale)):
                at = (3 * group + place) * heads
                scale_ref[rows, at : at + heads] = part[:, 0:heads]
    spread = one(
        rows_iota((LANES, channels)) == cols_iota((LANES, channels)) // P_SIZE
    ).astype(bf16)
    half = CHUNK // 2
    chunk = rows_iota((chunks, tokens)) * CHUNK + half
    col = cols_iota((chunks, tokens))
    for place in range(2):
        begin = chunk + place * half
        steps = exact(one((col >= begin) & (col < begin + half)).astype(bf16), parts, NT)
        kappa_ref[place * chunks : (place + 1) * chunks, :] = exact(thirds(jnp.exp(steps)), spread)
    whole = jnp.exp(before[0:8, :]) * one(note_before == note_last)
    through_ref[...] = exact(thirds(whole), spread)


def adjoint_kernel(
    grad_ref, scale_ref, hi_ref, lo_ref, through_ref, gh_ref, gl_ref, send_ref, spread, *, heads
):
    channels = grad_ref.shape[1]

    @pl.when(pl.program_id(0) == 0)
    def _():
        spread[...] = expander(spread.shape[0], heads, channels, 2)
        send_ref[...] = jnp.zeros_like(send_ref)
        send_ref[N : N + 8, :] = through_ref[...]

    scaled = grad_ref[...].astype(f32) * dot(scale_ref[...], spread[...])
    parts = split(scaled)
    gh_ref[...], gl_ref[...] = parts
    send_ref[0:N, :] += dot3((hi_ref[:, N:], lo_ref[:, N:]), parts, TN)


def state_kernel(
    lens_ref, start_ref, pre_ref, halo_ref, taps_ref, scale_ref, hi_ref, lo_ref, through_ref,
    x_ref, slope_ref, xh_ref, xl_ref, send_ref, spread, ext, *, heads
):
    rows, channels = pre_ref.shape
    step = pl.program_id(0)

    @pl.when(step == 0)
    def _():
        spread[...] = expander(spread.shape[0], heads, channels, 3)
        send_ref[...] = jnp.zeros_like(send_ref)
        send_ref[N : N + 8, :] = through_ref[...]
        ext[0:8, :] = halo_ref[8:16, :].astype(f32)

    @pl.when(step > 0)
    def _():
        ext[0:8, :] = ext[rows : rows + 8, :]

    ext[8:, :] = pre_ref[...].astype(f32)
    u = conv_ahead(ext, taps_ref, rows, start_ref[0] + step * rows, lens_ref, channels)
    value, slope = silu_and_slope(u)
    x_ref[...] = value
    slope_ref[...] = slope
    parts = split(value * dot(scale_ref[...], spread[...]))
    xh_ref[...], xl_ref[...] = parts
    send_ref[0:N, :] += dot3((hi_ref[:, :N], lo_ref[:, :N]), parts, TN)


def local_kernel(
    lens_ref, start_ref, x_ref, grad_ref, scale_ref, hi_ref, lo_ref, kappa_ref,
    dx_ref, dbc_ref, rate_ref,
    xh, xl, gh, gl, product, score_h, score_l, state, spread_r, spread_q, summer, *, heads
):
    phase, step = pl.program_id(0), pl.program_id(1)
    chunks = pl.num_programs(1)
    channels = x_ref.shape[1]
    chunk = jnp.where(phase == 0, step, chunks - 1 - step)
    rows = pl.ds(pl.multiple_of(chunk * CHUNK, CHUNK), CHUNK)

    @pl.when((phase == 0) & (step == 0))
    def _():
        spread_r[...] = expander(spread_r.shape[0], heads, channels, 0)
        spread_q[...] = expander(spread_q.shape[0], heads, channels, 1)
        summer[...] = head_summer(channels)

    @pl.when(step == 0)
    def _():
        state[...] = jnp.zeros_like(state)

    first = start_ref[0] + chunk * CHUNK
    note_before = note_of(first - 1, lens_ref)
    note_last = note_of(first + CHUNK - 1, lens_ref)
    keep = jnp.where(note_before == note_last, 1.0, 0.0)
    note = note_of(first + rows_iota((CHUNK, LANES)), lens_ref)
    enters = note == note_before
    leaves = note == note_last
    square = (CHUNK, CHUNK)
    row, col = rows_iota(square), cols_iota(square)
    linked = note_of(first + row, lens_ref) == note_of(first + col, lens_ref)
    b_parts = (hi_ref[:, :N], lo_ref[:, :N])
    c_parts = (hi_ref[:, N:], lo_ref[:, N:])
    pick = lambda flag, parts: tuple(
        jnp.where(flag, part.astype(f32), 0.0).astype(bf16) for part in parts
    )
    b_leaving, c_entering = pick(leaves, b_parts), pick(enters, c_parts)

    def advance(fresh, place):
        near = (state[...] * keep + fresh) * kappa_ref[pl.ds(place, 1), :]
        state[...] = near * kappa_ref[pl.ds(chunks + place, 1), :]

    @pl.when(phase == 0)
    def _():
        x_scaled = x_ref[...] * dot(scale_ref[...], spread_q[...])
        g_scaled = grad_ref[...].astype(f32) * dot(scale_ref[...], spread_r[...])
        x_parts, g_parts = split(x_scaled), split(g_scaled)
        xh[rows, :], xl[rows, :] = x_parts
        gh[rows, :], gl[rows, :] = g_parts
        s_parts = split(state[...])
        scores = jnp.where(linked & (col < row), dot3(c_parts, b_parts, NT), 0.0)
        left = [jnp.concatenate(p, axis=1) for p in zip(c_entering, split(scores))]
        right = [jnp.concatenate(p, axis=0) for p in zip(s_parts, x_parts)]
        product[rows, :] = g_scaled * dot3(left, right)
        inner = dot3(g_parts, right, NT)
        d_scores = split(jnp.where(linked & (col <= row), inner[:, N:], 0.0))
        score_h[rows, :], score_l[rows, :] = d_scores
        dbc_ref[rows, N:] = jnp.where(enters, inner[:, :N], 0.0) + dot3(d_scores, b_parts)
        fresh = dot3(b_leaving, x_parts, TN)
        advance(fresh, chunk)

    @pl.when(phase == 1)
    def _():
        x_parts = (xh[rows, :], xl[rows, :])
        g_parts = (gh[rows, :], gl[rows, :])
        a_parts = split(state[...])
        scores = jnp.where(linked & (row < col), dot3(b_parts, c_parts, NT), 0.0)
        left = [jnp.concatenate(p, axis=1) for p in zip(b_leaving, split(scores))]
        right = [jnp.concatenate(p, axis=0) for p in zip(a_parts, g_parts)]
        dx = dot3(left, right)
        full = lambda parts: parts[0].astype(f32) + parts[1].astype(f32)
        own = jnp.sum(full(b_parts) * full(c_parts), axis=1, keepdims=True)
        dx_ref[...] = dx * dot(scale_ref[...], spread_q[...]) + own * grad_ref[...].astype(f32)
        rate = split(product[rows, :] - full(x_parts) * dx)
        rate_ref[rows, :] = dot(rate[0], summer[...]) + dot(rate[1], summer[...])
        inner = dot3(x_parts, a_parts, NT)
        d_scores = (score_h[rows, :], score_l[rows, :])
        dbc_ref[rows, :N] = jnp.where(leaves, inner, 0.0) + dot3(d_scores, c_parts, TN)
        fresh = dot3(c_entering, g_parts, TN)
        advance(fresh, jnp.maximum(chunk - 1, 0))


def joined(messages):
    total = jnp.zeros((N, messages[0].shape[1]), f32)
    for message in reversed(messages):
        total = message[0:N, :] + message[N : N + 1, :] * total
    return total


def shared_kernel(lens_ref, start_ref, *refs, count):
    forward, backward = refs[: count - 1], refs[count - 1 : 2 * count - 2]
    (
        own_ref, gh_ref, gl_ref, xh_ref, xl_ref, dbc_ref, slope_ref, taps_ref,
        out_ref, head_ref, s2_ref, a2_ref, end_ref, ext,
    ) = refs[2 * count - 2 :]
    step = pl.program_id(0)
    rows = gh_ref.shape[0]
    tokens = out_ref.shape[0]

    @pl.when(step == 0)
    def _():
        state, adjoint = joined(forward), joined(backward)
        s2_ref[0:N, :], s2_ref[N:, :] = split(state)
        a2_ref[0:N, :], a2_ref[N:, :] = split(adjoint)
        last = own_ref[0:N, :] + own_ref[N : N + 1, :] * state
        end_ref[...] = jnp.broadcast_to(
            jnp.sum(last * adjoint, axis=0, keepdims=True), end_ref.shape
        )
        ext[tokens:, :] = jnp.zeros((8, 2 * N), f32)

    def pull(high, low, both):
        most = dot(high, both[...], NT)
        return most[:, :N] + most[:, N:] + dot(low, both[0:N, :], NT)

    at = pl.ds(pl.multiple_of(step * rows, rows), rows)
    for_c = pull(gh_ref[...], gl_ref[...], s2_ref)
    for_b = pull(xh_ref[...], xl_ref[...], a2_ref)
    ext[at, :] = (dbc_ref[...] + jnp.concatenate([for_b, for_c], axis=1)) * slope_ref[...]

    @pl.when(step == pl.num_programs(0) - 1)
    def _():
        out_ref[...] = conv_back(ext, taps_ref, tokens, start_ref[0], lens_ref, 2 * N)
        head_ref[...] = ext[0:8, :]


def final_kernel(
    lens_ref, start_ref, gh_ref, gl_ref, xh_ref, xl_ref, hi_ref, lo_ref, scale_ref,
    dx_ref, slope_ref, rate_ref, s2_ref, a2_ref, end_ref, taps_ref,
    out_ref, head_ref, log_ref, spread, summer, ext, carry, *, heads
):
    step = pl.program_id(0)
    steps = pl.num_programs(0)
    rows, channels = gh_ref.shape

    @pl.when(step == 0)
    def _():
        spread[...] = expander(spread.shape[0], heads, channels, 3)
        summer[...] = head_summer(channels)
        ext[rows:, :] = jnp.zeros((8, channels), f32)
        carry[...] = jnp.zeros_like(carry)

    @pl.when(step > 0)
    def _():
        ext[rows:, :] = ext[0:8, :]

    def push(high, low, both):
        return dot(high, both[0:N, :]) + dot(high, both[N:, :]) + dot(low, both[0:N, :])

    full = lambda high, low: high[...].astype(f32) + low[...].astype(f32)
    y = push(hi_ref[:, N:], lo_ref[:, N:], s2_ref)
    dx = push(hi_ref[:, :N], lo_ref[:, :N], a2_ref)
    rate = split(full(gh_ref, gl_ref) * y - full(xh_ref, xl_ref) * dx)
    rates = rate_ref[...] + dot(rate[0], summer[...]) + dot(rate[1], summer[...])
    last = rows_iota((rows, LANES)) == rows - 1
    beyond = exact(thirds(end_ref[...]), summer[...])[0:1, :]
    rates = rates + jnp.where(last & (step == 0), beyond, 0.0)
    later = rows_iota((rows, rows)) >= cols_iota((rows, rows))
    ones = jnp.ones((rows, LANES), f32)
    marks = jnp.concatenate([jnp.where(later, 1.0, 0.0), ones], axis=1).astype(bf16)
    sums = exact(thirds(rates), marks, TN)
    log = sums[:, :rows] + widen(carry[...], rows)
    log_ref[...] = log[0:heads, :]
    carry[...] += sums[:, rows:]
    ext[0:rows, :] = (dx_ref[...] + dx * dot(scale_ref[...], spread[...])) * slope_ref[...]
    first = start_ref[0] + (steps - 1 - step) * rows
    out_ref[...] = conv_back(ext, taps_ref, rows, first, lens_ref, channels)

    @pl.when(step == steps - 1)
    def _():
        head_ref[...] = ext[0:8, :]


def shifted(value, axis, steps):
    count = lax.axis_size(axis)
    initial, last = (max(0, -steps), min(count, count - steps))
    return lax.ppermute(value, axis, [(source, source + steps) for source in range(initial, last)])


def head_scatter(value):
    count = lax.axis_size("head")
    if count & (count - 1):
        return lax.psum_scatter(value, "head", scatter_dimension=0, tiled=True)
    mine = lax.axis_index("head")
    rows, width = value.shape
    value = value.reshape(count, rows // count, width)
    bit = 1
    while bit < count:
        pairs = value.reshape(value.shape[0] // 2, 2, rows // count, width)
        side = (mine // bit) % 2
        keep = lax.dynamic_index_in_dim(pairs, side, 1, keepdims=False)
        give = lax.dynamic_index_in_dim(pairs, 1 - side, 1, keepdims=False)
        value = keep + lax.ppermute(give, "head", [(i, i ^ bit) for i in range(count)])
        bit *= 2
    return value.reshape(rows // count, width)


def spill(next_rows, taps, position, lengths):
    ends = jnp.cumsum(lengths)
    note = lambda p: jnp.sum((p[:, None] >= ends[None, :]).astype(jnp.int32), axis=1)
    rows = position + jnp.arange(-8, 0)
    total = jnp.zeros_like(next_rows)
    for lag in range(1, K):
        moved = jnp.pad(next_rows[:lag], ((8 - lag, 0), (0, 0)))
        linked = (note(rows + lag) == note(rows)).astype(f32)
        total = total + moved * taps[K - 1 - lag][None, :] * linked[:, None]
    return total


def local(pre_x, pre_bc, conv_x, conv_bc, log_decay, lengths, grad_out):
    tokens, channels = pre_x.shape
    heads = log_decay.shape[0]
    count = lax.axis_size("seq")
    chunks = tokens // CHUNK
    big = 256
    width = -(-12 * heads // LANES) * LANES
    start = (lax.axis_index("seq") * tokens).astype(jnp.int32).reshape(1)
    halo = shifted(jnp.concatenate([pre_x[-16:], pre_bc[-16:]], axis=1), "seq", 1)
    halo_x, halo_bc = halo[:, :channels], halo[:, channels:]
    shape = jax.ShapeDtypeStruct
    smem = pl.BlockSpec(memory_space=pltpu.SMEM)
    vmem = pl.BlockSpec(memory_space=pltpu.VMEM)
    params = pltpu.CompilerParams(vmem_limit_bytes=VMEM_LIMIT)

    hi, lo, slope_bc, scale, kappa, through = pl.pallas_call(
        prep_kernel,
        out_shape=(
            shape((tokens, 2 * N), bf16), shape((tokens, 2 * N), bf16), shape((tokens, 2 * N), f32),
            shape((tokens, width), bf16), shape((2 * chunks, channels), f32), shape((8, channels), f32),
        ),
        in_specs=[smem, smem, vmem, vmem, vmem, vmem],
        out_specs=(vmem,) * 6,
        scratch_shapes=[pltpu.VMEM((tokens + 8, 2 * N), f32), pltpu.VMEM((LANES, tokens), f32)],
        compiler_params=params,
    )(lengths, start, pre_bc, halo_bc, conv_bc, log_decay)

    by_rows = lambda rows, cols: pl.BlockSpec((rows, cols), lambda i: (i, 0))
    whole = lambda rows, cols: pl.BlockSpec((rows, cols), lambda *i: (0, 0))
    steps = tokens // big
    cost = lambda work: pl.CostEstimate(flops=work, bytes_accessed=tokens * channels * 16, transcendentals=0)
    wide = tokens * channels
    g_high, g_low, send_adjoint = pl.pallas_call(
        functools.partial(adjoint_kernel, heads=heads),
        grid=(steps,),
        out_shape=(
            shape((tokens, channels), bf16), shape((tokens, channels), bf16), shape((N + 8, channels), f32),
        ),
        in_specs=[
            by_rows(big, channels), by_rows(big, width), by_rows(big, 2 * N), by_rows(big, 2 * N),
            whole(8, channels),
        ],
        out_specs=(by_rows(big, channels), by_rows(big, channels), whole(N + 8, channels)),
        scratch_shapes=[pltpu.VMEM((width, channels), bf16)],
        compiler_params=params,
        cost_estimate=cost(wide * 1000),
    )(grad_out, scale, hi, lo, through)
    backward = [shifted(send_adjoint, "seq", -lag) for lag in range(1, count)]

    x, slope_x, x_high, x_low, send_state = pl.pallas_call(
        functools.partial(state_kernel, heads=heads),
        grid=(steps,),
        out_shape=(
            shape((tokens, channels), f32), shape((tokens, channels), f32),
            shape((tokens, channels), bf16), shape((tokens, channels), bf16),
            shape((N + 8, channels), f32),
        ),
        in_specs=[
            smem, smem, by_rows(big, channels), whole(16, channels), whole(K, channels),
            by_rows(big, width), by_rows(big, 2 * N), by_rows(big, 2 * N), whole(8, channels),
        ],
        out_specs=(by_rows(big, channels),) * 4 + (whole(N + 8, channels),),
        scratch_shapes=[pltpu.VMEM((width, channels), bf16), pltpu.VMEM((big + 8, channels), f32)],
        compiler_params=params,
        cost_estimate=cost(wide * 1000),
    )(lengths, start, pre_x, halo_x, conv_x, scale, hi, lo, through)
    forward = [shifted(send_state, "seq", lag) for lag in range(1, count)]

    two_way = lambda rows, cols: pl.BlockSpec(
        (rows, cols), lambda p, i: (jnp.where(p == 0, i, chunks - 1 - i), 0)
    )
    only_first = lambda rows, cols: pl.BlockSpec(
        (rows, cols), lambda p, i: (jnp.where(p == 0, i, chunks - 1), 0)
    )
    only_second = lambda rows, cols: pl.BlockSpec((rows, cols), lambda p, i: (chunks - 1 - p * i, 0))
    dx, dbc, rate = pl.pallas_call(
        functools.partial(local_kernel, heads=heads),
        grid=(2, chunks),
        out_shape=(
            shape((tokens, channels), f32), shape((tokens, 2 * N), f32), shape((tokens, LANES), f32),
        ),
        in_specs=[
            smem, smem, only_first(CHUNK, channels), two_way(CHUNK, channels), two_way(CHUNK, width),
            two_way(CHUNK, 2 * N), two_way(CHUNK, 2 * N), whole(2 * chunks, channels),
        ],
        out_specs=(only_second(CHUNK, channels), whole(tokens, 2 * N), whole(tokens, LANES)),
        scratch_shapes=[pltpu.VMEM((tokens, channels), bf16)] * 4
        + [
            pltpu.VMEM((tokens, channels), f32), pltpu.VMEM((tokens, CHUNK), bf16),
            pltpu.VMEM((tokens, CHUNK), bf16), pltpu.VMEM((N, channels), f32),
            pltpu.VMEM((width, channels), bf16), pltpu.VMEM((width, channels), bf16),
            pltpu.VMEM((channels, LANES), bf16),
        ],
        compiler_params=params,
        cost_estimate=cost(wide * 8000),
    )(lengths, start, x, grad_out, scale, hi, lo, kappa)

    part_bc, head_bc, s2, a2, end = pl.pallas_call(
        functools.partial(shared_kernel, count=count),
        grid=(steps,),
        out_shape=(
            shape((tokens, 2 * N), f32), shape((8, 2 * N), f32), shape((2 * N, channels), bf16),
            shape((2 * N, channels), bf16), shape((8, channels), f32),
        ),
        in_specs=[smem, smem]
        + [whole(N + 8, channels)] * (2 * count - 1)
        + [by_rows(big, channels)] * 4
        + [by_rows(big, 2 * N)] * 2
        + [whole(K, 2 * N)],
        out_specs=(
            whole(tokens, 2 * N), whole(8, 2 * N), whole(2 * N, channels), whole(2 * N, channels),
            whole(8, channels),
        ),
        scratch_shapes=[pltpu.VMEM((tokens + 8, 2 * N), f32)],
        compiler_params=params,
        cost_estimate=cost(wide * 1500),
    )(
        lengths, start, *forward, *backward, send_state, g_high, g_low, x_high, x_low, dbc, slope_bc,
        conv_bc,
    )
    after_bc = shifted(head_bc, "seq", -1)
    edge = start[0] + tokens
    part_bc = part_bc.at[-8:].add(spill(after_bc, conv_bc, edge, lengths))
    grad_pre_bc = head_scatter(part_bc)

    back_rows = lambda rows, cols: pl.BlockSpec((rows, cols), lambda i: (steps - 1 - i, 0))
    grad_pre_x, head_x, grad_log = pl.pallas_call(
        functools.partial(final_kernel, heads=heads),
        grid=(steps,),
        out_shape=(
            shape((tokens, channels), f32), shape((8, channels), f32), shape((heads, tokens), f32),
        ),
        in_specs=[smem, smem]
        + [back_rows(big, channels)] * 4
        + [back_rows(big, 2 * N)] * 2
        + [back_rows(big, width)]
        + [back_rows(big, channels)] * 2
        + [
            back_rows(big, LANES), whole(2 * N, channels), whole(2 * N, channels),
            whole(8, channels), whole(K, channels),
        ],
        out_specs=(
            back_rows(big, channels), whole(8, channels),
            pl.BlockSpec((heads, big), lambda i: (0, steps - 1 - i)),
        ),
        scratch_shapes=[
            pltpu.VMEM((width, channels), bf16), pltpu.VMEM((channels, LANES), bf16),
            pltpu.VMEM((big + 8, channels), f32), pltpu.VMEM((LANES, LANES), f32),
        ],
        compiler_params=params,
        cost_estimate=cost(wide * 1500),
    )(
        lengths, start, g_high, g_low, x_high, x_low, hi, lo, scale, dx, slope_x, rate, s2, a2, end,
        conv_x,
    )
    after_x = shifted(head_x, "seq", -1)
    grad_pre_x = grad_pre_x.at[-8:].add(spill(after_x, conv_x, edge, lengths))
    return (grad_pre_x, grad_pre_bc, grad_log)


def solution(mesh):
    placed = (
        P("seq", "head"),
        P("seq", None),
        P(None, "head"),
        P(),
        P("head", "seq"),
        P(),
        P("seq", "head"),
    )
    return jax.shard_map(
        local,
        mesh=mesh,
        in_specs=placed,
        out_specs=(P("seq", "head"), P(("seq", "head"), None), P("head", "seq")),
        check_vma=False,
    )
```

```python
import functools
import jax
import jax.numpy as jnp
from jax import lax
from jax.experimental import pallas as pl
from jax.experimental.pallas import tpu as pltpu
from jax.sharding import PartitionSpec as P

P_SIZE = 64
N = 128
K = 4
CHUNK = 64
LANES = 128
f32 = jnp.float32
bf16 = jnp.bfloat16
NN = (((1,), (0,)), ((), ()))
NT = (((1,), (1,)), ((), ()))
TN = (((0,), (0,)), ((), ()))
VMEM_LIMIT = 56 * 1024 * 1024


def split(value):
    high = value.astype(bf16)
    return high, (value - high.astype(f32)).astype(bf16)


def dot(left, right, dims=NN):
    return lax.dot_general(left, right, dims, preferred_element_type=f32)


def thirds(value):
    high, low = split(value)
    return high, low, (value - high.astype(f32) - low.astype(f32)).astype(bf16)


def exact(left, right, dims=NN):
    if isinstance(left, tuple):
        return dot(left[0], right, dims) + dot(left[1], right, dims) + dot(left[2], right, dims)
    return dot(left, right[0], dims) + dot(left, right[1], dims) + dot(left, right[2], dims)


def stack(*parts):
    return jnp.concatenate(parts, axis=0)


def dot3(left, right, dims=NN):
    rows = left[0].shape[0]
    most = dot(stack(*left), right[0], dims)
    return most[:rows] + most[rows:] + dot(left[0], right[1], dims)


def dot3_tn(left, right):
    return dot(stack(left[0], left[1], left[0]), stack(right[0], right[0], right[1]), TN)


def whole_of(parts):
    return parts[0].astype(f32) + parts[1].astype(f32)


def rows_iota(shape):
    return lax.broadcasted_iota(jnp.int32, shape, 0)


def cols_iota(shape):
    return lax.broadcasted_iota(jnp.int32, shape, 1)


def note_of(position, lens_ref):
    first = lens_ref[0]
    second = first + lens_ref[1]
    third = second + lens_ref[2]
    one = lambda flag: jnp.where(flag, 1, 0)
    return one(position >= 0) + one(position >= first) + one(position >= second) + one(
        position >= third
    )


def widen(block, width):
    return block if width == LANES else jnp.concatenate([block] * (width // LANES), axis=1)


def links(first, rows, sign, lens_ref):
    position = first + rows_iota((rows, LANES))
    here = note_of(position, lens_ref)
    return [
        jnp.where(note_of(position + sign * lag, lens_ref) == here, 1.0, 0.0) for lag in range(1, K)
    ]


def conv_tile(ext_ref, taps_ref, first, rows, over, linked, sign):
    total = ext_ref[first : first + rows, over] * taps_ref[K - 1 : K, over]
    for lag in range(1, K):
        moved = first + sign * lag
        tap = taps_ref[K - 1 - lag : K - lag, over]
        tap = tap if linked is None else tap * linked[lag - 1]
        total = total + ext_ref[moved : moved + rows, over] * tap
    return total


def conv_rows(ext_ref, taps_ref, first, rows, width, position, sign, lens_ref, emit):
    begins = [0, lens_ref[0], lens_ref[0] + lens_ref[1], lens_ref[0] + lens_ref[1] + lens_ref[2]]
    near = [(begin > position - K) & (begin < position + rows + K) for begin in begins]
    cut = near[0] | near[1] | near[2] | near[3]

    def body(linked):
        for c in range(0, width, LANES):
            over = slice(c, c + LANES)
            emit(over, conv_tile(ext_ref, taps_ref, first, rows, over, linked, sign))

    @pl.when(cut)
    def _():
        body(links(position, rows, sign, lens_ref))

    @pl.when(jnp.logical_not(cut))
    def _():
        body(None)


def silu_and_slope(u):
    sigma = 1.0 / (1.0 + jnp.exp(-u))
    value = u * sigma
    return value, sigma + value * (1.0 - sigma)


def expander(heads, channels, group):
    row = rows_iota((2 * LANES, channels)) % LANES
    own = cols_iota((2 * LANES, channels)) // P_SIZE
    return jnp.where(row == group * heads + own, 1.0, 0.0).astype(bf16)


def head_summer(channels):
    same = rows_iota((channels, LANES)) // P_SIZE == cols_iota((channels, LANES))
    return jnp.where(same, 1.0, 0.0).astype(bf16)


def scales_kernel(lens_ref, start_ref, log_ref, scale_ref, kappa_ref, through_ref, padded):
    heads, tokens = log_ref.shape
    channels = kappa_ref.shape[1]
    chunks = tokens // CHUNK
    start = start_ref[0]
    padded[...] = jnp.zeros_like(padded)
    for group in range(4):
        padded[group * heads : (group + 1) * heads, :] = log_ref[...]
    size = 2 * LANES
    square = (size, size)
    row, col = rows_iota(square), cols_iota(square)
    same = row // CHUNK == col // CHUNK
    one = lambda flag: jnp.where(flag, 1.0, 0.0)
    inner = one(same & (col <= row)) - one(same & (col % CHUNK < CHUNK // 2))
    sums = stack(inner, one(col <= row), one(col > row), jnp.ones((16, size), f32)).astype(bf16)
    blocks = tokens // size
    parts = thirds(padded[...])
    tables = [
        exact(sums, tuple(part[:, b * size : (b + 1) * size] for part in parts), NT)
        for b in range(blocks)
    ]
    totals = [table[3 * size : 3 * size + 1, :] for table in tables]
    offsets = [jnp.zeros((1, LANES), f32)]
    for total in totals:
        offsets.append(offsets[-1] + total)
    after = jnp.zeros((1, LANES), f32)
    note_before = note_of(start - 1, lens_ref)
    note_last = note_of(start + tokens - 1, lens_ref)
    shape = (size, LANES)
    group = cols_iota(shape) // heads
    for b in reversed(range(blocks)):
        near, ahead, behind = (tables[b][i * size : (i + 1) * size, :] for i in range(3))
        note = note_of(start + b * size + rows_iota(shape), lens_ref)
        power = jnp.where(group == 0, near, -near)
        power = jnp.where(group == 2, ahead + offsets[b], power)
        power = jnp.where(group >= 3, behind + after, power)
        kept = (group < 2) | ((group == 2) & (note == note_before)) | ((group == 3) & (note == note_last))
        after = after + totals[b]
        rows = slice(b * size, (b + 1) * size)
        scale_ref[rows, :LANES], scale_ref[rows, LANES:] = split(jnp.where(kept, jnp.exp(power), 0.0))
    spread = one(
        rows_iota((LANES, channels)) == cols_iota((LANES, channels)) // P_SIZE
    ).astype(bf16)
    half = CHUNK // 2
    chunk = rows_iota((chunks, tokens)) * CHUNK + half
    col = cols_iota((chunks, tokens))
    for place in range(2):
        begin = chunk + place * half
        steps = exact(one((col >= begin) & (col < begin + half)).astype(bf16), parts, NT)
        kappa_ref[place * chunks : (place + 1) * chunks, :] = exact(thirds(jnp.exp(steps)), spread)
    through = jnp.broadcast_to(jnp.exp(offsets[-1]), (8, LANES)) * one(note_before == note_last)
    through_ref[...] = exact(thirds(through), spread)


def tiles(rows, channels, high=64, wide=LANES):
    return [
        (slice(r, r + high), slice(c, c + wide))
        for r in range(0, rows, high)
        for c in range(0, channels, wide)
    ]


def adjoint_kernel(
    lens_ref, start_ref, grad_ref, scale_ref, pre_ref, halo_ref, taps_ref, through_ref,
    hi_ref, lo_ref, slope_ref, rh_ref, rl_ref, gh_ref, gl_ref, send_ref,
    spread, spread_r, entry, near, ext, *, heads
):
    rows, channels = grad_ref.shape
    step = pl.program_id(0)

    @pl.when(step == 0)
    def _():
        spread[...] = expander(heads, channels, 2)
        spread_r[...] = expander(heads, channels, 0)
        send_ref[...] = jnp.zeros_like(send_ref)
        send_ref[N : N + 8, :] = through_ref[...]
        ext[0:8, :] = halo_ref[8:16, channels:].astype(f32)

    @pl.when(step > 0)
    def _():
        ext[0:8, :] = ext[rows : rows + 8, :]

    ext[8:, :] = pre_ref[...].astype(f32)
    scale = scale_ref[...]
    entry[...] = dot(scale, spread[...])
    near[...] = dot(scale, spread_r[...])
    for first in range(0, rows, 64):
        at = slice(first, first + 64)

        def emit(over, u, at=at):
            value, slope_ref[at, over] = silu_and_slope(u)
            hi_ref[at, over], lo_ref[at, over] = split(value)

        place = start_ref[0] + step * rows + first
        conv_rows(ext, taps_ref, 8 + first, 64, 2 * N, place, -1, lens_ref, emit)
    for at, over in tiles(rows, channels):
        grad = grad_ref[at, over].astype(f32)
        gh_ref[at, over], gl_ref[at, over] = split(grad * entry[at, over])
        rh_ref[at, over], rl_ref[at, over] = split(grad * near[at, over])
    send_ref[0:N, :] += dot3_tn((hi_ref[:, N:], lo_ref[:, N:]), (gh_ref[...], gl_ref[...]))


def state_kernel(
    lens_ref, start_ref, pre_ref, halo_ref, taps_ref, scale_ref, hi_ref, lo_ref, through_ref, other_ref,
    slope_ref, qh_ref, ql_ref, xh_ref, xl_ref, own_ref, *refs, heads, count
):
    messages = refs[: count - 1]
    spread, spread_q, leave, near, ext = refs[count - 1 :]
    rows, channels = pre_ref.shape
    step, steps = pl.program_id(0), pl.num_programs(0)

    @pl.when(step == 0)
    def _():
        spread[...] = expander(heads, channels, 3)
        spread_q[...] = expander(heads, channels, 1)
        own_ref[...] = jnp.zeros_like(own_ref)
        own_ref[N : N + 8, :] = through_ref[...]
        ext[0:8, :] = halo_ref[8:16, :channels].astype(f32)

    @pl.when(step > 0)
    def _():
        ext[0:8, :] = ext[rows : rows + 8, :]

    ext[8:, :] = pre_ref[...].astype(f32)
    scale = scale_ref[...]
    leave[...] = dot(scale, spread[...])
    near[...] = dot(scale, spread_q[...])
    for first in range(0, rows, 64):
        at = slice(first, first + 64)

        def emit(over, u, at=at):
            value, slope_ref[at, over] = silu_and_slope(u)
            xh_ref[at, over], xl_ref[at, over] = split(value * leave[at, over])
            qh_ref[at, over], ql_ref[at, over] = split(value * near[at, over])

        place = start_ref[0] + step * rows + first
        conv_rows(ext, taps_ref, 8 + first, 64, channels, place, -1, lens_ref, emit)
    own_ref[0:N, :] += dot3_tn((hi_ref[:, :N], lo_ref[:, :N]), (xh_ref[...], xl_ref[...]))

    @pl.when(step == steps - 1)
    def _():
        for lag in range(1, count):
            ahead = start_ref[0] + lag * rows * steps < count * rows * steps
            messages[lag - 1][...] = jnp.where(ahead, own_ref[...], other_ref[...])


def local_kernel(
    lens_ref, start_ref, kappa_ref,
    fx_h, fx_l, fg_h, fg_l, f_hi, f_lo, bx_h, bx_l, bg_h, bg_l, b_hi, b_lo,
    dx_ref, dbc_ref, rate_ref, state, adjoint, summer, product
):
    step = pl.program_id(0)
    chunks = pl.num_programs(0)
    channels = dx_ref.shape[1]
    here, there = step, chunks - 1 - step

    @pl.when(step == 0)
    def _():
        summer[...] = head_summer(channels)
        state[...] = jnp.zeros_like(state)
        adjoint[...] = jnp.zeros_like(adjoint)
        dbc_ref[...] = jnp.zeros_like(dbc_ref)
        rate_ref[...] = jnp.zeros_like(rate_ref)

    square = (CHUNK, CHUNK)
    row, col = rows_iota(square), cols_iota(square)
    pick = lambda flag, parts: tuple(
        jnp.where(flag, part.astype(f32), 0.0).astype(bf16) for part in parts
    )
    beside = lambda left, right: tuple(jnp.concatenate(p, axis=1) for p in zip(left, right))
    below = lambda left, right: tuple(stack(*p) for p in zip(left, right))
    turned = lambda parts: stack(parts[0], parts[1], parts[0]).astype(f32).T.astype(bf16)

    def setting(chunk, hi_ref, lo_ref):
        first = start_ref[0] + chunk * CHUNK
        note_before = note_of(first - 1, lens_ref)
        note_last = note_of(first + CHUNK - 1, lens_ref)
        keep = jnp.where(note_before == note_last, 1.0, 0.0)
        note = note_of(first + rows_iota((CHUNK, LANES)), lens_ref)
        linked = note_of(first + row, lens_ref) == note_of(first + col, lens_ref)
        b_parts = (hi_ref[:, :N], lo_ref[:, :N])
        c_parts = (hi_ref[:, N:], lo_ref[:, N:])
        return keep, note == note_before, note == note_last, linked, b_parts, c_parts

    def walk(ref, left, turn, x_refs, keep, place, over):
        held = ref[:, over]
        held_parts = split(held)
        x_parts = (x_refs[0][:, over], x_refs[1][:, over])
        right = below(held_parts, x_parts)
        fresh = dot(turn, stack(x_parts[0], x_parts[0], x_parts[1]))
        moved = (held * keep + fresh) * kappa_ref[pl.ds(place, 1), over]
        ref[:, over] = moved * kappa_ref[pl.ds(chunks + place, 1), over]
        return dot3(left, right), right, held_parts

    rows_f = pl.ds(pl.multiple_of(here * CHUNK, CHUNK), CHUNK)
    rows_b = pl.ds(pl.multiple_of(there * CHUNK, CHUNK), CHUNK)
    f_keep, f_enters, f_leaves, f_linked, fb, fc = setting(here, f_hi, f_lo)
    b_keep, b_enters, b_leaves, b_linked, bb, bc = setting(there, b_hi, b_lo)
    f_scores = jnp.where(f_linked & (col < row), dot3(fc, fb, NT), 0.0)
    b_scores = jnp.where(b_linked & (row < col), dot3(bb, bc, NT), 0.0)
    f_left = beside(pick(f_enters, fc), split(f_scores))
    b_left = beside(pick(b_leaves, bb), split(b_scores))
    f_turn, b_turn = turned(pick(f_leaves, fb)), turned(pick(b_enters, bc))
    own = jnp.sum(whole_of(bb) * whole_of(bc), axis=1, keepdims=True)
    wide = min(2 * LANES, channels)
    inner = outer = 0.0
    for first in range(0, channels, wide):
        over = slice(first, first + wide)
        y, right, _ = walk(state, f_left, f_turn, (fx_h, fx_l), f_keep, here, over)
        inner = inner + dot3((fg_h[:, over], fg_l[:, over]), right, NT)
        product[0:CHUNK, over], product[CHUNK : 2 * CHUNK, over] = split(
            whole_of((fg_h[:, over], fg_l[:, over])) * y
        )
        before = jnp.maximum(there - 1, 0)
        dx, _, a_parts = walk(adjoint, b_left, b_turn, (bg_h, bg_l), b_keep, before, over)
        outer = outer + dot3((bx_h[:, over], bx_l[:, over]), a_parts, NT)
        dx_ref[:, over] = dx + own * whole_of((bg_h[:, over], bg_l[:, over]))
        product[2 * CHUNK : 3 * CHUNK, over], product[3 * CHUNK :, over] = split(
            whole_of((bx_h[:, over], bx_l[:, over])) * dx
        )
    d_scores = split(jnp.where(f_linked & (col <= row), inner[:, N:], 0.0))
    for_c = jnp.where(f_enters, inner[:, :N], 0.0) + dot3(d_scores, fb)
    for_b = dot3_tn(d_scores, fc)
    dbc_ref[rows_f, :] += jnp.concatenate([for_b, for_c], axis=1)
    dbc_ref[rows_b, :N] += jnp.where(b_leaves, outer, 0.0)
    rates = dot(product[...], summer[...])
    rate_ref[rows_f, :] += rates[:CHUNK] + rates[CHUNK : 2 * CHUNK]
    rate_ref[rows_b, :] -= rates[2 * CHUNK : 3 * CHUNK] + rates[3 * CHUNK :]


def joined(messages):
    total = jnp.zeros((N, messages[0].shape[1]), f32)
    for message in reversed(messages):
        total = message[0:N, :] + message[N : N + 1, :] * total
    return total


def pull(high, low, both):
    most = dot(high, both[...], NT)
    return most[:, :N] + most[:, N:] + dot(low, both[0:N, :], NT)


def push(high, low, both, over=slice(None)):
    first = both[0:N, over]
    return dot(jnp.concatenate([high, low, high], axis=1), stack(first, first, both[N:, over]))


def entering_kernel(start_ref, *refs, count, heads, tokens):
    messages = refs[: count - 1]
    place = start_ref[0]
    forward = [
        jnp.where(place >= lag * tokens, messages[lag - 1][...], 0.0) for lag in range(1, count)
    ]
    backward = [
        jnp.where(place + lag * tokens < count * tokens, messages[count - 1 - lag][...], 0.0)
        for lag in range(1, count)
    ]
    (
        own_ref, gh_ref, gl_ref, xh_ref, xl_ref, hi_ref, lo_ref, scale_ref, dx_ref, dbc_ref,
        slope_ref, slope_bc_ref, s2_ref, a2_ref, end_ref, head_ref,
    ) = refs[count - 1 :]
    channels = gh_ref.shape[1]
    state, adjoint = joined(forward), joined(backward)
    s2_ref[0:N, :], s2_ref[N:, :] = split(state)
    a2_ref[0:N, :], a2_ref[N:, :] = split(adjoint)
    last = own_ref[0:N, :] + own_ref[N : N + 1, :] * state
    end_ref[...] = jnp.broadcast_to(jnp.sum(last * adjoint, axis=0, keepdims=True), end_ref.shape)
    for_c = pull(gh_ref[...], gl_ref[...], s2_ref)
    for_b = pull(xh_ref[...], xl_ref[...], a2_ref)
    shared = (dbc_ref[...] + jnp.concatenate([for_b, for_c], axis=1)) * slope_bc_ref[...]
    scale = scale_ref[...]
    dx = dx_ref[...] * dot(scale, expander(heads, channels, 1))
    dx = dx + push(hi_ref[:, :N], lo_ref[:, :N], a2_ref) * dot(scale, expander(heads, channels, 3))
    head_ref[:, :channels] = (dx * slope_ref[...])[0:8, :]
    head_ref[:, channels:] = shared[0:8, :]


def shared_kernel(gh_ref, gl_ref, xh_ref, xl_ref, dbc_ref, slope_ref, s2_ref, a2_ref, out_ref):
    for_c = pull(gh_ref[...], gl_ref[...], s2_ref)
    for_b = pull(xh_ref[...], xl_ref[...], a2_ref)
    out_ref[...] = (dbc_ref[...] + jnp.concatenate([for_b, for_c], axis=1)) * slope_ref[...]


def arrange_kernel(
    lens_ref, start_ref, side_ref, shared_ref, halo_ref, taps_ref, keep_ref, give_ref, ext, total, *, sharers
):
    tokens = shared_ref.shape[0]
    ext[0:tokens, :] = shared_ref[...]
    ext[tokens:, :] = halo_ref[:, -2 * N :]
    size = tokens // sharers
    high = min(size, 64)
    odd = side_ref[0] == 1
    for block in range(sharers):
        for part in range(0, size, high):
            first = block * size + part

            def emit(over, value, at=slice(first, first + high)):
                total[at, over] = value

            conv_rows(ext, taps_ref, first, high, 2 * N, start_ref[0] + first, 1, lens_ref, emit)
    for pair in range(sharers // 2):
        even, uneven = (total[(2 * pair + i) * size : (2 * pair + i + 1) * size, :] for i in range(2))
        at = slice(pair * size, (pair + 1) * size)
        keep_ref[at, :] = jnp.where(odd, uneven, even)
        give_ref[at, :] = jnp.where(odd, even, uneven)


def final_kernel(
    lens_ref, start_ref, gh_ref, gl_ref, xh_ref, xl_ref, hi_ref, lo_ref, scale_ref,
    dx_ref, slope_ref, rate_ref, s2_ref, a2_ref, taps_ref, tail_ref, from_ref,
    *refs, heads, first_block, last
):
    out_ref, log_ref, head_ref, carry, spread, spread_q, summer, ext = refs[-13:-5]
    product, y_tile, dx_tile, near, leave = refs[-5:]
    step = pl.program_id(0)
    rows, channels = gh_ref.shape

    @pl.when(step == 0)
    def _():
        spread[...] = expander(heads, channels, 3)
        spread_q[...] = expander(heads, channels, 1)
        summer[...] = head_summer(channels)
        ext[rows:, :] = tail_ref[:, :channels]
        carry[...] = jnp.zeros_like(carry) if last else from_ref[...]

    @pl.when(step > 0)
    def _():
        ext[rows:, :] = ext[0:8, :]

    scale = scale_ref[...]
    wide = min(2 * LANES, channels)
    for c in range(0, channels, wide):
        whole = slice(c, c + wide)
        y_tile[...] = push(hi_ref[:, N:], lo_ref[:, N:], s2_ref, whole)
        dx_tile[...] = push(hi_ref[:, :N], lo_ref[:, :N], a2_ref, whole)
        near[...] = dot(scale, spread_q[:, whole])
        leave[...] = dot(scale, spread[:, whole])
        for at, inside in tiles(rows, wide):
            over = slice(c + inside.start, c + inside.stop)
            dx = dx_tile[at, inside]
            rate = whole_of((gh_ref[at, over], gl_ref[at, over])) * y_tile[at, inside]
            rate = rate - whole_of((xh_ref[at, over], xl_ref[at, over])) * dx
            product[at, over], product[rows + at.start : rows + at.stop, over] = split(rate)
            grad = dx_ref[at, over] * near[at, inside] + dx * leave[at, inside]
            ext[at, over] = grad * slope_ref[at, over]
    rates = dot(product[...], summer[...])
    rates = rate_ref[...] + rates[:rows] + rates[rows:]
    if last:
        end_row = (rows_iota((rows, LANES)) == rows - 1) & (step == 0)
        beyond = exact(thirds(from_ref[...]), summer[...])[0:1, :]
        rates = rates + jnp.where(end_row, beyond, 0.0)
    later = rows_iota((rows, rows)) >= cols_iota((rows, rows))
    ones = jnp.ones((rows, LANES), f32)
    marks = jnp.concatenate([jnp.where(later, 1.0, 0.0), ones], axis=1).astype(bf16)
    sums = exact(thirds(rates), marks, TN)
    log = sums[:, :rows] + widen(carry[...], rows)
    log_ref[...] = log[0:heads, :]
    carry[...] += sums[:, rows:]
    first = start_ref[0] + (first_block - step) * rows
    for r in range(0, rows, 64):

        def emit(over, value, at=slice(r, r + 64)):
            out_ref[at, over] = value

        conv_rows(ext, taps_ref, r, 64, channels, first + r, 1, lens_ref, emit)

    @pl.when(step == pl.num_programs(0) - 1)
    def _():
        head_ref[...] = ext[0:8, :]


def shifted(value, axis, steps):
    count = lax.axis_size(axis)
    initial, last = (max(0, -steps), min(count, count - steps))
    return lax.ppermute(value, axis, [(source, source + steps) for source in range(initial, last)])


def head_scatter(keep, give):
    count = lax.axis_size("head")
    mine = lax.axis_index("head")
    swap = lambda value, bit: lax.ppermute(value, "head", [(i, i ^ bit) for i in range(count)])
    value = keep + swap(give, 1)
    size = 2 * value.shape[0] // count
    value = value.reshape(count // 2, size, value.shape[1])
    bit = 2
    while bit < count:
        pairs = value.reshape(value.shape[0] // 2, 2, size, value.shape[2])
        side = (mine // bit) % 2
        kept = lax.dynamic_index_in_dim(pairs, side, 1, keepdims=False)
        given = lax.dynamic_index_in_dim(pairs, 1 - side, 1, keepdims=False)
        value = kept + swap(given, bit)
        bit *= 2
    return value.reshape(size, value.shape[2])


def local(pre_x, pre_bc, conv_x, conv_bc, log_decay, lengths, grad_out):
    tokens, channels = pre_x.shape
    heads = log_decay.shape[0]
    count = lax.axis_size("seq")
    sharers = lax.axis_size("head")
    chunks = tokens // CHUNK
    big = 256
    steps = tokens // big
    width = 2 * LANES
    start = (lax.axis_index("seq") * tokens).astype(jnp.int32).reshape(1)
    side = (lax.axis_index("head") % 2).astype(jnp.int32).reshape(1)
    halo = shifted(jnp.concatenate([pre_x[-16:], pre_bc[-16:]], axis=1), "seq", 1)
    shape = jax.ShapeDtypeStruct
    smem = pl.BlockSpec(memory_space=pltpu.SMEM)
    vmem = pl.BlockSpec(memory_space=pltpu.VMEM)
    params = pltpu.CompilerParams(vmem_limit_bytes=VMEM_LIMIT)
    by_rows = lambda rows, cols: pl.BlockSpec((rows, cols), lambda i: (i, 0))
    whole = lambda rows, cols: pl.BlockSpec((rows, cols), lambda *i: (0, 0))
    wide = tokens * channels
    cost = lambda work: pl.CostEstimate(flops=wide * work, bytes_accessed=wide * 16, transcendentals=0)
    rows_f32, rows_bf16 = shape((tokens, channels), f32), shape((tokens, channels), bf16)
    bc_f32, bc_bf16 = shape((tokens, 2 * N), f32), shape((tokens, 2 * N), bf16)

    scale, kappa, through = pl.pallas_call(
        scales_kernel,
        out_shape=(
            shape((tokens, width), bf16), shape((2 * chunks, channels), f32), shape((8, channels), f32),
        ),
        in_specs=[smem, smem, vmem],
        out_specs=(vmem,) * 3,
        scratch_shapes=[pltpu.VMEM((LANES, tokens), f32)],
        compiler_params=params,
        cost_estimate=cost(1000),
    )(lengths, start, log_decay)

    spread = pltpu.VMEM((width, channels), bf16)
    block = pltpu.VMEM((big, channels), f32)
    hi, lo, slope_bc, r_high, r_low, g_high, g_low, send_adjoint = pl.pallas_call(
        functools.partial(adjoint_kernel, heads=heads),
        grid=(steps,),
        out_shape=(bc_bf16, bc_bf16, bc_f32) + (rows_bf16,) * 4 + (shape((N + 8, channels), f32),),
        in_specs=[
            smem, smem, by_rows(big, channels), by_rows(big, width), by_rows(big, 2 * N),
            whole(16, channels + 2 * N), whole(K, 2 * N), whole(8, channels),
        ],
        out_specs=(by_rows(big, 2 * N),) * 3 + (by_rows(big, channels),) * 4 + (whole(N + 8, channels),),
        scratch_shapes=[spread, spread, block, block, pltpu.VMEM((big + 8, 2 * N), f32)],
        compiler_params=params,
        cost_estimate=cost(1000),
    )(lengths, start, grad_out, scale, pre_bc, halo, conv_bc, through)

    slope_x, q_high, q_low, x_high, x_low, own_state, *messages = pl.pallas_call(
        functools.partial(state_kernel, heads=heads, count=count),
        grid=(steps,),
        out_shape=(rows_f32,) + (rows_bf16,) * 4 + (shape((N + 8, channels), f32),) * count,
        in_specs=[
            smem, smem, by_rows(big, channels), whole(16, channels + 2 * N), whole(K, channels),
            by_rows(big, width), by_rows(big, 2 * N), by_rows(big, 2 * N), whole(8, channels),
            whole(N + 8, channels),
        ],
        out_specs=(by_rows(big, channels),) * 5 + (whole(N + 8, channels),) * count,
        scratch_shapes=[spread, spread, block, block, pltpu.VMEM((big + 8, channels), f32)],
        compiler_params=params,
        cost_estimate=cost(1000),
    )(lengths, start, pre_x, halo, conv_x, scale, hi, lo, through, send_adjoint)
    received = [
        lax.ppermute(message, "seq", [(i, (i + lag) % count) for i in range(count)])
        for lag, message in enumerate(messages, 1)
    ]

    from_end = lambda rows, cols: pl.BlockSpec((rows, cols), lambda i: (chunks - 1 - i, 0))
    both_ways = [
        place(CHUNK, size)
        for place in (by_rows, from_end)
        for size in (channels, channels, channels, channels, 2 * N, 2 * N)
    ]
    dx, dbc, rate = pl.pallas_call(
        local_kernel,
        grid=(chunks,),
        out_shape=(rows_f32, bc_f32, shape((tokens, LANES), f32)),
        in_specs=[smem, smem, whole(2 * chunks, channels)] + both_ways,
        out_specs=(from_end(CHUNK, channels), whole(tokens, 2 * N), whole(tokens, LANES)),
        scratch_shapes=[
            pltpu.VMEM((N, channels), f32), pltpu.VMEM((N, channels), f32),
            pltpu.VMEM((channels, LANES), bf16),
        ]
        + [pltpu.VMEM((4 * CHUNK, channels), bf16)],
        compiler_params=params,
        cost_estimate=cost(8000),
    )(lengths, start, kappa, *([q_high, q_low, r_high, r_low, hi, lo] * 2))

    message = whole(N + 8, channels)
    s2, a2, end, head = pl.pallas_call(
        functools.partial(entering_kernel, count=count, heads=heads, tokens=tokens),
        grid=(1,),
        out_shape=(
            shape((2 * N, channels), bf16), shape((2 * N, channels), bf16), shape((8, channels), f32),
            shape((8, channels + 2 * N), f32),
        ),
        in_specs=[smem]
        + [message] * count
        + [whole(16, channels)] * 4
        + [whole(16, 2 * N)] * 2
        + [whole(16, width), whole(16, channels), whole(16, 2 * N), whole(16, channels), whole(16, 2 * N)],
        out_specs=(
            whole(2 * N, channels), whole(2 * N, channels), whole(8, channels),
            whole(8, channels + 2 * N),
        ),
        compiler_params=params,
        cost_estimate=cost(200),
    )(
        start, *received, own_state, g_high, g_low, x_high, x_low, hi, lo, scale, dx, dbc,
        slope_x, slope_bc,
    )
    after = shifted(head, "seq", -1)

    shared = pl.pallas_call(
        shared_kernel,
        grid=(steps,),
        out_shape=bc_f32,
        in_specs=[by_rows(big, channels)] * 4
        + [by_rows(big, 2 * N)] * 2
        + [whole(2 * N, channels)] * 2,
        out_specs=by_rows(big, 2 * N),
        compiler_params=params,
        cost_estimate=cost(1500),
    )(g_high, g_low, x_high, x_low, dbc, slope_bc, s2, a2)

    half = shape((tokens // 2, 2 * N), f32)
    keep, give = pl.pallas_call(
        functools.partial(arrange_kernel, sharers=sharers),
        out_shape=(half, half),
        in_specs=[smem, smem, smem, vmem, vmem, vmem],
        out_specs=(vmem, vmem),
        scratch_shapes=[pltpu.VMEM((tokens + 8, 2 * N), f32), pltpu.VMEM((tokens, 2 * N), f32)],
        compiler_params=params,
    )(lengths, start, side, shared, after, conv_bc)
    grad_pre_bc = head_scatter(keep, give)

    part = steps // 2
    tail, carry = after, end
    done = ()
    for first_block in (steps - 1, steps - 1 - part):
        back = lambda rows, cols, top=first_block: pl.BlockSpec((rows, cols), lambda i: (top - i, 0))
        grad_pre_x, grad_log, tail, carry = pl.pallas_call(
            functools.partial(final_kernel, heads=heads, first_block=first_block, last=not done),
            grid=(part,),
            out_shape=(
                rows_f32, shape((heads, tokens), f32), shape((8, channels), f32),
                shape((LANES, LANES), f32),
            ),
            in_specs=[smem, smem]
            + [back(big, channels)] * 4
            + [back(big, 2 * N)] * 2
            + [back(big, width)]
            + [back(big, channels)] * 2
            + [
                back(big, LANES), whole(2 * N, channels), whole(2 * N, channels),
                whole(K, channels), whole(*tail.shape), whole(*carry.shape),
            ]
            + [pl.BlockSpec(memory_space=pl.ANY)] * len(done),
            out_specs=(
                back(big, channels),
                pl.BlockSpec((heads, big), lambda i, top=first_block: (0, top - i)),
                whole(8, channels), whole(LANES, LANES),
            ),
            scratch_shapes=[
                spread, spread, pltpu.VMEM((channels, LANES), bf16),
                pltpu.VMEM((big + 8, channels), f32), pltpu.VMEM((2 * big, channels), bf16),
            ]
            + [pltpu.VMEM((big, min(2 * LANES, channels)), f32)] * 4,
            input_output_aliases={17 + i: i for i in range(len(done))},
            compiler_params=params,
            cost_estimate=cost(1500),
        )(
            lengths, start, g_high, g_low, x_high, x_low, hi, lo, scale, dx, slope_x, rate, s2, a2,
            conv_x, tail, carry, *done,
        )
        done = (grad_pre_x, grad_log)
    return (grad_pre_x, grad_pre_bc, grad_log)


def solution(mesh):
    placed = (
        P("seq", "head"),
        P("seq", None),
        P(None, "head"),
        P(),
        P("head", "seq"),
        P(),
        P("seq", "head"),
    )
    return jax.shard_map(
        local,
        mesh=mesh,
        in_specs=placed,
        out_specs=(P("seq", "head"), P(("seq", "head"), None), P("head", "seq")),
        check_vma=False,
    )
```

```python
import functools
import jax
import jax.numpy as jnp
from jax import lax
from jax.experimental import pallas as pl
from jax.experimental.pallas import tpu as pltpu
from jax.sharding import PartitionSpec as P

P_SIZE = 64
N = 128
K = 4
CHUNK = 64
LANES = 128
f32 = jnp.float32
bf16 = jnp.bfloat16
NN = (((1,), (0,)), ((), ()))
NT = (((1,), (1,)), ((), ()))
TN = (((0,), (0,)), ((), ()))
VMEM_LIMIT = 24 * 1024 * 1024


def split(value):
    high = value.astype(bf16)
    return high, (value - high.astype(f32)).astype(bf16)


def dot(left, right, dims=NN):
    return lax.dot_general(left, right, dims, preferred_element_type=f32)


def thirds(value):
    high, low = split(value)
    return high, low, (value - high.astype(f32) - low.astype(f32)).astype(bf16)


def exact(left, right, dims=NN):
    if isinstance(left, tuple):
        return dot(left[0], right, dims) + dot(left[1], right, dims) + dot(left[2], right, dims)
    return dot(left, right[0], dims) + dot(left, right[1], dims) + dot(left, right[2], dims)


def stack(*parts):
    return jnp.concatenate(parts, axis=0)


def dot3(left, right, dims=NN):
    rows = left[0].shape[0]
    most = dot(stack(*left), right[0], dims)
    return most[:rows] + most[rows:] + dot(left[0], right[1], dims)


def dot3_tn(left, right):
    return dot(stack(left[0], left[1], left[0]), stack(right[0], right[0], right[1]), TN)


def whole_of(parts):
    return parts[0].astype(f32) + parts[1].astype(f32)


def rows_iota(shape):
    return lax.broadcasted_iota(jnp.int32, shape, 0)


def cols_iota(shape):
    return lax.broadcasted_iota(jnp.int32, shape, 1)


def note_of(position, lens_ref):
    first = lens_ref[0]
    second = first + lens_ref[1]
    third = second + lens_ref[2]
    one = lambda flag: jnp.where(flag, 1, 0)
    return one(position >= 0) + one(position >= first) + one(position >= second) + one(
        position >= third
    )


def widen(block, width):
    return block if width == LANES else jnp.concatenate([block] * (width // LANES), axis=1)


def links(first, rows, sign, lens_ref):
    position = first + rows_iota((rows, LANES))
    here = note_of(position, lens_ref)
    return [
        jnp.where(note_of(position + sign * lag, lens_ref) == here, 1.0, 0.0) for lag in range(1, K)
    ]


def conv_tile(ext_ref, taps_ref, first, rows, over, linked, sign):
    total = ext_ref[first : first + rows, over] * taps_ref[K - 1 : K, over]
    for lag in range(1, K):
        moved = first + sign * lag
        tap = taps_ref[K - 1 - lag : K - lag, over]
        tap = tap if linked is None else tap * linked[lag - 1]
        total = total + ext_ref[moved : moved + rows, over] * tap
    return total


def conv_rows(ext_ref, taps_ref, first, rows, width, position, sign, lens_ref, emit):
    begins = [0, lens_ref[0], lens_ref[0] + lens_ref[1], lens_ref[0] + lens_ref[1] + lens_ref[2]]
    near = [(begin > position - K) & (begin < position + rows + K) for begin in begins]
    cut = near[0] | near[1] | near[2] | near[3]

    def body(linked):
        for c in range(0, width, LANES):
            over = slice(c, c + LANES)
            emit(over, conv_tile(ext_ref, taps_ref, first, rows, over, linked, sign))

    @pl.when(cut)
    def _():
        body(links(position, rows, sign, lens_ref))

    @pl.when(jnp.logical_not(cut))
    def _():
        body(None)


def silu_and_slope(u):
    sigma = 1.0 / (1.0 + jnp.exp(-u))
    value = u * sigma
    return value, sigma + value * (1.0 - sigma)


def expander(heads, channels, group):
    row = rows_iota((2 * LANES, channels)) % LANES
    own = cols_iota((2 * LANES, channels)) // P_SIZE
    return jnp.where(row == group * heads + own, 1.0, 0.0).astype(bf16)


def head_summer(channels):
    same = rows_iota((channels, LANES)) // P_SIZE == cols_iota((channels, LANES))
    return jnp.where(same, 1.0, 0.0).astype(bf16)


def scales_kernel(lens_ref, start_ref, log_ref, scale_ref, kappa_ref, through_ref, padded):
    heads, tokens = log_ref.shape
    channels = kappa_ref.shape[1]
    chunks = tokens // CHUNK
    start = start_ref[0]
    padded[...] = jnp.zeros_like(padded)
    for group in range(4):
        padded[group * heads : (group + 1) * heads, :] = log_ref[...]
    size = 2 * LANES
    square = (size, size)
    row, col = rows_iota(square), cols_iota(square)
    same = row // CHUNK == col // CHUNK
    one = lambda flag: jnp.where(flag, 1.0, 0.0)
    inner = one(same & (col <= row)) - one(same & (col % CHUNK < CHUNK // 2))
    sums = stack(inner, one(col <= row), one(col > row), jnp.ones((16, size), f32)).astype(bf16)
    blocks = tokens // size
    parts = thirds(padded[...])
    tables = [
        exact(sums, tuple(part[:, b * size : (b + 1) * size] for part in parts), NT)
        for b in range(blocks)
    ]
    totals = [table[3 * size : 3 * size + 1, :] for table in tables]
    offsets = [jnp.zeros((1, LANES), f32)]
    for total in totals:
        offsets.append(offsets[-1] + total)
    after = jnp.zeros((1, LANES), f32)
    note_before = note_of(start - 1, lens_ref)
    note_last = note_of(start + tokens - 1, lens_ref)
    shape = (size, LANES)
    group = cols_iota(shape) // heads
    for b in reversed(range(blocks)):
        near, ahead, behind = (tables[b][i * size : (i + 1) * size, :] for i in range(3))
        note = note_of(start + b * size + rows_iota(shape), lens_ref)
        power = jnp.where(group == 0, near, -near)
        power = jnp.where(group == 2, ahead + offsets[b], power)
        power = jnp.where(group >= 3, behind + after, power)
        kept = (group < 2) | ((group == 2) & (note == note_before)) | ((group == 3) & (note == note_last))
        after = after + totals[b]
        rows = slice(b * size, (b + 1) * size)
        scale_ref[rows, :LANES], scale_ref[rows, LANES:] = split(jnp.where(kept, jnp.exp(power), 0.0))
    spread = one(
        rows_iota((LANES, channels)) == cols_iota((LANES, channels)) // P_SIZE
    ).astype(bf16)
    half = CHUNK // 2
    chunk = rows_iota((chunks, tokens)) * CHUNK + half
    col = cols_iota((chunks, tokens))
    for place in range(2):
        begin = chunk + place * half
        steps = exact(one((col >= begin) & (col < begin + half)).astype(bf16), parts, NT)
        kappa_ref[place * chunks : (place + 1) * chunks, :] = exact(thirds(jnp.exp(steps)), spread)
    through = jnp.broadcast_to(jnp.exp(offsets[-1]), (8, LANES)) * one(note_before == note_last)
    through_ref[...] = exact(thirds(through), spread)


def tiles(rows, channels, high=64, wide=LANES):
    return [
        (slice(r, r + high), slice(c, c + wide))
        for r in range(0, rows, high)
        for c in range(0, channels, wide)
    ]


def adjoint_kernel(
    lens_ref, start_ref, grad_ref, scale_ref, pre_ref, halo_ref, taps_ref, through_ref,
    hi_ref, lo_ref, slope_ref, rh_ref, rl_ref, gh_ref, gl_ref, send_ref,
    spread, spread_r, entry, near, ext, *, heads
):
    rows, channels = grad_ref.shape
    step = pl.program_id(0)

    @pl.when(step == 0)
    def _():
        spread[...] = expander(heads, channels, 2)
        spread_r[...] = expander(heads, channels, 0)
        send_ref[...] = jnp.zeros_like(send_ref)
        send_ref[N : N + 8, :] = through_ref[...]
        ext[0:8, :] = halo_ref[8:16, channels:].astype(f32)

    @pl.when(step > 0)
    def _():
        ext[0:8, :] = ext[rows : rows + 8, :]

    ext[8:, :] = pre_ref[...].astype(f32)
    scale = scale_ref[...]
    entry[...] = dot(scale, spread[...])
    near[...] = dot(scale, spread_r[...])
    for first in range(0, rows, 64):
        at = slice(first, first + 64)

        def emit(over, u, at=at):
            value, slope_ref[at, over] = silu_and_slope(u)
            hi_ref[at, over], lo_ref[at, over] = split(value)

        place = start_ref[0] + step * rows + first
        conv_rows(ext, taps_ref, 8 + first, 64, 2 * N, place, -1, lens_ref, emit)
    for at, over in tiles(rows, channels):
        grad = grad_ref[at, over].astype(f32)
        gh_ref[at, over], gl_ref[at, over] = split(grad * entry[at, over])
        rh_ref[at, over], rl_ref[at, over] = split(grad * near[at, over])
    send_ref[0:N, :] += dot3_tn((hi_ref[:, N:], lo_ref[:, N:]), (gh_ref[...], gl_ref[...]))


def state_kernel(
    lens_ref, start_ref, pre_ref, halo_ref, taps_ref, scale_ref, hi_ref, lo_ref, through_ref, other_ref,
    slope_ref, qh_ref, ql_ref, xh_ref, xl_ref, own_ref, *refs, heads, count
):
    messages = refs[: count - 1]
    spread, spread_q, leave, near, ext = refs[count - 1 :]
    rows, channels = pre_ref.shape
    step, steps = pl.program_id(0), pl.num_programs(0)

    @pl.when(step == 0)
    def _():
        spread[...] = expander(heads, channels, 3)
        spread_q[...] = expander(heads, channels, 1)
        own_ref[...] = jnp.zeros_like(own_ref)
        own_ref[N : N + 8, :] = through_ref[...]
        ext[0:8, :] = halo_ref[8:16, :channels].astype(f32)

    @pl.when(step > 0)
    def _():
        ext[0:8, :] = ext[rows : rows + 8, :]

    ext[8:, :] = pre_ref[...].astype(f32)
    scale = scale_ref[...]
    leave[...] = dot(scale, spread[...])
    near[...] = dot(scale, spread_q[...])
    for first in range(0, rows, 64):
        at = slice(first, first + 64)

        def emit(over, u, at=at):
            value, slope_ref[at, over] = silu_and_slope(u)
            xh_ref[at, over], xl_ref[at, over] = split(value * leave[at, over])
            qh_ref[at, over], ql_ref[at, over] = split(value * near[at, over])

        place = start_ref[0] + step * rows + first
        conv_rows(ext, taps_ref, 8 + first, 64, channels, place, -1, lens_ref, emit)
    own_ref[0:N, :] += dot3_tn((hi_ref[:, :N], lo_ref[:, :N]), (xh_ref[...], xl_ref[...]))

    @pl.when(step == steps - 1)
    def _():
        for lag in range(1, count):
            ahead = start_ref[0] + lag * rows * steps < count * rows * steps
            messages[lag - 1][...] = jnp.where(ahead, own_ref[...], other_ref[...])


def local_kernel(
    lens_ref, start_ref, kappa_ref,
    fx_h, fx_l, fg_h, fg_l, f_hi, f_lo, bx_h, bx_l, bg_h, bg_l, b_hi, b_lo,
    dx_ref, dbc_ref, rate_ref, state, adjoint, summer, product
):
    step = pl.program_id(0)
    chunks = pl.num_programs(0)
    channels = dx_ref.shape[1]
    here, there = step, chunks - 1 - step

    @pl.when(step == 0)
    def _():
        summer[...] = head_summer(channels)
        state[...] = jnp.zeros_like(state)
        adjoint[...] = jnp.zeros_like(adjoint)
        dbc_ref[...] = jnp.zeros_like(dbc_ref)
        rate_ref[...] = jnp.zeros_like(rate_ref)

    square = (CHUNK, CHUNK)
    row, col = rows_iota(square), cols_iota(square)
    pick = lambda flag, parts: tuple(
        jnp.where(flag, part.astype(f32), 0.0).astype(bf16) for part in parts
    )
    beside = lambda left, right: tuple(jnp.concatenate(p, axis=1) for p in zip(left, right))
    below = lambda left, right: tuple(stack(*p) for p in zip(left, right))
    turned = lambda parts: stack(parts[0], parts[1], parts[0]).astype(f32).T.astype(bf16)

    def setting(chunk, hi_ref, lo_ref):
        first = start_ref[0] + chunk * CHUNK
        note_before = note_of(first - 1, lens_ref)
        note_last = note_of(first + CHUNK - 1, lens_ref)
        keep = jnp.where(note_before == note_last, 1.0, 0.0)
        note = note_of(first + rows_iota((CHUNK, LANES)), lens_ref)
        linked = note_of(first + row, lens_ref) == note_of(first + col, lens_ref)
        b_parts = (hi_ref[:, :N], lo_ref[:, :N])
        c_parts = (hi_ref[:, N:], lo_ref[:, N:])
        return keep, note == note_before, note == note_last, linked, b_parts, c_parts

    def walk(ref, left, turn, x_refs, keep, place, over):
        held = ref[:, over]
        held_parts = split(held)
        x_parts = (x_refs[0][:, over], x_refs[1][:, over])
        right = below(held_parts, x_parts)
        fresh = dot(turn, stack(x_parts[0], x_parts[0], x_parts[1]))
        moved = (held * keep + fresh) * kappa_ref[pl.ds(place, 1), over]
        ref[:, over] = moved * kappa_ref[pl.ds(chunks + place, 1), over]
        return dot3(left, right), right, held_parts

    rows_f = pl.ds(pl.multiple_of(here * CHUNK, CHUNK), CHUNK)
    rows_b = pl.ds(pl.multiple_of(there * CHUNK, CHUNK), CHUNK)
    f_keep, f_enters, f_leaves, f_linked, fb, fc = setting(here, f_hi, f_lo)
    b_keep, b_enters, b_leaves, b_linked, bb, bc = setting(there, b_hi, b_lo)
    f_scores = jnp.where(f_linked & (col < row), dot3(fc, fb, NT), 0.0)
    b_scores = jnp.where(b_linked & (row < col), dot3(bb, bc, NT), 0.0)
    f_left = beside(pick(f_enters, fc), split(f_scores))
    b_left = beside(pick(b_leaves, bb), split(b_scores))
    f_turn, b_turn = turned(pick(f_leaves, fb)), turned(pick(b_enters, bc))
    own = jnp.sum(whole_of(bb) * whole_of(bc), axis=1, keepdims=True)
    wide = min(2 * LANES, channels)
    inner = outer = 0.0
    for first in range(0, channels, wide):
        over = slice(first, first + wide)
        y, right, _ = walk(state, f_left, f_turn, (fx_h, fx_l), f_keep, here, over)
        inner = inner + dot3((fg_h[:, over], fg_l[:, over]), right, NT)
        product[0:CHUNK, over], product[CHUNK : 2 * CHUNK, over] = split(
            whole_of((fg_h[:, over], fg_l[:, over])) * y
        )
        before = jnp.maximum(there - 1, 0)
        dx, _, a_parts = walk(adjoint, b_left, b_turn, (bg_h, bg_l), b_keep, before, over)
        outer = outer + dot3((bx_h[:, over], bx_l[:, over]), a_parts, NT)
        dx_ref[:, over] = dx + own * whole_of((bg_h[:, over], bg_l[:, over]))
        product[2 * CHUNK : 3 * CHUNK, over], product[3 * CHUNK :, over] = split(
            whole_of((bx_h[:, over], bx_l[:, over])) * dx
        )
    d_scores = split(jnp.where(f_linked & (col <= row), inner[:, N:], 0.0))
    for_c = jnp.where(f_enters, inner[:, :N], 0.0) + dot3(d_scores, fb)
    for_b = dot3_tn(d_scores, fc)
    dbc_ref[rows_f, :] += jnp.concatenate([for_b, for_c], axis=1)
    dbc_ref[rows_b, :N] += jnp.where(b_leaves, outer, 0.0)
    rates = dot(product[...], summer[...])
    rate_ref[rows_f, :] += rates[:CHUNK] + rates[CHUNK : 2 * CHUNK]
    rate_ref[rows_b, :] -= rates[2 * CHUNK : 3 * CHUNK] + rates[3 * CHUNK :]


def joined(messages):
    total = jnp.zeros((N, messages[0].shape[1]), f32)
    for message in reversed(messages):
        total = message[0:N, :] + message[N : N + 1, :] * total
    return total


def pull(high, low, both):
    most = dot(high, both[...], NT)
    return most[:, :N] + most[:, N:] + dot(low, both[0:N, :], NT)


def push(high, low, both, over=slice(None)):
    first = both[0:N, over]
    return dot(jnp.concatenate([high, low, high], axis=1), stack(first, first, both[N:, over]))


def entering_kernel(start_ref, *refs, count, heads, tokens):
    messages = refs[: count - 1]
    place = start_ref[0]
    forward = [
        jnp.where(place >= lag * tokens, messages[lag - 1][...], 0.0) for lag in range(1, count)
    ]
    backward = [
        jnp.where(place + lag * tokens < count * tokens, messages[count - 1 - lag][...], 0.0)
        for lag in range(1, count)
    ]
    (
        own_ref, gh_ref, gl_ref, xh_ref, xl_ref, hi_ref, lo_ref, scale_ref, dx_ref, dbc_ref,
        slope_ref, slope_bc_ref, s2_ref, a2_ref, end_ref, head_ref,
    ) = refs[count - 1 :]
    channels = gh_ref.shape[1]
    state, adjoint = joined(forward), joined(backward)
    s2_ref[0:N, :], s2_ref[N:, :] = split(state)
    a2_ref[0:N, :], a2_ref[N:, :] = split(adjoint)
    last = own_ref[0:N, :] + own_ref[N : N + 1, :] * state
    end_ref[...] = jnp.broadcast_to(jnp.sum(last * adjoint, axis=0, keepdims=True), end_ref.shape)
    for_c = pull(gh_ref[...], gl_ref[...], s2_ref)
    for_b = pull(xh_ref[...], xl_ref[...], a2_ref)
    shared = (dbc_ref[...] + jnp.concatenate([for_b, for_c], axis=1)) * slope_bc_ref[...]
    scale = scale_ref[...]
    dx = dx_ref[...] * dot(scale, expander(heads, channels, 1))
    dx = dx + push(hi_ref[:, :N], lo_ref[:, :N], a2_ref) * dot(scale, expander(heads, channels, 3))
    head_ref[:, :channels] = (dx * slope_ref[...])[0:8, :]
    head_ref[:, channels:] = shared[0:8, :]


def shared_kernel(gh_ref, gl_ref, xh_ref, xl_ref, dbc_ref, slope_ref, s2_ref, a2_ref, out_ref):
    for_c = pull(gh_ref[...], gl_ref[...], s2_ref)
    for_b = pull(xh_ref[...], xl_ref[...], a2_ref)
    out_ref[...] = (dbc_ref[...] + jnp.concatenate([for_b, for_c], axis=1)) * slope_ref[...]


def arrange_kernel(
    lens_ref, start_ref, side_ref, shared_ref, halo_ref, taps_ref, keep_ref, give_ref, ext, total, *, sharers
):
    tokens = shared_ref.shape[0]
    ext[0:tokens, :] = shared_ref[...]
    ext[tokens:, :] = halo_ref[:, -2 * N :]
    size = tokens // sharers
    high = min(size, 64)
    odd = side_ref[0] % 2 == 1
    for block in range(sharers):
        for part in range(0, size, high):
            first = block * size + part

            def emit(over, value, at=slice(first, first + high)):
                total[at, over] = value

            conv_rows(ext, taps_ref, first, high, 2 * N, start_ref[0] + first, 1, lens_ref, emit)
    for pair in range(sharers // 2):
        even, uneven = (total[(2 * pair + i) * size : (2 * pair + i + 1) * size, :] for i in range(2))
        at = slice(pair * size, (pair + 1) * size)
        keep_ref[at, :] = jnp.where(odd, uneven, even)
        give_ref[at, :] = jnp.where(odd, even, uneven)


def final_kernel(
    lens_ref, start_ref, gh_ref, gl_ref, xh_ref, xl_ref, hi_ref, lo_ref, scale_ref,
    dx_ref, slope_ref, rate_ref, s2_ref, a2_ref, taps_ref, tail_ref, from_ref,
    *refs, heads, first_block, last
):
    out_ref, log_ref, head_ref, carry, spread, spread_q, summer, ext = refs[-13:-5]
    product, y_tile, dx_tile, near, leave = refs[-5:]
    step = pl.program_id(0)
    rows, channels = gh_ref.shape

    @pl.when(step == 0)
    def _():
        spread[...] = expander(heads, channels, 3)
        spread_q[...] = expander(heads, channels, 1)
        summer[...] = head_summer(channels)
        ext[rows:, :] = tail_ref[:, :channels]
        carry[...] = jnp.zeros_like(carry) if last else from_ref[...]

    @pl.when(step > 0)
    def _():
        ext[rows:, :] = ext[0:8, :]

    scale = scale_ref[...]
    wide = min(2 * LANES, channels)
    for c in range(0, channels, wide):
        whole = slice(c, c + wide)
        y_tile[...] = push(hi_ref[:, N:], lo_ref[:, N:], s2_ref, whole)
        dx_tile[...] = push(hi_ref[:, :N], lo_ref[:, :N], a2_ref, whole)
        near[...] = dot(scale, spread_q[:, whole])
        leave[...] = dot(scale, spread[:, whole])
        for at, inside in tiles(rows, wide):
            over = slice(c + inside.start, c + inside.stop)
            dx = dx_tile[at, inside]
            rate = whole_of((gh_ref[at, over], gl_ref[at, over])) * y_tile[at, inside]
            rate = rate - whole_of((xh_ref[at, over], xl_ref[at, over])) * dx
            product[at, over], product[rows + at.start : rows + at.stop, over] = split(rate)
            grad = dx_ref[at, over] * near[at, inside] + dx * leave[at, inside]
            ext[at, over] = grad * slope_ref[at, over]
    rates = dot(product[...], summer[...])
    rates = rate_ref[...] + rates[:rows] + rates[rows:]
    if last:
        end_row = (rows_iota((rows, LANES)) == rows - 1) & (step == 0)
        beyond = exact(thirds(from_ref[...]), summer[...])[0:1, :]
        rates = rates + jnp.where(end_row, beyond, 0.0)
    later = rows_iota((rows, rows)) >= cols_iota((rows, rows))
    ones = jnp.ones((rows, LANES), f32)
    marks = jnp.concatenate([jnp.where(later, 1.0, 0.0), ones], axis=1).astype(bf16)
    sums = exact(thirds(rates), marks, TN)
    log = sums[:, :rows] + widen(carry[...], rows)
    log_ref[...] = log[0:heads, :]
    carry[...] += sums[:, rows:]
    first = start_ref[0] + (first_block - step) * rows
    for r in range(0, rows, 64):

        def emit(over, value, at=slice(r, r + 64)):
            out_ref[at, over] = value

        conv_rows(ext, taps_ref, r, 64, channels, first + r, 1, lens_ref, emit)

    @pl.when(step == pl.num_programs(0) - 1)
    def _():
        head_ref[...] = ext[0:8, :]


def shifted(value, axis, steps):
    count = lax.axis_size(axis)
    initial, last = (max(0, -steps), min(count, count - steps))
    return lax.ppermute(value, axis, [(source, source + steps) for source in range(initial, last)])


def merge_kernel(side_ref, kept_ref, came_ref, keep_ref, give_ref):
    odd = side_ref[0] == 1
    for pair in range(keep_ref.shape[0]):
        even, uneven = (kept_ref[2 * pair + i] + came_ref[2 * pair + i] for i in range(2))
        keep_ref[pair] = jnp.where(odd, uneven, even)
        give_ref[pair] = jnp.where(odd, even, uneven)


def last_kernel(kept_ref, came_ref, out_ref):
    out_ref[...] = kept_ref[...] + came_ref[...]


def head_scatter(keep, give, mine, params):
    count = lax.axis_size("head")
    swap = lambda value, bit: lax.ppermute(value, "head", [(i, i ^ bit) for i in range(count)])
    size, width = 2 * keep.shape[0] // count, keep.shape[1]
    blocks = lambda value: value.reshape(-1, size, width)
    smem = pl.BlockSpec(memory_space=pltpu.SMEM)
    vmem = pl.BlockSpec(memory_space=pltpu.VMEM)
    keep, give, bit = blocks(keep), blocks(give), 1
    while 2 * bit < count:
        came = swap(give, bit)
        bit *= 2
        half = jax.ShapeDtypeStruct((keep.shape[0] // 2, size, width), f32)
        keep, give = pl.pallas_call(
            merge_kernel,
            out_shape=(half, half),
            in_specs=[smem, vmem, vmem],
            out_specs=(vmem, vmem),
            compiler_params=params,
        )((mine // bit) % 2, keep, came)
    return pl.pallas_call(
        last_kernel,
        out_shape=jax.ShapeDtypeStruct((size, width), f32),
        in_specs=[vmem, vmem],
        out_specs=vmem,
        compiler_params=params,
    )(keep[0], swap(give, bit)[0])


def local(pre_x, pre_bc, conv_x, conv_bc, log_decay, lengths, grad_out):
    tokens, channels = pre_x.shape
    heads = log_decay.shape[0]
    count = lax.axis_size("seq")
    sharers = lax.axis_size("head")
    chunks = tokens // CHUNK
    big = 256
    steps = tokens // big
    width = 2 * LANES
    start = (lax.axis_index("seq") * tokens).astype(jnp.int32).reshape(1)
    mine = lax.axis_index("head").astype(jnp.int32).reshape(1)
    halo = shifted(jnp.concatenate([pre_x[-16:], pre_bc[-16:]], axis=1), "seq", 1)
    shape = jax.ShapeDtypeStruct
    smem = pl.BlockSpec(memory_space=pltpu.SMEM)
    vmem = pl.BlockSpec(memory_space=pltpu.VMEM)
    params = pltpu.CompilerParams(vmem_limit_bytes=VMEM_LIMIT)
    by_rows = lambda rows, cols: pl.BlockSpec((rows, cols), lambda i: (i, 0))
    whole = lambda rows, cols: pl.BlockSpec((rows, cols), lambda *i: (0, 0))
    wide = tokens * channels
    cost = lambda work: pl.CostEstimate(flops=wide * work, bytes_accessed=wide * 16, transcendentals=0)
    grad_out = pltpu.with_memory_space_constraint(grad_out, pltpu.HBM)
    pre_x = pltpu.with_memory_space_constraint(pre_x, pltpu.HBM)
    pre_bc = pltpu.with_memory_space_constraint(pre_bc, pltpu.HBM)
    rows_f32, rows_bf16 = shape((tokens, channels), f32), shape((tokens, channels), bf16)
    bc_f32, bc_bf16 = shape((tokens, 2 * N), f32), shape((tokens, 2 * N), bf16)

    scale, kappa, through = pl.pallas_call(
        scales_kernel,
        out_shape=(
            shape((tokens, width), bf16), shape((2 * chunks, channels), f32), shape((8, channels), f32),
        ),
        in_specs=[smem, smem, vmem],
        out_specs=(vmem,) * 3,
        scratch_shapes=[pltpu.VMEM((LANES, tokens), f32)],
        compiler_params=params,
        cost_estimate=cost(1000),
    )(lengths, start, log_decay)

    spread = pltpu.VMEM((width, channels), bf16)
    block = pltpu.VMEM((big, channels), f32)
    hi, lo, slope_bc, r_high, r_low, g_high, g_low, send_adjoint = pl.pallas_call(
        functools.partial(adjoint_kernel, heads=heads),
        grid=(steps,),
        out_shape=(bc_bf16, bc_bf16, bc_f32) + (rows_bf16,) * 4 + (shape((N + 8, channels), f32),),
        in_specs=[
            smem, smem, by_rows(big, channels), by_rows(big, width), by_rows(big, 2 * N),
            whole(16, channels + 2 * N), whole(K, 2 * N), whole(8, channels),
        ],
        out_specs=(by_rows(big, 2 * N),) * 3 + (by_rows(big, channels),) * 4 + (whole(N + 8, channels),),
        scratch_shapes=[spread, spread, block, block, pltpu.VMEM((big + 8, 2 * N), f32)],
        compiler_params=params,
        cost_estimate=cost(1000),
    )(lengths, start, grad_out, scale, pre_bc, halo, conv_bc, through)

    slope_x, q_high, q_low, x_high, x_low, own_state, *messages = pl.pallas_call(
        functools.partial(state_kernel, heads=heads, count=count),
        grid=(steps,),
        out_shape=(rows_f32,) + (rows_bf16,) * 4 + (shape((N + 8, channels), f32),) * count,
        in_specs=[
            smem, smem, by_rows(big, channels), whole(16, channels + 2 * N), whole(K, channels),
            by_rows(big, width), by_rows(big, 2 * N), by_rows(big, 2 * N), whole(8, channels),
            whole(N + 8, channels),
        ],
        out_specs=(by_rows(big, channels),) * 5 + (whole(N + 8, channels),) * count,
        scratch_shapes=[spread, spread, block, block, pltpu.VMEM((big + 8, channels), f32)],
        compiler_params=params,
        cost_estimate=cost(1000),
    )(lengths, start, pre_x, halo, conv_x, scale, hi, lo, through, send_adjoint)
    received = [
        lax.ppermute(message, "seq", [(i, (i + lag) % count) for i in range(count)])
        for lag, message in enumerate(messages, 1)
    ]

    from_end = lambda rows, cols: pl.BlockSpec((rows, cols), lambda i: (chunks - 1 - i, 0))
    both_ways = [
        place(CHUNK, size)
        for place in (by_rows, from_end)
        for size in (channels, channels, channels, channels, 2 * N, 2 * N)
    ]
    dx, dbc, rate = pl.pallas_call(
        local_kernel,
        grid=(chunks,),
        out_shape=(rows_f32, bc_f32, shape((tokens, LANES), f32)),
        in_specs=[smem, smem, whole(2 * chunks, channels)] + both_ways,
        out_specs=(from_end(CHUNK, channels), whole(tokens, 2 * N), whole(tokens, LANES)),
        scratch_shapes=[
            pltpu.VMEM((N, channels), f32), pltpu.VMEM((N, channels), f32),
            pltpu.VMEM((channels, LANES), bf16),
        ]
        + [pltpu.VMEM((4 * CHUNK, channels), bf16)],
        compiler_params=params,
        cost_estimate=cost(8000),
    )(lengths, start, kappa, *([q_high, q_low, r_high, r_low, hi, lo] * 2))

    message = whole(N + 8, channels)
    s2, a2, end, head = pl.pallas_call(
        functools.partial(entering_kernel, count=count, heads=heads, tokens=tokens),
        grid=(1,),
        out_shape=(
            shape((2 * N, channels), bf16), shape((2 * N, channels), bf16), shape((8, channels), f32),
            shape((8, channels + 2 * N), f32),
        ),
        in_specs=[smem]
        + [message] * count
        + [whole(16, channels)] * 4
        + [whole(16, 2 * N)] * 2
        + [whole(16, width), whole(16, channels), whole(16, 2 * N), whole(16, channels), whole(16, 2 * N)],
        out_specs=(
            whole(2 * N, channels), whole(2 * N, channels), whole(8, channels),
            whole(8, channels + 2 * N),
        ),
        compiler_params=params,
        cost_estimate=cost(200),
    )(
        start, *received, own_state, g_high, g_low, x_high, x_low, hi, lo, scale, dx, dbc,
        slope_x, slope_bc,
    )
    after = shifted(head, "seq", -1)

    shared = pl.pallas_call(
        shared_kernel,
        grid=(steps,),
        out_shape=bc_f32,
        in_specs=[by_rows(big, channels)] * 4
        + [by_rows(big, 2 * N)] * 2
        + [whole(2 * N, channels)] * 2,
        out_specs=by_rows(big, 2 * N),
        compiler_params=params,
        cost_estimate=cost(1500),
    )(g_high, g_low, x_high, x_low, dbc, slope_bc, s2, a2)

    half = shape((tokens // 2, 2 * N), f32)
    keep, give = pl.pallas_call(
        functools.partial(arrange_kernel, sharers=sharers),
        out_shape=(half, half),
        in_specs=[smem, smem, smem, vmem, vmem, vmem],
        out_specs=(vmem, vmem),
        scratch_shapes=[pltpu.VMEM((tokens + 8, 2 * N), f32), pltpu.VMEM((tokens, 2 * N), f32)],
        compiler_params=params,
    )(lengths, start, mine, shared, after, conv_bc)
    grad_pre_bc = head_scatter(keep, give, mine, params)

    part = steps // 2
    tail, carry = after, end
    done = ()
    for first_block in (steps - 1, steps - 1 - part):
        back = lambda rows, cols, top=first_block: pl.BlockSpec((rows, cols), lambda i: (top - i, 0))
        grad_pre_x, grad_log, tail, carry = pl.pallas_call(
            functools.partial(final_kernel, heads=heads, first_block=first_block, last=not done),
            grid=(part,),
            out_shape=(
                rows_f32, shape((heads, tokens), f32), shape((8, channels), f32),
                shape((LANES, LANES), f32),
            ),
            in_specs=[smem, smem]
            + [back(big, channels)] * 4
            + [back(big, 2 * N)] * 2
            + [back(big, width)]
            + [back(big, channels)] * 2
            + [
                back(big, LANES), whole(2 * N, channels), whole(2 * N, channels),
                whole(K, channels), whole(*tail.shape), whole(*carry.shape),
            ]
            + [pl.BlockSpec(memory_space=pl.ANY)] * len(done),
            out_specs=(
                back(big, channels),
                pl.BlockSpec((heads, big), lambda i, top=first_block: (0, top - i)),
                whole(8, channels), whole(LANES, LANES),
            ),
            scratch_shapes=[
                spread, spread, pltpu.VMEM((channels, LANES), bf16),
                pltpu.VMEM((big + 8, channels), f32), pltpu.VMEM((2 * big, channels), bf16),
            ]
            + [pltpu.VMEM((big, min(2 * LANES, channels)), f32)] * 4,
            input_output_aliases={17 + i: i for i in range(len(done))},
            compiler_params=params,
            cost_estimate=cost(1500),
        )(
            lengths, start, g_high, g_low, x_high, x_low, hi, lo, scale, dx, slope_x, rate, s2, a2,
            conv_x, tail, carry, *done,
        )
        done = (grad_pre_x, grad_log)
    return (grad_pre_x, grad_pre_bc, grad_log)


def solution(mesh):
    placed = (
        P("seq", "head"),
        P("seq", None),
        P(None, "head"),
        P(),
        P("head", "seq"),
        P(),
        P("seq", "head"),
    )
    return jax.shard_map(
        local,
        mesh=mesh,
        in_specs=placed,
        out_specs=(P("seq", "head"), P(("seq", "head"), None), P("head", "seq")),
        check_vma=False,
    )
```

```python
import functools
import jax
import jax.numpy as jnp
from jax import lax
from jax.experimental import pallas as pl
from jax.experimental.pallas import tpu as pltpu
from jax.sharding import PartitionSpec as P

P_SIZE = 64
N = 128
K = 4
CHUNK = 64
LANES = 128
f32 = jnp.float32
bf16 = jnp.bfloat16
NN = (((1,), (0,)), ((), ()))
NT = (((1,), (1,)), ((), ()))
TN = (((0,), (0,)), ((), ()))
VMEM_LIMIT = 24 * 1024 * 1024


def split(value):
    high = value.astype(bf16)
    return high, (value - high.astype(f32)).astype(bf16)


def dot(left, right, dims=NN):
    return lax.dot_general(left, right, dims, preferred_element_type=f32)


def thirds(value):
    high, low = split(value)
    return high, low, (value - high.astype(f32) - low.astype(f32)).astype(bf16)


def exact(left, right, dims=NN):
    if isinstance(left, tuple):
        return dot(left[0], right, dims) + dot(left[1], right, dims) + dot(left[2], right, dims)
    return dot(left, right[0], dims) + dot(left, right[1], dims) + dot(left, right[2], dims)


def stack(*parts):
    return jnp.concatenate(parts, axis=0)


def dot3(left, right, dims=NN):
    rows = left[0].shape[0]
    most = dot(stack(*left), right[0], dims)
    return most[:rows] + most[rows:] + dot(left[0], right[1], dims)


def dot3_tn(left, right):
    return dot(stack(left[0], left[1], left[0]), stack(right[0], right[0], right[1]), TN)


def whole_of(parts):
    return parts[0].astype(f32) + parts[1].astype(f32)


def rows_iota(shape):
    return lax.broadcasted_iota(jnp.int32, shape, 0)


def cols_iota(shape):
    return lax.broadcasted_iota(jnp.int32, shape, 1)


def note_of(position, lens_ref):
    first = lens_ref[0]
    second = first + lens_ref[1]
    third = second + lens_ref[2]
    one = lambda flag: jnp.where(flag, 1, 0)
    return one(position >= 0) + one(position >= first) + one(position >= second) + one(
        position >= third
    )


def widen(block, width):
    return block if width == LANES else jnp.concatenate([block] * (width // LANES), axis=1)


def links(first, rows, sign, lens_ref):
    position = first + rows_iota((rows, LANES))
    here = note_of(position, lens_ref)
    return [
        jnp.where(note_of(position + sign * lag, lens_ref) == here, 1.0, 0.0) for lag in range(1, K)
    ]


def conv_tile(ext_ref, taps_ref, first, rows, over, linked, sign):
    total = ext_ref[first : first + rows, over] * taps_ref[K - 1 : K, over]
    for lag in range(1, K):
        moved = first + sign * lag
        tap = taps_ref[K - 1 - lag : K - lag, over]
        tap = tap if linked is None else tap * linked[lag - 1]
        total = total + ext_ref[moved : moved + rows, over] * tap
    return total


def near_start(position, rows, lens_ref):
    begins = [0, lens_ref[0], lens_ref[0] + lens_ref[1], lens_ref[0] + lens_ref[1] + lens_ref[2]]
    near = [(begin > position - K) & (begin < position + rows + K) for begin in begins]
    return near[0] | near[1] | near[2] | near[3]


def two_ways(position, rows, sign, lens_ref, body):
    cut = near_start(position, rows, lens_ref)

    @pl.when(cut)
    def _():
        body(lambda first, high: links(position + first, high, sign, lens_ref))

    @pl.when(jnp.logical_not(cut))
    def _():
        body(lambda first, high: None)


def silu_and_slope(u):
    sigma = 1.0 / (1.0 + jnp.exp(-u))
    value = u * sigma
    return value, sigma + value * (1.0 - sigma)


def expander(heads, channels, group):
    row = rows_iota((2 * LANES, channels)) % LANES
    own = cols_iota((2 * LANES, channels)) // P_SIZE
    return jnp.where(row == group * heads + own, 1.0, 0.0).astype(bf16)


def head_summer(channels):
    same = rows_iota((channels, LANES)) // P_SIZE == cols_iota((channels, LANES))
    return jnp.where(same, 1.0, 0.0).astype(bf16)


def edge_kernel(x_ref, bc_ref, edge_ref):
    channels = x_ref.shape[1]
    edge_ref[:, :channels] = x_ref[...]
    edge_ref[:, channels:] = bc_ref[...]


def scales_kernel(lens_ref, start_ref, log_ref, scale_ref, kappa_ref, through_ref, padded):
    heads, tokens = log_ref.shape
    channels = kappa_ref.shape[1]
    chunks = tokens // CHUNK
    start = start_ref[0]
    padded[...] = jnp.zeros_like(padded)
    for group in range(4):
        padded[group * heads : (group + 1) * heads, :] = log_ref[...]
    size = 2 * LANES
    square = (size, size)
    row, col = rows_iota(square), cols_iota(square)
    same = row // CHUNK == col // CHUNK
    one = lambda flag: jnp.where(flag, 1.0, 0.0)
    inner = one(same & (col <= row)) - one(same & (col % CHUNK < CHUNK // 2))
    sums = stack(inner, one(col <= row), one(col > row), jnp.ones((16, size), f32)).astype(bf16)
    blocks = tokens // size
    parts = thirds(padded[...])
    tables = [
        exact(sums, tuple(part[:, b * size : (b + 1) * size] for part in parts), NT)
        for b in range(blocks)
    ]
    totals = [table[3 * size : 3 * size + 1, :] for table in tables]
    offsets = [jnp.zeros((1, LANES), f32)]
    for total in totals:
        offsets.append(offsets[-1] + total)
    after = jnp.zeros((1, LANES), f32)
    note_before = note_of(start - 1, lens_ref)
    note_last = note_of(start + tokens - 1, lens_ref)
    shape = (size, LANES)
    group = cols_iota(shape) // heads
    for b in reversed(range(blocks)):
        near, ahead, behind = (tables[b][i * size : (i + 1) * size, :] for i in range(3))
        note = note_of(start + b * size + rows_iota(shape), lens_ref)
        power = jnp.where(group == 0, near, -near)
        power = jnp.where(group == 2, ahead + offsets[b], power)
        power = jnp.where(group >= 3, behind + after, power)
        kept = (group < 2) | ((group == 2) & (note == note_before)) | ((group == 3) & (note == note_last))
        after = after + totals[b]
        rows = slice(b * size, (b + 1) * size)
        scale_ref[rows, :LANES], scale_ref[rows, LANES:] = split(jnp.where(kept, jnp.exp(power), 0.0))
    spread = one(
        rows_iota((LANES, channels)) == cols_iota((LANES, channels)) // P_SIZE
    ).astype(bf16)
    half = CHUNK // 2
    chunk = rows_iota((chunks, tokens)) * CHUNK + half
    col = cols_iota((chunks, tokens))
    for place in range(2):
        begin = chunk + place * half
        steps = exact(one((col >= begin) & (col < begin + half)).astype(bf16), parts, NT)
        kappa_ref[place * chunks : (place + 1) * chunks, :] = exact(thirds(jnp.exp(steps)), spread)
    through = jnp.broadcast_to(jnp.exp(offsets[-1]), (8, LANES)) * one(note_before == note_last)
    through_ref[...] = exact(thirds(through), spread)


def tiles(rows, channels, high=64, wide=LANES):
    return [
        (slice(r, r + high), slice(c, c + wide))
        for r in range(0, rows, high)
        for c in range(0, channels, wide)
    ]


def adjoint_kernel(
    lens_ref, start_ref, grad_ref, scale_ref, pre_ref, halo_ref, taps_ref, through_ref,
    hi_ref, lo_ref, slope_ref, rh_ref, rl_ref, gh_ref, gl_ref, send_ref,
    spread, spread_r, ext, *, heads
):
    rows, channels = grad_ref.shape
    step = pl.program_id(0)

    @pl.when(step == 0)
    def _():
        spread[...] = expander(heads, channels, 2)
        spread_r[...] = expander(heads, channels, 0)
        send_ref[...] = jnp.zeros_like(send_ref)
        send_ref[N : N + 8, :] = through_ref[...]
        ext[0:8, :] = halo_ref[8:16, channels:].astype(f32)

    @pl.when(step > 0)
    def _():
        ext[0:8, :] = ext[rows : rows + 8, :]

    ext[8:, :] = pre_ref[...].astype(f32)
    scale = scale_ref[...]
    wide = min(2 * LANES, channels)

    def spreads(c):
        over = slice(c, c + wide)
        return dot(scale, spread[:, over]), dot(scale, spread_r[:, over])

    def conv(link):
        for first in range(0, rows, 64):
            at, linked = slice(first, first + 64), link(first, 64)
            for c in range(0, 2 * N, LANES):
                over = slice(c, c + LANES)
                u = conv_tile(ext, taps_ref, 8 + first, 64, over, linked, -1)
                value, slope_ref[at, over] = silu_and_slope(u)
                hi_ref[at, over], lo_ref[at, over] = split(value)

    two_ways(start_ref[0] + step * rows, rows, -1, lens_ref, conv)
    ready = spreads(0)
    for c in range(0, channels, wide):
        entry, near = ready
        ready = spreads(c + wide) if c + wide < channels else None
        for at, inside in tiles(rows, wide):
            over = slice(c + inside.start, c + inside.stop)
            grad = grad_ref[at, over].astype(f32)
            gh_ref[at, over], gl_ref[at, over] = split(grad * entry[at, inside])
            rh_ref[at, over], rl_ref[at, over] = split(grad * near[at, inside])
    send_ref[0:N, :] += dot3_tn((hi_ref[:, N:], lo_ref[:, N:]), (gh_ref[...], gl_ref[...]))


def state_kernel(
    lens_ref, start_ref, pre_ref, halo_ref, taps_ref, scale_ref, hi_ref, lo_ref, through_ref, other_ref,
    slope_ref, qh_ref, ql_ref, xh_ref, xl_ref, own_ref, *refs, heads, count
):
    messages = refs[: count - 1]
    spread, spread_q, ext = refs[count - 1 :]
    rows, channels = pre_ref.shape
    step, steps = pl.program_id(0), pl.num_programs(0)

    @pl.when(step == 0)
    def _():
        spread[...] = expander(heads, channels, 3)
        spread_q[...] = expander(heads, channels, 1)
        own_ref[...] = jnp.zeros_like(own_ref)
        own_ref[N : N + 8, :] = through_ref[...]
        ext[0:8, :] = halo_ref[8:16, :channels].astype(f32)

    @pl.when(step > 0)
    def _():
        ext[0:8, :] = ext[rows : rows + 8, :]

    ext[8:, :] = pre_ref[...].astype(f32)
    scale = scale_ref[...]
    wide = min(2 * LANES, channels)

    def spreads(c):
        over = slice(c, c + wide)
        return dot(scale, spread[:, over]), dot(scale, spread_q[:, over])

    def body(link):
        ready = spreads(0)
        linked = [link(first, 64) for first in range(0, rows, 64)]
        for c in range(0, channels, wide):
            leave, near = ready
            ready = spreads(c + wide) if c + wide < channels else None
            for at, inside in tiles(rows, wide):
                over = slice(c + inside.start, c + inside.stop)
                u = conv_tile(ext, taps_ref, 8 + at.start, 64, over, linked[at.start // 64], -1)
                value, slope_ref[at, over] = silu_and_slope(u)
                xh_ref[at, over], xl_ref[at, over] = split(value * leave[at, inside])
                qh_ref[at, over], ql_ref[at, over] = split(value * near[at, inside])

    two_ways(start_ref[0] + step * rows, rows, -1, lens_ref, body)
    own_ref[0:N, :] += dot3_tn((hi_ref[:, :N], lo_ref[:, :N]), (xh_ref[...], xl_ref[...]))

    @pl.when(step == steps - 1)
    def _():
        for lag in range(1, count):
            ahead = start_ref[0] + lag * rows * steps < count * rows * steps
            messages[lag - 1][...] = jnp.where(ahead, own_ref[...], other_ref[...])


def local_kernel(
    lens_ref, start_ref, kappa_ref,
    fx_h, fx_l, fg_h, fg_l, f_hi, f_lo, bx_h, bx_l, bg_h, bg_l, b_hi, b_lo,
    dx_ref, dbc_ref, rate_ref, state, adjoint, summer, product
):
    step = pl.program_id(0)
    chunks = pl.num_programs(0)
    channels = dx_ref.shape[1]
    here, there = step, chunks - 1 - step

    @pl.when(step == 0)
    def _():
        summer[...] = head_summer(channels)
        state[...] = jnp.zeros_like(state)
        adjoint[...] = jnp.zeros_like(adjoint)
        dbc_ref[...] = jnp.zeros_like(dbc_ref)
        rate_ref[...] = jnp.zeros_like(rate_ref)

    square = (CHUNK, CHUNK)
    row, col = rows_iota(square), cols_iota(square)
    pick = lambda flag, parts: tuple(
        jnp.where(flag, part.astype(f32), 0.0).astype(bf16) for part in parts
    )
    beside = lambda left, right: tuple(jnp.concatenate(p, axis=1) for p in zip(left, right))
    below = lambda left, right: tuple(stack(*p) for p in zip(left, right))
    turned = lambda parts: stack(parts[0], parts[1], parts[0]).astype(f32).T.astype(bf16)

    def setting(chunk, hi_ref, lo_ref):
        first = start_ref[0] + chunk * CHUNK
        note_before = note_of(first - 1, lens_ref)
        note_last = note_of(first + CHUNK - 1, lens_ref)
        keep = jnp.where(note_before == note_last, 1.0, 0.0)
        note = note_of(first + rows_iota((CHUNK, LANES)), lens_ref)
        linked = note_of(first + row, lens_ref) == note_of(first + col, lens_ref)
        b_parts = (hi_ref[:, :N], lo_ref[:, :N])
        c_parts = (hi_ref[:, N:], lo_ref[:, N:])
        return keep, note == note_before, note == note_last, linked, b_parts, c_parts

    def walk(ref, left, turn, x_refs, keep, place, over):
        held = ref[:, over]
        held_parts = split(held)
        x_parts = (x_refs[0][:, over], x_refs[1][:, over])
        right = below(held_parts, x_parts)
        fresh = dot(turn, stack(x_parts[0], x_parts[0], x_parts[1]))
        moved = (held * keep + fresh) * kappa_ref[pl.ds(place, 1), over]
        ref[:, over] = moved * kappa_ref[pl.ds(chunks + place, 1), over]
        return dot3(left, right), right, held_parts

    rows_f = pl.ds(pl.multiple_of(here * CHUNK, CHUNK), CHUNK)
    rows_b = pl.ds(pl.multiple_of(there * CHUNK, CHUNK), CHUNK)
    f_keep, f_enters, f_leaves, f_linked, fb, fc = setting(here, f_hi, f_lo)
    b_keep, b_enters, b_leaves, b_linked, bb, bc = setting(there, b_hi, b_lo)
    f_scores = jnp.where(f_linked & (col < row), dot3(fc, fb, NT), 0.0)
    b_scores = jnp.where(b_linked & (row < col), dot3(bb, bc, NT), 0.0)
    f_left = beside(pick(f_enters, fc), split(f_scores))
    b_left = beside(pick(b_leaves, bb), split(b_scores))
    f_turn, b_turn = turned(pick(f_leaves, fb)), turned(pick(b_enters, bc))
    own = jnp.sum(whole_of(bb) * whole_of(bc), axis=1, keepdims=True)
    wide = min(2 * LANES, channels)
    inner = outer = 0.0
    for first in range(0, channels, wide):
        over = slice(first, first + wide)
        y, right, _ = walk(state, f_left, f_turn, (fx_h, fx_l), f_keep, here, over)
        inner = inner + dot3((fg_h[:, over], fg_l[:, over]), right, NT)
        product[0:CHUNK, over], product[CHUNK : 2 * CHUNK, over] = split(
            whole_of((fg_h[:, over], fg_l[:, over])) * y
        )
        before = jnp.maximum(there - 1, 0)
        dx, _, a_parts = walk(adjoint, b_left, b_turn, (bg_h, bg_l), b_keep, before, over)
        outer = outer + dot3((bx_h[:, over], bx_l[:, over]), a_parts, NT)
        dx_ref[:, over] = dx + own * whole_of((bg_h[:, over], bg_l[:, over]))
        product[2 * CHUNK : 3 * CHUNK, over], product[3 * CHUNK :, over] = split(
            whole_of((bx_h[:, over], bx_l[:, over])) * dx
        )
    d_scores = split(jnp.where(f_linked & (col <= row), inner[:, N:], 0.0))
    for_c = jnp.where(f_enters, inner[:, :N], 0.0) + dot3(d_scores, fb)
    for_b = dot3_tn(d_scores, fc)
    dbc_ref[rows_f, :] += jnp.concatenate([for_b, for_c], axis=1)
    dbc_ref[rows_b, :N] += jnp.where(b_leaves, outer, 0.0)
    rates = dot(product[...], summer[...])
    rate_ref[rows_f, :] += rates[:CHUNK] + rates[CHUNK : 2 * CHUNK]
    rate_ref[rows_b, :] -= rates[2 * CHUNK : 3 * CHUNK] + rates[3 * CHUNK :]


def joined(messages):
    total = jnp.zeros((N, messages[0].shape[1]), f32)
    for message in reversed(messages):
        total = message[0:N, :] + message[N : N + 1, :] * total
    return total


def pull(high, low, both):
    most = dot(high, both[...], NT)
    return most[:, :N] + most[:, N:] + dot(low, both[0:N, :], NT)


def push(high, low, both, over=slice(None)):
    first = both[0:N, over]
    return dot(jnp.concatenate([high, low, high], axis=1), stack(first, first, both[N:, over]))


def entering_kernel(start_ref, *refs, count, heads, tokens):
    messages = refs[: count - 1]
    place = start_ref[0]
    forward = [
        jnp.where(place >= lag * tokens, messages[lag - 1][...], 0.0) for lag in range(1, count)
    ]
    backward = [
        jnp.where(place + lag * tokens < count * tokens, messages[count - 1 - lag][...], 0.0)
        for lag in range(1, count)
    ]
    (
        own_ref, gh_ref, gl_ref, xh_ref, xl_ref, hi_ref, lo_ref, scale_ref, dx_ref, dbc_ref,
        slope_ref, slope_bc_ref, s2_ref, a2_ref, end_ref, head_ref,
    ) = refs[count - 1 :]
    channels = gh_ref.shape[1]
    state, adjoint = joined(forward), joined(backward)
    s2_ref[0:N, :], s2_ref[N:, :] = split(state)
    a2_ref[0:N, :], a2_ref[N:, :] = split(adjoint)
    last = own_ref[0:N, :] + own_ref[N : N + 1, :] * state
    end_ref[...] = jnp.broadcast_to(jnp.sum(last * adjoint, axis=0, keepdims=True), end_ref.shape)
    for_c = pull(gh_ref[...], gl_ref[...], s2_ref)
    for_b = pull(xh_ref[...], xl_ref[...], a2_ref)
    shared = (dbc_ref[...] + jnp.concatenate([for_b, for_c], axis=1)) * slope_bc_ref[...]
    scale = scale_ref[...]
    dx = dx_ref[...] * dot(scale, expander(heads, channels, 1))
    dx = dx + push(hi_ref[:, :N], lo_ref[:, :N], a2_ref) * dot(scale, expander(heads, channels, 3))
    head_ref[:, :channels] = (dx * slope_ref[...])[0:8, :]
    head_ref[:, channels:] = shared[0:8, :]


def shared_kernel(gh_ref, gl_ref, xh_ref, xl_ref, dbc_ref, slope_ref, s2_ref, a2_ref, out_ref):
    for_c = pull(gh_ref[...], gl_ref[...], s2_ref)
    for_b = pull(xh_ref[...], xl_ref[...], a2_ref)
    out_ref[...] = (dbc_ref[...] + jnp.concatenate([for_b, for_c], axis=1)) * slope_ref[...]


def arrange_kernel(
    lens_ref, start_ref, side_ref, shared_ref, halo_ref, taps_ref, keep_ref, give_ref, ext, total, *, sharers
):
    tokens = shared_ref.shape[0]
    ext[0:tokens, :] = shared_ref[...]
    ext[tokens:, :] = halo_ref[:, -2 * N :]
    size = tokens // sharers
    high = 64
    odd = side_ref[0] % 2 == 1

    for first in range(0, tokens, high):

        def body(link, at=slice(first, first + high)):
            linked = link(0, high)
            for c in range(0, 2 * N, LANES):
                over = slice(c, c + LANES)
                total[at, over] = conv_tile(ext, taps_ref, at.start, high, over, linked, 1)

        two_ways(start_ref[0] + first, high, 1, lens_ref, body)
    for pair in range(sharers // 2):
        even, uneven = (total[(2 * pair + i) * size : (2 * pair + i + 1) * size, :] for i in range(2))
        at = slice(pair * size, (pair + 1) * size)
        keep_ref[at, :] = jnp.where(odd, uneven, even)
        give_ref[at, :] = jnp.where(odd, even, uneven)


def final_kernel(
    lens_ref, start_ref, gh_ref, gl_ref, xh_ref, xl_ref, hi_ref, lo_ref, scale_ref,
    dx_ref, slope_ref, rate_ref, s2_ref, a2_ref, taps_ref, tail_ref, end_ref,
    out_ref, log_ref, carry, spread, spread_q, summer, ext, product, *, heads
):
    step = pl.program_id(0)
    rows, channels = gh_ref.shape

    @pl.when(step == 0)
    def _():
        spread[...] = expander(heads, channels, 3)
        spread_q[...] = expander(heads, channels, 1)
        summer[...] = head_summer(channels)
        ext[rows:, :] = tail_ref[:, :channels]
        carry[...] = jnp.zeros_like(carry)

    @pl.when(step > 0)
    def _():
        ext[rows:, :] = ext[0:8, :]

    scale = scale_ref[...]
    wide = min(2 * LANES, channels)

    def products(c):
        over = slice(c, c + wide)
        return (
            push(hi_ref[:, N:], lo_ref[:, N:], s2_ref, over),
            push(hi_ref[:, :N], lo_ref[:, :N], a2_ref, over),
            dot(scale, spread_q[:, over]),
            dot(scale, spread[:, over]),
        )

    ready = products(0)
    for c in range(0, channels, wide):
        y, entered, near, leave = ready
        ready = products(c + wide) if c + wide < channels else None
        for at, inside in tiles(rows, wide):
            over = slice(c + inside.start, c + inside.stop)
            dx = entered[at, inside]
            rate = whole_of((gh_ref[at, over], gl_ref[at, over])) * y[at, inside]
            rate = rate - whole_of((xh_ref[at, over], xl_ref[at, over])) * dx
            product[at, over], product[rows + at.start : rows + at.stop, over] = split(rate)
            grad = dx_ref[at, over] * near[at, inside] + dx * leave[at, inside]
            ext[at, over] = grad * slope_ref[at, over]
    rates = dot(product[...], summer[...])
    rates = rate_ref[...] + rates[:rows] + rates[rows:]
    end_row = (rows_iota((rows, LANES)) == rows - 1) & (step == 0)
    beyond = exact(thirds(end_ref[...]), summer[...])[0:1, :]
    rates = rates + jnp.where(end_row, beyond, 0.0)
    later = rows_iota((rows, rows)) >= cols_iota((rows, rows))
    ones = jnp.ones((rows, LANES), f32)
    marks = jnp.concatenate([jnp.where(later, 1.0, 0.0), ones], axis=1).astype(bf16)
    sums = exact(thirds(rates), marks, TN)
    log = sums[:, :rows] + widen(carry[...], rows)
    log_ref[...] = log[0:heads, :]
    carry[...] += sums[:, rows:]
    first = start_ref[0] + (pl.num_programs(0) - 1 - step) * rows

    def body(link):
        for r in range(0, rows, 64):
            at, linked = slice(r, r + 64), link(r, 64)
            for c in range(0, channels, LANES):
                over = slice(c, c + LANES)
                out_ref[at, over] = conv_tile(ext, taps_ref, r, 64, over, linked, 1)

    two_ways(first, rows, 1, lens_ref, body)


def shifted(value, axis, steps):
    count = lax.axis_size(axis)
    initial, last = (max(0, -steps), min(count, count - steps))
    return lax.ppermute(value, axis, [(source, source + steps) for source in range(initial, last)])


def merge_kernel(side_ref, kept_ref, came_ref, keep_ref, give_ref):
    odd = side_ref[0] == 1
    for pair in range(keep_ref.shape[0]):
        even, uneven = (kept_ref[2 * pair + i] + came_ref[2 * pair + i] for i in range(2))
        keep_ref[pair] = jnp.where(odd, uneven, even)
        give_ref[pair] = jnp.where(odd, even, uneven)


def pieces_kernel(place_ref, kept_ref, came_ref, *piece_refs):
    for i, piece_ref in enumerate(piece_refs):
        block = place_ref[0] ^ i
        piece_ref[...] = kept_ref[block] + came_ref[block]


def total_kernel(*refs):
    total = refs[0][...]
    for ref in refs[1:-1]:
        total = total + ref[...]
    refs[-1][...] = total


def head_scatter(keep, give, mine, params):
    count = lax.axis_size("head")
    swap = lambda value, bits: lax.ppermute(value, "head", [(i, i ^ bits) for i in range(count)])
    size, width = 2 * keep.shape[0] // count, keep.shape[1]
    blocks = lambda value: value.reshape(-1, size, width)
    smem = pl.BlockSpec(memory_space=pltpu.SMEM)
    vmem = pl.BlockSpec(memory_space=pltpu.VMEM)
    keep, give, bit = blocks(keep), blocks(give), 1
    while keep.shape[0] > 4:
        came = swap(give, bit)
        bit *= 2
        half = jax.ShapeDtypeStruct((keep.shape[0] // 2, size, width), f32)
        keep, give = pl.pallas_call(
            merge_kernel,
            out_shape=(half, half),
            in_specs=[smem, vmem, vmem],
            out_specs=(vmem, vmem),
            compiler_params=params,
        )((mine // bit) % 2, keep, came)
    came = swap(give, bit)
    bit *= 2
    left = keep.shape[0]
    block = jax.ShapeDtypeStruct((size, width), f32)
    pieces = pl.pallas_call(
        pieces_kernel,
        out_shape=(block,) * left,
        in_specs=[smem, vmem, vmem],
        out_specs=(vmem,) * left,
        compiler_params=params,
    )(mine // bit, keep, came)
    return pl.pallas_call(
        total_kernel,
        out_shape=block,
        in_specs=[vmem] * left,
        out_specs=vmem,
        compiler_params=params,
    )(pieces[0], *[swap(pieces[i], i * bit) for i in range(1, left)])


def local(pre_x, pre_bc, conv_x, conv_bc, log_decay, lengths, grad_out):
    tokens, channels = pre_x.shape
    heads = log_decay.shape[0]
    count = lax.axis_size("seq")
    sharers = lax.axis_size("head")
    chunks = tokens // CHUNK
    big = 256
    steps = tokens // big
    width = 2 * LANES
    start = (lax.axis_index("seq") * tokens).astype(jnp.int32).reshape(1)
    mine = lax.axis_index("head").astype(jnp.int32).reshape(1)
    shape = jax.ShapeDtypeStruct
    smem = pl.BlockSpec(memory_space=pltpu.SMEM)
    vmem = pl.BlockSpec(memory_space=pltpu.VMEM)
    params = pltpu.CompilerParams(vmem_limit_bytes=VMEM_LIMIT)
    by_rows = lambda rows, cols: pl.BlockSpec((rows, cols), lambda i: (i, 0))
    whole = lambda rows, cols: pl.BlockSpec((rows, cols), lambda *i: (0, 0))
    wide = tokens * channels
    cost = lambda work: pl.CostEstimate(flops=wide * work, bytes_accessed=wide * 16, transcendentals=0)
    grad_out = pltpu.with_memory_space_constraint(grad_out, pltpu.HBM)
    pre_x = pltpu.with_memory_space_constraint(pre_x, pltpu.HBM)
    pre_bc = pltpu.with_memory_space_constraint(pre_bc, pltpu.HBM)
    rows_f32, rows_bf16 = shape((tokens, channels), f32), shape((tokens, channels), bf16)
    bc_f32, bc_bf16 = shape((tokens, 2 * N), f32), shape((tokens, 2 * N), bf16)

    last_rows = lambda cols: pl.BlockSpec((16, cols), lambda i: (tokens // 16 - 1, 0))
    edge = pl.pallas_call(
        edge_kernel,
        grid=(1,),
        out_shape=shape((16, channels + 2 * N), bf16),
        in_specs=[last_rows(channels), last_rows(2 * N)],
        out_specs=whole(16, channels + 2 * N),
        compiler_params=params,
    )(pre_x, pre_bc)
    halo = shifted(edge, "seq", 1)

    scale, kappa, through = pl.pallas_call(
        scales_kernel,
        out_shape=(
            shape((tokens, width), bf16), shape((2 * chunks, channels), f32), shape((8, channels), f32),
        ),
        in_specs=[smem, smem, vmem],
        out_specs=(vmem,) * 3,
        scratch_shapes=[pltpu.VMEM((LANES, tokens), f32)],
        compiler_params=params,
        cost_estimate=cost(1000),
    )(lengths, start, log_decay)

    spread = pltpu.VMEM((width, channels), bf16)
    hi, lo, slope_bc, r_high, r_low, g_high, g_low, send_adjoint = pl.pallas_call(
        functools.partial(adjoint_kernel, heads=heads),
        grid=(steps,),
        out_shape=(bc_bf16, bc_bf16, bc_f32) + (rows_bf16,) * 4 + (shape((N + 8, channels), f32),),
        in_specs=[
            smem, smem, by_rows(big, channels), by_rows(big, width), by_rows(big, 2 * N),
            whole(16, channels + 2 * N), whole(K, 2 * N), whole(8, channels),
        ],
        out_specs=(by_rows(big, 2 * N),) * 3 + (by_rows(big, channels),) * 4 + (whole(N + 8, channels),),
        scratch_shapes=[spread, spread, pltpu.VMEM((big + 8, 2 * N), f32)],
        compiler_params=params,
        cost_estimate=cost(1000),
    )(lengths, start, grad_out, scale, pre_bc, halo, conv_bc, through)

    slope_x, q_high, q_low, x_high, x_low, own_state, *messages = pl.pallas_call(
        functools.partial(state_kernel, heads=heads, count=count),
        grid=(steps,),
        out_shape=(rows_f32,) + (rows_bf16,) * 4 + (shape((N + 8, channels), f32),) * count,
        in_specs=[
            smem, smem, by_rows(big, channels), whole(16, channels + 2 * N), whole(K, channels),
            by_rows(big, width), by_rows(big, 2 * N), by_rows(big, 2 * N), whole(8, channels),
            whole(N + 8, channels),
        ],
        out_specs=(by_rows(big, channels),) * 5 + (whole(N + 8, channels),) * count,
        scratch_shapes=[spread, spread, pltpu.VMEM((big + 8, channels), f32)],
        compiler_params=params,
        cost_estimate=cost(1000),
    )(lengths, start, pre_x, halo, conv_x, scale, hi, lo, through, send_adjoint)
    received = [
        lax.ppermute(message, "seq", [(i, (i + lag) % count) for i in range(count)])
        for lag, message in enumerate(messages, 1)
    ]

    from_end = lambda rows, cols: pl.BlockSpec((rows, cols), lambda i: (chunks - 1 - i, 0))
    both_ways = [
        place(CHUNK, size)
        for place in (by_rows, from_end)
        for size in (channels, channels, channels, channels, 2 * N, 2 * N)
    ]
    dx, dbc, rate = pl.pallas_call(
        local_kernel,
        grid=(chunks,),
        out_shape=(rows_f32, bc_f32, shape((tokens, LANES), f32)),
        in_specs=[smem, smem, whole(2 * chunks, channels)] + both_ways,
        out_specs=(from_end(CHUNK, channels), whole(tokens, 2 * N), whole(tokens, LANES)),
        scratch_shapes=[
            pltpu.VMEM((N, channels), f32), pltpu.VMEM((N, channels), f32),
            pltpu.VMEM((channels, LANES), bf16),
        ]
        + [pltpu.VMEM((4 * CHUNK, channels), bf16)],
        compiler_params=params,
        cost_estimate=cost(8000),
    )(lengths, start, kappa, *([q_high, q_low, r_high, r_low, hi, lo] * 2))

    message = whole(N + 8, channels)
    s2, a2, end, head = pl.pallas_call(
        functools.partial(entering_kernel, count=count, heads=heads, tokens=tokens),
        grid=(1,),
        out_shape=(
            shape((2 * N, channels), bf16), shape((2 * N, channels), bf16), shape((8, channels), f32),
            shape((8, channels + 2 * N), f32),
        ),
        in_specs=[smem]
        + [message] * count
        + [whole(16, channels)] * 4
        + [whole(16, 2 * N)] * 2
        + [whole(16, width), whole(16, channels), whole(16, 2 * N), whole(16, channels), whole(16, 2 * N)],
        out_specs=(
            whole(2 * N, channels), whole(2 * N, channels), whole(8, channels),
            whole(8, channels + 2 * N),
        ),
        compiler_params=params,
        cost_estimate=cost(200),
    )(
        start, *received, own_state, g_high, g_low, x_high, x_low, hi, lo, scale, dx, dbc,
        slope_x, slope_bc,
    )
    after = shifted(head, "seq", -1)

    high = 512
    shared = pl.pallas_call(
        shared_kernel,
        grid=(tokens // high,),
        out_shape=bc_f32,
        in_specs=[by_rows(high, channels)] * 4
        + [by_rows(high, 2 * N)] * 2
        + [whole(2 * N, channels)] * 2,
        out_specs=by_rows(high, 2 * N),
        compiler_params=params,
        cost_estimate=cost(1500),
    )(g_high, g_low, x_high, x_low, dbc, slope_bc, s2, a2)

    half = shape((tokens // 2, 2 * N), f32)
    keep, give = pl.pallas_call(
        functools.partial(arrange_kernel, sharers=sharers),
        out_shape=(half, half),
        in_specs=[smem, smem, smem, vmem, vmem, vmem],
        out_specs=(vmem, vmem),
        scratch_shapes=[pltpu.VMEM((tokens + 8, 2 * N), f32), pltpu.VMEM((tokens, 2 * N), f32)],
        compiler_params=params,
    )(lengths, start, mine, shared, after, conv_bc)
    grad_pre_bc = head_scatter(keep, give, mine, params)

    back = lambda rows, cols: pl.BlockSpec((rows, cols), lambda i: (steps - 1 - i, 0))
    grad_pre_x, grad_log = pl.pallas_call(
        functools.partial(final_kernel, heads=heads),
        grid=(steps,),
        out_shape=(rows_f32, shape((heads, tokens), f32)),
        in_specs=[smem, smem]
        + [back(big, channels)] * 4
        + [back(big, 2 * N)] * 2
        + [back(big, width)]
        + [back(big, channels)] * 2
        + [
            back(big, LANES), whole(2 * N, channels), whole(2 * N, channels),
            whole(K, channels), whole(8, channels + 2 * N), whole(8, channels),
        ],
        out_specs=(
            back(big, channels), pl.BlockSpec((heads, big), lambda i: (0, steps - 1 - i)),
        ),
        scratch_shapes=[
            pltpu.VMEM((LANES, LANES), f32), spread, spread, pltpu.VMEM((channels, LANES), bf16),
            pltpu.VMEM((big + 8, channels), f32), pltpu.VMEM((2 * big, channels), bf16),
        ],
        compiler_params=params,
        cost_estimate=cost(3000),
    )(
        lengths, start, g_high, g_low, x_high, x_low, hi, lo, scale, dx, slope_x, rate, s2, a2,
        conv_x, after, end,
    )
    return (grad_pre_x, grad_pre_bc, grad_log)


def solution(mesh):
    placed = (
        P("seq", "head"),
        P("seq", None),
        P(None, "head"),
        P(),
        P("head", "seq"),
        P(),
        P("seq", "head"),
    )
    return jax.shard_map(
        local,
        mesh=mesh,
        in_specs=placed,
        out_specs=(P("seq", "head"), P(("seq", "head"), None), P("head", "seq")),
        check_vma=False,
    )
```

```python
import functools
import jax
import jax.numpy as jnp
from jax import lax
from jax.experimental import pallas as pl
from jax.experimental.pallas import tpu as pltpu
from jax.sharding import PartitionSpec as P

P_SIZE = 64
N = 128
K = 4
CHUNK = 64
LANES = 128
f32 = jnp.float32
bf16 = jnp.bfloat16
NN = (((1,), (0,)), ((), ()))
NT = (((1,), (1,)), ((), ()))
TN = (((0,), (0,)), ((), ()))
VMEM_LIMIT = 24 * 1024 * 1024


def split(value):
    high = value.astype(bf16)
    return high, (value - high.astype(f32)).astype(bf16)


def dot(left, right, dims=NN):
    return lax.dot_general(left, right, dims, preferred_element_type=f32)


def thirds(value):
    high, low = split(value)
    return high, low, (value - high.astype(f32) - low.astype(f32)).astype(bf16)


def exact(left, right, dims=NN):
    if isinstance(left, tuple):
        return dot(left[0], right, dims) + dot(left[1], right, dims) + dot(left[2], right, dims)
    return dot(left, right[0], dims) + dot(left, right[1], dims) + dot(left, right[2], dims)


def stack(*parts):
    return jnp.concatenate(parts, axis=0)


def dot3(left, right, dims=NN):
    rows = left[0].shape[0]
    most = dot(stack(*left), right[0], dims)
    return most[:rows] + most[rows:] + dot(left[0], right[1], dims)


def dot3_tn(left, right):
    return dot(stack(left[0], left[1], left[0]), stack(right[0], right[0], right[1]), TN)


def whole_of(parts):
    return parts[0].astype(f32) + parts[1].astype(f32)


def rows_iota(shape):
    return lax.broadcasted_iota(jnp.int32, shape, 0)


def cols_iota(shape):
    return lax.broadcasted_iota(jnp.int32, shape, 1)


def note_of(position, lens_ref):
    first = lens_ref[0]
    second = first + lens_ref[1]
    third = second + lens_ref[2]
    one = lambda flag: jnp.where(flag, 1, 0)
    return one(position >= 0) + one(position >= first) + one(position >= second) + one(
        position >= third
    )


def widen(block, width):
    return block if width == LANES else jnp.concatenate([block] * (width // LANES), axis=1)


def links(first, rows, sign, lens_ref):
    position = first + rows_iota((rows, LANES))
    here = note_of(position, lens_ref)
    return [
        jnp.where(note_of(position + sign * lag, lens_ref) == here, 1.0, 0.0) for lag in range(1, K)
    ]


def conv_tile(ext_ref, taps_ref, first, rows, over, linked, sign):
    total = ext_ref[first : first + rows, over] * taps_ref[K - 1 : K, over]
    for lag in range(1, K):
        moved = first + sign * lag
        tap = taps_ref[K - 1 - lag : K - lag, over]
        tap = tap if linked is None else tap * linked[lag - 1]
        total = total + ext_ref[moved : moved + rows, over] * tap
    return total


def near_start(position, rows, lens_ref):
    begins = [0, lens_ref[0], lens_ref[0] + lens_ref[1], lens_ref[0] + lens_ref[1] + lens_ref[2]]
    near = [(begin > position - K) & (begin < position + rows + K) for begin in begins]
    return near[0] | near[1] | near[2] | near[3]


def two_ways(position, rows, sign, lens_ref, body):
    cut = near_start(position, rows, lens_ref)

    @pl.when(cut)
    def _():
        body(lambda first, high: links(position + first, high, sign, lens_ref))

    @pl.when(jnp.logical_not(cut))
    def _():
        body(lambda first, high: None)


def silu_and_slope(u):
    sigma = 1.0 / (1.0 + jnp.exp(-u))
    value = u * sigma
    return value, sigma + value * (1.0 - sigma)


def expander(heads, channels, group):
    row = rows_iota((2 * LANES, channels)) % LANES
    own = cols_iota((2 * LANES, channels)) // P_SIZE
    return jnp.where(row == group * heads + own, 1.0, 0.0).astype(bf16)


def head_summer(channels):
    same = rows_iota((channels, LANES)) // P_SIZE == cols_iota((channels, LANES))
    return jnp.where(same, 1.0, 0.0).astype(bf16)


def edge_kernel(x_ref, bc_ref, edge_ref):
    channels = x_ref.shape[1]
    edge_ref[:, :channels] = x_ref[...]
    edge_ref[:, channels:] = bc_ref[...]


def scales_kernel(lens_ref, start_ref, log_ref, scale_ref, kappa_ref, through_ref, padded):
    heads, tokens = log_ref.shape
    channels = kappa_ref.shape[1]
    chunks = tokens // CHUNK
    start = start_ref[0]
    padded[...] = jnp.zeros_like(padded)
    for group in range(4):
        padded[group * heads : (group + 1) * heads, :] = log_ref[...]
    size = 2 * LANES
    square = (size, size)
    row, col = rows_iota(square), cols_iota(square)
    same = row // CHUNK == col // CHUNK
    one = lambda flag: jnp.where(flag, 1.0, 0.0)
    inner = one(same & (col <= row)) - one(same & (col % CHUNK < CHUNK // 2))
    sums = stack(inner, one(col <= row), one(col > row), jnp.ones((16, size), f32)).astype(bf16)
    blocks = tokens // size
    parts = thirds(padded[...])
    tables = [
        exact(sums, tuple(part[:, b * size : (b + 1) * size] for part in parts), NT)
        for b in range(blocks)
    ]
    totals = [table[3 * size : 3 * size + 1, :] for table in tables]
    offsets = [jnp.zeros((1, LANES), f32)]
    for total in totals:
        offsets.append(offsets[-1] + total)
    after = jnp.zeros((1, LANES), f32)
    note_before = note_of(start - 1, lens_ref)
    note_last = note_of(start + tokens - 1, lens_ref)
    shape = (size, LANES)
    group = cols_iota(shape) // heads
    for b in reversed(range(blocks)):
        near, ahead, behind = (tables[b][i * size : (i + 1) * size, :] for i in range(3))
        note = note_of(start + b * size + rows_iota(shape), lens_ref)
        power = jnp.where(group == 0, near, -near)
        power = jnp.where(group == 2, ahead + offsets[b], power)
        power = jnp.where(group >= 3, behind + after, power)
        kept = (group < 2) | ((group == 2) & (note == note_before)) | ((group == 3) & (note == note_last))
        after = after + totals[b]
        rows = slice(b * size, (b + 1) * size)
        scale_ref[rows, :LANES], scale_ref[rows, LANES:] = split(jnp.where(kept, jnp.exp(power), 0.0))
    spread = one(
        rows_iota((LANES, channels)) == cols_iota((LANES, channels)) // P_SIZE
    ).astype(bf16)
    half = CHUNK // 2
    chunk = rows_iota((chunks, tokens)) * CHUNK + half
    col = cols_iota((chunks, tokens))
    for place in range(2):
        begin = chunk + place * half
        steps = exact(one((col >= begin) & (col < begin + half)).astype(bf16), parts, NT)
        kappa_ref[place * chunks : (place + 1) * chunks, :] = exact(thirds(jnp.exp(steps)), spread)
    through = jnp.broadcast_to(jnp.exp(offsets[-1]), (8, LANES)) * one(note_before == note_last)
    through_ref[...] = exact(thirds(through), spread)


def tiles(rows, channels, high=64, wide=LANES):
    return [
        (slice(r, r + high), slice(c, c + wide))
        for r in range(0, rows, high)
        for c in range(0, channels, wide)
    ]


def adjoint_kernel(
    lens_ref, start_ref, grad_ref, scale_ref, pre_ref, halo_ref, taps_ref, through_ref,
    hi_ref, lo_ref, slope_ref, rh_ref, rl_ref, gh_ref, gl_ref, send_ref,
    spread, spread_r, ext, *, heads
):
    rows, channels = grad_ref.shape
    step = pl.program_id(0)

    @pl.when(step == 0)
    def _():
        spread[...] = expander(heads, channels, 2)
        spread_r[...] = expander(heads, channels, 0)
        send_ref[...] = jnp.zeros_like(send_ref)
        send_ref[N : N + 8, :] = through_ref[...]
        ext[0:8, :] = halo_ref[8:16, channels:].astype(f32)

    @pl.when(step > 0)
    def _():
        ext[0:8, :] = ext[rows : rows + 8, :]

    ext[8:, :] = pre_ref[...].astype(f32)
    scale = scale_ref[...]
    wide = min(2 * LANES, channels)

    def spreads(c):
        over = slice(c, c + wide)
        return dot(scale, spread[:, over]), dot(scale, spread_r[:, over])

    def conv(link):
        for first in range(0, rows, 64):
            at, linked = slice(first, first + 64), link(first, 64)
            for c in range(0, 2 * N, LANES):
                over = slice(c, c + LANES)
                u = conv_tile(ext, taps_ref, 8 + first, 64, over, linked, -1)
                value, slope_ref[at, over] = silu_and_slope(u)
                hi_ref[at, over], lo_ref[at, over] = split(value)

    two_ways(start_ref[0] + step * rows, rows, -1, lens_ref, conv)
    ready = spreads(0)
    for c in range(0, channels, wide):
        entry, near = ready
        ready = spreads(c + wide) if c + wide < channels else None
        for at, inside in tiles(rows, wide):
            over = slice(c + inside.start, c + inside.stop)
            grad = grad_ref[at, over].astype(f32)
            gh_ref[at, over], gl_ref[at, over] = split(grad * entry[at, inside])
            rh_ref[at, over], rl_ref[at, over] = split(grad * near[at, inside])
    send_ref[0:N, :] += dot3_tn((hi_ref[:, N:], lo_ref[:, N:]), (gh_ref[...], gl_ref[...]))


def state_kernel(
    lens_ref, start_ref, pre_ref, halo_ref, taps_ref, scale_ref, hi_ref, lo_ref, through_ref, other_ref,
    slope_ref, qh_ref, ql_ref, xh_ref, xl_ref, own_ref, *refs, heads, count
):
    messages = refs[: count - 1]
    spread, spread_q, ext = refs[count - 1 :]
    rows, channels = pre_ref.shape
    step, steps = pl.program_id(0), pl.num_programs(0)

    @pl.when(step == 0)
    def _():
        spread[...] = expander(heads, channels, 3)
        spread_q[...] = expander(heads, channels, 1)
        own_ref[...] = jnp.zeros_like(own_ref)
        own_ref[N : N + 8, :] = through_ref[...]
        ext[0:8, :] = halo_ref[8:16, :channels].astype(f32)

    @pl.when(step > 0)
    def _():
        ext[0:8, :] = ext[rows : rows + 8, :]

    ext[8:, :] = pre_ref[...].astype(f32)
    scale = scale_ref[...]
    wide = min(2 * LANES, channels)

    def spreads(c):
        over = slice(c, c + wide)
        return dot(scale, spread[:, over]), dot(scale, spread_q[:, over])

    def body(link):
        ready = spreads(0)
        linked = [link(first, 64) for first in range(0, rows, 64)]
        for c in range(0, channels, wide):
            leave, near = ready
            ready = spreads(c + wide) if c + wide < channels else None
            for at, inside in tiles(rows, wide):
                over = slice(c + inside.start, c + inside.stop)
                u = conv_tile(ext, taps_ref, 8 + at.start, 64, over, linked[at.start // 64], -1)
                value, slope_ref[at, over] = silu_and_slope(u)
                xh_ref[at, over], xl_ref[at, over] = split(value * leave[at, inside])
                qh_ref[at, over], ql_ref[at, over] = split(value * near[at, inside])

    two_ways(start_ref[0] + step * rows, rows, -1, lens_ref, body)
    own_ref[0:N, :] += dot3_tn((hi_ref[:, :N], lo_ref[:, :N]), (xh_ref[...], xl_ref[...]))

    @pl.when(step == steps - 1)
    def _():
        for lag in range(1, count):
            ahead = start_ref[0] + lag * rows * steps < count * rows * steps
            for part in range(channels // LANES):
                over, at = slice(part * LANES, (part + 1) * LANES), N * part
                held = jnp.where(ahead, own_ref[:, over], other_ref[:, over])
                messages[lag - 1][at : at + N, :] = held[:N]
                messages[lag - 1][N * channels // LANES + part : N * channels // LANES + part + 1, :] = held[N : N + 1]


def local_kernel(
    lens_ref, start_ref, kappa_ref,
    fx_h, fx_l, fg_h, fg_l, f_hi, f_lo, bx_h, bx_l, bg_h, bg_l, b_hi, b_lo,
    scale_ref, dx_ref, dbc_ref, rate_ref, state, adjoint, summer, product, spread, *, heads
):
    step = pl.program_id(0)
    chunks = pl.num_programs(0)
    channels = dx_ref.shape[1]
    here, there = step, chunks - 1 - step

    @pl.when(step == 0)
    def _():
        summer[...] = head_summer(channels)
        spread[...] = expander(heads, channels, 1)
        state[...] = jnp.zeros_like(state)
        adjoint[...] = jnp.zeros_like(adjoint)
        dbc_ref[...] = jnp.zeros_like(dbc_ref)
        rate_ref[...] = jnp.zeros_like(rate_ref)

    square = (CHUNK, CHUNK)
    row, col = rows_iota(square), cols_iota(square)
    pick = lambda flag, parts: tuple(
        jnp.where(flag, part.astype(f32), 0.0).astype(bf16) for part in parts
    )
    beside = lambda left, right: tuple(jnp.concatenate(p, axis=1) for p in zip(left, right))
    below = lambda left, right: tuple(stack(*p) for p in zip(left, right))
    turned = lambda parts: stack(parts[0], parts[1], parts[0]).astype(f32).T.astype(bf16)

    def setting(chunk, hi_ref, lo_ref):
        first = start_ref[0] + chunk * CHUNK
        note_before = note_of(first - 1, lens_ref)
        note_last = note_of(first + CHUNK - 1, lens_ref)
        keep = jnp.where(note_before == note_last, 1.0, 0.0)
        note = note_of(first + rows_iota((CHUNK, LANES)), lens_ref)
        linked = note_of(first + row, lens_ref) == note_of(first + col, lens_ref)
        b_parts = (hi_ref[:, :N], lo_ref[:, :N])
        c_parts = (hi_ref[:, N:], lo_ref[:, N:])
        return keep, note == note_before, note == note_last, linked, b_parts, c_parts

    def walk(ref, left, turn, x_refs, keep, place, over):
        held = ref[:, over]
        held_parts = split(held)
        x_parts = (x_refs[0][:, over], x_refs[1][:, over])
        right = below(held_parts, x_parts)
        fresh = dot(turn, stack(x_parts[0], x_parts[0], x_parts[1]))
        moved = (held * keep + fresh) * kappa_ref[pl.ds(place, 1), over]
        ref[:, over] = moved * kappa_ref[pl.ds(chunks + place, 1), over]
        return dot3(left, right), right, held_parts

    rows_f = pl.ds(pl.multiple_of(here * CHUNK, CHUNK), CHUNK)
    rows_b = pl.ds(pl.multiple_of(there * CHUNK, CHUNK), CHUNK)
    f_keep, f_enters, f_leaves, f_linked, fb, fc = setting(here, f_hi, f_lo)
    b_keep, b_enters, b_leaves, b_linked, bb, bc = setting(there, b_hi, b_lo)
    f_scores = jnp.where(f_linked & (col < row), dot3(fc, fb, NT), 0.0)
    b_scores = jnp.where(b_linked & (row < col), dot3(bb, bc, NT), 0.0)
    f_left = beside(pick(f_enters, fc), split(f_scores))
    b_left = beside(pick(b_leaves, bb), split(b_scores))
    f_turn, b_turn = turned(pick(f_leaves, fb)), turned(pick(b_enters, bc))
    own = jnp.sum(whole_of(bb) * whole_of(bc), axis=1, keepdims=True)
    wide = min(2 * LANES, channels)
    inner = outer = 0.0
    for first in range(0, channels, wide):
        over = slice(first, first + wide)
        y, right, _ = walk(state, f_left, f_turn, (fx_h, fx_l), f_keep, here, over)
        inner = inner + dot3((fg_h[:, over], fg_l[:, over]), right, NT)
        product[0:CHUNK, over], product[CHUNK : 2 * CHUNK, over] = split(
            whole_of((fg_h[:, over], fg_l[:, over])) * y
        )
        before = jnp.maximum(there - 1, 0)
        dx, _, a_parts = walk(adjoint, b_left, b_turn, (bg_h, bg_l), b_keep, before, over)
        outer = outer + dot3((bx_h[:, over], bx_l[:, over]), a_parts, NT)
        near = dot(scale_ref[...], spread[:, over])
        dx_ref[:, over] = (dx + own * whole_of((bg_h[:, over], bg_l[:, over]))) * near
        product[2 * CHUNK : 3 * CHUNK, over], product[3 * CHUNK :, over] = split(
            whole_of((bx_h[:, over], bx_l[:, over])) * dx
        )
    d_scores = split(jnp.where(f_linked & (col <= row), inner[:, N:], 0.0))
    for_c = jnp.where(f_enters, inner[:, :N], 0.0) + dot3(d_scores, fb)
    for_b = dot3_tn(d_scores, fc)
    dbc_ref[rows_f, :] += jnp.concatenate([for_b, for_c], axis=1)
    dbc_ref[rows_b, :N] += jnp.where(b_leaves, outer, 0.0)
    rates = dot(product[...], summer[...])
    rate_ref[rows_f, :] += rates[:CHUNK] + rates[CHUNK : 2 * CHUNK]
    rate_ref[rows_b, :] -= rates[2 * CHUNK : 3 * CHUNK] + rates[3 * CHUNK :]


def joined(messages):
    parts = (messages[0].shape[0] - 8) // N
    tiles_of = []
    for part in range(parts):
        total = jnp.zeros((N, LANES), f32)
        for message in reversed(messages):
            through = message[N * parts + part : N * parts + part + 1, :]
            total = message[part * N : (part + 1) * N, :] + through * total
        tiles_of.append(total)
    return jnp.concatenate(tiles_of, axis=1)


def pull(high, low, both):
    most = dot(high, both[...], NT)
    return most[:, :N] + most[:, N:] + dot(low, both[0:N, :], NT)


def push(high, low, both, over=slice(None)):
    first = both[0:N, over]
    return dot(jnp.concatenate([high, low, high], axis=1), stack(first, first, both[N:, over]))


def entering_kernel(start_ref, *refs, count, heads, tokens):
    messages = refs[: count - 1]
    place = start_ref[0]
    forward = [
        jnp.where(place >= lag * tokens, messages[lag - 1][...], 0.0) for lag in range(1, count)
    ]
    backward = [
        jnp.where(place + lag * tokens < count * tokens, messages[count - 1 - lag][...], 0.0)
        for lag in range(1, count)
    ]
    (
        own_ref, gh_ref, gl_ref, xh_ref, xl_ref, hi_ref, lo_ref, scale_ref, dx_ref, dbc_ref,
        slope_ref, slope_bc_ref, s2_ref, a2_ref, end_ref, head_ref,
    ) = refs[count - 1 :]
    channels = gh_ref.shape[1]
    state, adjoint = joined(forward), joined(backward)
    s2_ref[0:N, :], s2_ref[N:, :] = split(state)
    a2_ref[0:N, :], a2_ref[N:, :] = split(adjoint)
    last = own_ref[0:N, :] + own_ref[N : N + 1, :] * state
    end_ref[...] = jnp.broadcast_to(jnp.sum(last * adjoint, axis=0, keepdims=True), end_ref.shape)
    for_c = pull(gh_ref[...], gl_ref[...], s2_ref)
    for_b = pull(xh_ref[...], xl_ref[...], a2_ref)
    shared = (dbc_ref[...] + jnp.concatenate([for_b, for_c], axis=1)) * slope_bc_ref[...]
    scale = scale_ref[...]
    dx = push(hi_ref[:, :N], lo_ref[:, :N], a2_ref) * dot(scale, expander(heads, channels, 3))
    dx = dx_ref[...] + dx
    head_ref[:, :channels] = (dx * slope_ref[...])[0:8, :]
    head_ref[:, channels:] = shared[0:8, :]


def shared_kernel(gh_ref, gl_ref, xh_ref, xl_ref, dbc_ref, slope_ref, s2_ref, a2_ref, out_ref):
    for_c = pull(gh_ref[...], gl_ref[...], s2_ref)
    for_b = pull(xh_ref[...], xl_ref[...], a2_ref)
    out_ref[...] = (dbc_ref[...] + jnp.concatenate([for_b, for_c], axis=1)) * slope_ref[...]


def arrange_kernel(
    lens_ref, start_ref, side_ref, shared_ref, halo_ref, taps_ref, keep_ref, give_ref, ext, total, *, sharers
):
    tokens = shared_ref.shape[0]
    ext[0:tokens, :] = shared_ref[...]
    ext[tokens:, :] = halo_ref[:, -2 * N :]
    size = tokens // sharers
    high = 64
    odd = side_ref[0] % 2 == 1

    for first in range(0, tokens, high):

        def body(link, at=slice(first, first + high)):
            linked = link(0, high)
            for c in range(0, 2 * N, LANES):
                over = slice(c, c + LANES)
                total[at, over] = conv_tile(ext, taps_ref, at.start, high, over, linked, 1)

        two_ways(start_ref[0] + first, high, 1, lens_ref, body)
    for pair in range(sharers // 2):
        even, uneven = (total[(2 * pair + i) * size : (2 * pair + i + 1) * size, :] for i in range(2))
        at = slice(pair * size, (pair + 1) * size)
        keep_ref[at, :] = jnp.where(odd, uneven, even)
        give_ref[at, :] = jnp.where(odd, even, uneven)


def final_kernel(
    lens_ref, start_ref, gh_ref, gl_ref, xh_ref, xl_ref, hi_ref, lo_ref, scale_ref,
    dx_ref, slope_ref, rate_ref, s2_ref, a2_ref, taps_ref, tail_ref, end_ref,
    out_ref, log_ref, carry, spread, summer, ext, product, *, heads
):
    step = pl.program_id(0)
    rows, channels = gh_ref.shape

    @pl.when(step == 0)
    def _():
        spread[...] = expander(heads, channels, 3)
        summer[...] = head_summer(channels)
        ext[rows:, :] = tail_ref[:, :channels]
        carry[...] = jnp.zeros_like(carry)

    @pl.when(step > 0)
    def _():
        ext[rows:, :] = ext[0:8, :]

    scale = scale_ref[...]
    wide = min(2 * LANES, channels)

    def products(c):
        over = slice(c, c + wide)
        return (
            push(hi_ref[:, N:], lo_ref[:, N:], s2_ref, over),
            push(hi_ref[:, :N], lo_ref[:, :N], a2_ref, over),
            dot(scale, spread[:, over]),
        )

    ready = products(0)
    for c in range(0, channels, wide):
        y, entered, leave = ready
        ready = products(c + wide) if c + wide < channels else None
        for at, inside in tiles(rows, wide):
            over = slice(c + inside.start, c + inside.stop)
            dx = entered[at, inside]
            rate = whole_of((gh_ref[at, over], gl_ref[at, over])) * y[at, inside]
            rate = rate - whole_of((xh_ref[at, over], xl_ref[at, over])) * dx
            product[at, over], product[rows + at.start : rows + at.stop, over] = split(rate)
            grad = dx_ref[at, over] + dx * leave[at, inside]
            ext[at, over] = grad * slope_ref[at, over]
    rates = dot(product[...], summer[...])
    rates = rate_ref[...] + rates[:rows] + rates[rows:]
    end_row = (rows_iota((rows, LANES)) == rows - 1) & (step == 0)
    beyond = exact(thirds(end_ref[...]), summer[...])[0:1, :]
    rates = rates + jnp.where(end_row, beyond, 0.0)
    later = rows_iota((rows, rows)) >= cols_iota((rows, rows))
    ones = jnp.ones((rows, LANES), f32)
    marks = jnp.concatenate([jnp.where(later, 1.0, 0.0), ones], axis=1).astype(bf16)
    sums = exact(thirds(rates), marks, TN)
    log = sums[:, :rows] + widen(carry[...], rows)
    log_ref[...] = log[0:heads, :]
    carry[...] += sums[:, rows:]
    first = start_ref[0] + (pl.num_programs(0) - 1 - step) * rows

    def body(link):
        for r in range(0, rows, 64):
            at, linked = slice(r, r + 64), link(r, 64)
            for c in range(0, channels, LANES):
                over = slice(c, c + LANES)
                out_ref[at, over] = conv_tile(ext, taps_ref, r, 64, over, linked, 1)

    two_ways(first, rows, 1, lens_ref, body)


def shifted(value, axis, steps):
    count = lax.axis_size(axis)
    initial, last = (max(0, -steps), min(count, count - steps))
    return lax.ppermute(value, axis, [(source, source + steps) for source in range(initial, last)])


def merge_kernel(side_ref, kept_ref, came_ref, keep_ref, give_ref):
    odd = side_ref[0] == 1
    for pair in range(keep_ref.shape[0]):
        even, uneven = (kept_ref[2 * pair + i] + came_ref[2 * pair + i] for i in range(2))
        keep_ref[pair] = jnp.where(odd, uneven, even)
        give_ref[pair] = jnp.where(odd, even, uneven)


def pieces_kernel(place_ref, kept_ref, came_ref, *piece_refs):
    for i, piece_ref in enumerate(piece_refs):
        block = place_ref[0] ^ i
        piece_ref[...] = kept_ref[block] + came_ref[block]


def total_kernel(*refs):
    total = refs[0][...]
    for ref in refs[1:-1]:
        total = total + ref[...]
    refs[-1][...] = total


def head_scatter(keep, give, mine, params):
    count = lax.axis_size("head")
    swap = lambda value, bits: lax.ppermute(value, "head", [(i, i ^ bits) for i in range(count)])
    size, width = 2 * keep.shape[0] // count, keep.shape[1]
    blocks = lambda value: value.reshape(-1, size, width)
    smem = pl.BlockSpec(memory_space=pltpu.SMEM)
    vmem = pl.BlockSpec(memory_space=pltpu.VMEM)
    keep, give, bit = blocks(keep), blocks(give), 1
    while keep.shape[0] > 4:
        came = swap(give, bit)
        bit *= 2
        half = jax.ShapeDtypeStruct((keep.shape[0] // 2, size, width), f32)
        keep, give = pl.pallas_call(
            merge_kernel,
            out_shape=(half, half),
            in_specs=[smem, vmem, vmem],
            out_specs=(vmem, vmem),
            compiler_params=params,
        )((mine // bit) % 2, keep, came)
    came = swap(give, bit)
    bit *= 2
    left = keep.shape[0]
    block = jax.ShapeDtypeStruct((size, width), f32)
    pieces = pl.pallas_call(
        pieces_kernel,
        out_shape=(block,) * left,
        in_specs=[smem, vmem, vmem],
        out_specs=(vmem,) * left,
        compiler_params=params,
    )(mine // bit, keep, came)
    return pl.pallas_call(
        total_kernel,
        out_shape=block,
        in_specs=[vmem] * left,
        out_specs=vmem,
        compiler_params=params,
    )(pieces[0], *[swap(pieces[i], i * bit) for i in range(1, left)])


def local(pre_x, pre_bc, conv_x, conv_bc, log_decay, lengths, grad_out):
    tokens, channels = pre_x.shape
    heads = log_decay.shape[0]
    count = lax.axis_size("seq")
    sharers = lax.axis_size("head")
    chunks = tokens // CHUNK
    big = 256
    steps = tokens // big
    width = 2 * LANES
    start = (lax.axis_index("seq") * tokens).astype(jnp.int32).reshape(1)
    mine = lax.axis_index("head").astype(jnp.int32).reshape(1)
    shape = jax.ShapeDtypeStruct
    smem = pl.BlockSpec(memory_space=pltpu.SMEM)
    vmem = pl.BlockSpec(memory_space=pltpu.VMEM)
    params = pltpu.CompilerParams(vmem_limit_bytes=VMEM_LIMIT)
    by_rows = lambda rows, cols: pl.BlockSpec((rows, cols), lambda i: (i, 0))
    whole = lambda rows, cols: pl.BlockSpec((rows, cols), lambda *i: (0, 0))
    wide = tokens * channels
    cost = lambda work: pl.CostEstimate(flops=wide * work, bytes_accessed=wide * 16, transcendentals=0)
    grad_out = pltpu.with_memory_space_constraint(grad_out, pltpu.HBM)
    pre_x = pltpu.with_memory_space_constraint(pre_x, pltpu.HBM)
    pre_bc = pltpu.with_memory_space_constraint(pre_bc, pltpu.HBM)
    rows_f32, rows_bf16 = shape((tokens, channels), f32), shape((tokens, channels), bf16)
    bc_f32, bc_bf16 = shape((tokens, 2 * N), f32), shape((tokens, 2 * N), bf16)

    last_rows = lambda cols: pl.BlockSpec((16, cols), lambda i: (tokens // 16 - 1, 0))
    edge = pl.pallas_call(
        edge_kernel,
        grid=(1,),
        out_shape=shape((16, channels + 2 * N), bf16),
        in_specs=[last_rows(channels), last_rows(2 * N)],
        out_specs=whole(16, channels + 2 * N),
        compiler_params=params,
    )(pre_x, pre_bc)
    halo = shifted(edge, "seq", 1)

    scale, kappa, through = pl.pallas_call(
        scales_kernel,
        out_shape=(
            shape((tokens, width), bf16), shape((2 * chunks, channels), f32), shape((8, channels), f32),
        ),
        in_specs=[smem, smem, vmem],
        out_specs=(vmem,) * 3,
        scratch_shapes=[pltpu.VMEM((LANES, tokens), f32)],
        compiler_params=params,
        cost_estimate=cost(1000),
    )(lengths, start, log_decay)

    spread = pltpu.VMEM((width, channels), bf16)
    hi, lo, slope_bc, r_high, r_low, g_high, g_low, send_adjoint = pl.pallas_call(
        functools.partial(adjoint_kernel, heads=heads),
        grid=(steps,),
        out_shape=(bc_bf16, bc_bf16, bc_f32) + (rows_bf16,) * 4 + (shape((N + 8, channels), f32),),
        in_specs=[
            smem, smem, by_rows(big, channels), by_rows(big, width), by_rows(big, 2 * N),
            whole(16, channels + 2 * N), whole(K, 2 * N), whole(8, channels),
        ],
        out_specs=(by_rows(big, 2 * N),) * 3 + (by_rows(big, channels),) * 4 + (whole(N + 8, channels),),
        scratch_shapes=[spread, spread, pltpu.VMEM((big + 8, 2 * N), f32)],
        compiler_params=params,
        cost_estimate=cost(1000),
    )(lengths, start, grad_out, scale, pre_bc, halo, conv_bc, through)

    packed = (N * channels // LANES + 8, LANES)
    slope_x, q_high, q_low, x_high, x_low, own_state, *messages = pl.pallas_call(
        functools.partial(state_kernel, heads=heads, count=count),
        grid=(steps,),
        out_shape=(rows_f32,) + (rows_bf16,) * 4
        + (shape((N + 8, channels), f32),)
        + (shape(packed, f32),) * (count - 1),
        in_specs=[
            smem, smem, by_rows(big, channels), whole(16, channels + 2 * N), whole(K, channels),
            by_rows(big, width), by_rows(big, 2 * N), by_rows(big, 2 * N), whole(8, channels),
            whole(N + 8, channels),
        ],
        out_specs=(by_rows(big, channels),) * 5
        + (whole(N + 8, channels),)
        + (whole(*packed),) * (count - 1),
        scratch_shapes=[spread, spread, pltpu.VMEM((big + 8, channels), f32)],
        compiler_params=params,
        cost_estimate=cost(1000),
    )(lengths, start, pre_x, halo, conv_x, scale, hi, lo, through, send_adjoint)
    received = [
        lax.ppermute(message, "seq", [(i, (i + lag) % count) for i in range(count)])
        for lag, message in enumerate(messages, 1)
    ]

    from_end = lambda rows, cols: pl.BlockSpec((rows, cols), lambda i: (chunks - 1 - i, 0))
    both_ways = [
        place(CHUNK, size)
        for place in (by_rows, from_end)
        for size in (channels, channels, channels, channels, 2 * N, 2 * N)
    ]
    dx, dbc, rate = pl.pallas_call(
        functools.partial(local_kernel, heads=heads),
        grid=(chunks,),
        out_shape=(rows_f32, bc_f32, shape((tokens, LANES), f32)),
        in_specs=[smem, smem, whole(2 * chunks, channels)] + both_ways + [from_end(CHUNK, width)],
        out_specs=(from_end(CHUNK, channels), whole(tokens, 2 * N), whole(tokens, LANES)),
        scratch_shapes=[
            pltpu.VMEM((N, channels), f32), pltpu.VMEM((N, channels), f32),
            pltpu.VMEM((channels, LANES), bf16),
        ]
        + [pltpu.VMEM((4 * CHUNK, channels), bf16), spread],
        compiler_params=params,
        cost_estimate=cost(8000),
    )(lengths, start, kappa, *([q_high, q_low, r_high, r_low, hi, lo] * 2), scale)

    s2, a2, end, head = pl.pallas_call(
        functools.partial(entering_kernel, count=count, heads=heads, tokens=tokens),
        grid=(1,),
        out_shape=(
            shape((2 * N, channels), bf16), shape((2 * N, channels), bf16), shape((8, channels), f32),
            shape((8, channels + 2 * N), f32),
        ),
        in_specs=[smem]
        + [whole(*packed)] * (count - 1)
        + [whole(N + 8, channels)]
        + [whole(16, channels)] * 4
        + [whole(16, 2 * N)] * 2
        + [whole(16, width), whole(16, channels), whole(16, 2 * N), whole(16, channels), whole(16, 2 * N)],
        out_specs=(
            whole(2 * N, channels), whole(2 * N, channels), whole(8, channels),
            whole(8, channels + 2 * N),
        ),
        compiler_params=params,
        cost_estimate=cost(200),
    )(
        start, *received, own_state, g_high, g_low, x_high, x_low, hi, lo, scale, dx, dbc,
        slope_x, slope_bc,
    )
    after = shifted(head, "seq", -1)

    high = 512
    shared = pl.pallas_call(
        shared_kernel,
        grid=(tokens // high,),
        out_shape=bc_f32,
        in_specs=[by_rows(high, channels)] * 4
        + [by_rows(high, 2 * N)] * 2
        + [whole(2 * N, channels)] * 2,
        out_specs=by_rows(high, 2 * N),
        compiler_params=params,
        cost_estimate=cost(1500),
    )(g_high, g_low, x_high, x_low, dbc, slope_bc, s2, a2)

    half = shape((tokens // 2, 2 * N), f32)
    keep, give = pl.pallas_call(
        functools.partial(arrange_kernel, sharers=sharers),
        out_shape=(half, half),
        in_specs=[smem, smem, smem, vmem, vmem, vmem],
        out_specs=(vmem, vmem),
        scratch_shapes=[pltpu.VMEM((tokens + 8, 2 * N), f32), pltpu.VMEM((tokens, 2 * N), f32)],
        compiler_params=params,
    )(lengths, start, mine, shared, after, conv_bc)
    grad_pre_bc = head_scatter(keep, give, mine, params)

    back = lambda rows, cols: pl.BlockSpec((rows, cols), lambda i: (steps - 1 - i, 0))
    grad_pre_x, grad_log = pl.pallas_call(
        functools.partial(final_kernel, heads=heads),
        grid=(steps,),
        out_shape=(rows_f32, shape((heads, tokens), f32)),
        in_specs=[smem, smem]
        + [back(big, channels)] * 4
        + [back(big, 2 * N)] * 2
        + [back(big, width)]
        + [back(big, channels)] * 2
        + [
            back(big, LANES), whole(2 * N, channels), whole(2 * N, channels),
            whole(K, channels), whole(8, channels + 2 * N), whole(8, channels),
        ],
        out_specs=(
            back(big, channels), pl.BlockSpec((heads, big), lambda i: (0, steps - 1 - i)),
        ),
        scratch_shapes=[
            pltpu.VMEM((LANES, LANES), f32), spread, pltpu.VMEM((channels, LANES), bf16),
            pltpu.VMEM((big + 8, channels), f32), pltpu.VMEM((2 * big, channels), bf16),
        ],
        compiler_params=params,
        cost_estimate=cost(3000),
    )(
        lengths, start, g_high, g_low, x_high, x_low, hi, lo, scale, dx, slope_x, rate, s2, a2,
        conv_x, after, end,
    )
    return (grad_pre_x, grad_pre_bc, grad_log)


def solution(mesh):
    placed = (
        P("seq", "head"),
        P("seq", None),
        P(None, "head"),
        P(),
        P("head", "seq"),
        P(),
        P("seq", "head"),
    )
    return jax.shard_map(
        local,
        mesh=mesh,
        in_specs=placed,
        out_specs=(P("seq", "head"), P(("seq", "head"), None), P("head", "seq")),
        check_vma=False,
    )
```

```python
import functools
import jax
import jax.numpy as jnp
from jax import lax
from jax.experimental import pallas as pl
from jax.experimental.pallas import tpu as pltpu
from jax.sharding import PartitionSpec as P

P_SIZE = 64
N = 128
K = 4
CHUNK = 64
LANES = 128
f32 = jnp.float32
bf16 = jnp.bfloat16
NN = (((1,), (0,)), ((), ()))
NT = (((1,), (1,)), ((), ()))
TN = (((0,), (0,)), ((), ()))
VMEM_LIMIT = 24 * 1024 * 1024


def split(value):
    high = value.astype(bf16)
    return high, (value - high.astype(f32)).astype(bf16)


def dot(left, right, dims=NN):
    return lax.dot_general(left, right, dims, preferred_element_type=f32)


def thirds(value):
    high, low = split(value)
    return high, low, (value - high.astype(f32) - low.astype(f32)).astype(bf16)


def exact(left, right, dims=NN):
    if isinstance(left, tuple):
        return dot(left[0], right, dims) + dot(left[1], right, dims) + dot(left[2], right, dims)
    return dot(left, right[0], dims) + dot(left, right[1], dims) + dot(left, right[2], dims)


def stack(*parts):
    return jnp.concatenate(parts, axis=0)


def dot3(left, right, dims=NN):
    rows = left[0].shape[0]
    most = dot(stack(*left), right[0], dims)
    return most[:rows] + most[rows:] + dot(left[0], right[1], dims)


def dot3_tn(left, right):
    return dot(stack(left[0], left[1], left[0]), stack(right[0], right[0], right[1]), TN)


def whole_of(parts):
    return parts[0].astype(f32) + parts[1].astype(f32)


def rows_iota(shape):
    return lax.broadcasted_iota(jnp.int32, shape, 0)


def cols_iota(shape):
    return lax.broadcasted_iota(jnp.int32, shape, 1)


def note_of(position, lens_ref):
    first = lens_ref[0]
    second = first + lens_ref[1]
    third = second + lens_ref[2]
    one = lambda flag: jnp.where(flag, 1, 0)
    return one(position >= 0) + one(position >= first) + one(position >= second) + one(
        position >= third
    )


def widen(block, width):
    return block if width == LANES else jnp.concatenate([block] * (width // LANES), axis=1)


def links(first, rows, sign, lens_ref):
    position = first + rows_iota((rows, LANES))
    here = note_of(position, lens_ref)
    return [
        jnp.where(note_of(position + sign * lag, lens_ref) == here, 1.0, 0.0) for lag in range(1, K)
    ]


def conv_tile(ext_ref, taps_ref, first, rows, over, linked, sign):
    total = ext_ref[first : first + rows, over] * taps_ref[K - 1 : K, over]
    for lag in range(1, K):
        moved = first + sign * lag
        tap = taps_ref[K - 1 - lag : K - lag, over]
        tap = tap if linked is None else tap * linked[lag - 1]
        total = total + ext_ref[moved : moved + rows, over] * tap
    return total


def near_start(position, rows, lens_ref):
    begins = [0, lens_ref[0], lens_ref[0] + lens_ref[1], lens_ref[0] + lens_ref[1] + lens_ref[2]]
    near = [(begin > position - K) & (begin < position + rows + K) for begin in begins]
    return near[0] | near[1] | near[2] | near[3]


def two_ways(position, rows, sign, lens_ref, body):
    cut = near_start(position, rows, lens_ref)

    @pl.when(cut)
    def _():
        body(lambda first, high: links(position + first, high, sign, lens_ref))

    @pl.when(jnp.logical_not(cut))
    def _():
        body(lambda first, high: None)


def silu_and_slope(u):
    sigma = 1.0 / (1.0 + jnp.exp(-u))
    value = u * sigma
    return value, sigma + value * (1.0 - sigma)


def expander(heads, channels, group):
    row = rows_iota((2 * LANES, channels)) % LANES
    own = cols_iota((2 * LANES, channels)) // P_SIZE
    return jnp.where(row == group * heads + own, 1.0, 0.0).astype(bf16)


def head_summer(channels):
    same = rows_iota((channels, LANES)) // P_SIZE == cols_iota((channels, LANES))
    return jnp.where(same, 1.0, 0.0).astype(bf16)


def edge_kernel(x_ref, bc_ref, edge_ref):
    channels = x_ref.shape[1]
    edge_ref[:, :channels] = x_ref[...]
    edge_ref[:, channels:] = bc_ref[...]


def scales_kernel(lens_ref, start_ref, log_ref, scale_ref, kappa_ref, through_ref, padded):
    heads, tokens = log_ref.shape
    channels = kappa_ref.shape[1]
    chunks = tokens // CHUNK
    start = start_ref[0]
    padded[...] = jnp.zeros_like(padded)
    for group in range(4):
        padded[group * heads : (group + 1) * heads, :] = log_ref[...]
    size = 2 * LANES
    square = (size, size)
    row, col = rows_iota(square), cols_iota(square)
    same = row // CHUNK == col // CHUNK
    one = lambda flag: jnp.where(flag, 1.0, 0.0)
    inner = one(same & (col <= row)) - one(same & (col % CHUNK < CHUNK // 2))
    sums = stack(inner, one(col <= row), one(col > row), jnp.ones((16, size), f32)).astype(bf16)
    blocks = tokens // size
    parts = thirds(padded[...])
    tables = [
        exact(sums, tuple(part[:, b * size : (b + 1) * size] for part in parts), NT)
        for b in range(blocks)
    ]
    totals = [table[3 * size : 3 * size + 1, :] for table in tables]
    offsets = [jnp.zeros((1, LANES), f32)]
    for total in totals:
        offsets.append(offsets[-1] + total)
    after = jnp.zeros((1, LANES), f32)
    note_before = note_of(start - 1, lens_ref)
    note_last = note_of(start + tokens - 1, lens_ref)
    shape = (size, LANES)
    group = cols_iota(shape) // heads
    for b in reversed(range(blocks)):
        near, ahead, behind = (tables[b][i * size : (i + 1) * size, :] for i in range(3))
        note = note_of(start + b * size + rows_iota(shape), lens_ref)
        power = jnp.where(group == 0, near, -near)
        power = jnp.where(group == 2, ahead + offsets[b], power)
        power = jnp.where(group >= 3, behind + after, power)
        kept = (group < 2) | ((group == 2) & (note == note_before)) | ((group == 3) & (note == note_last))
        after = after + totals[b]
        rows = slice(b * size, (b + 1) * size)
        scale_ref[rows, :LANES], scale_ref[rows, LANES:] = split(jnp.where(kept, jnp.exp(power), 0.0))
    spread = one(
        rows_iota((LANES, channels)) == cols_iota((LANES, channels)) // P_SIZE
    ).astype(bf16)
    half = CHUNK // 2
    chunk = rows_iota((chunks, tokens)) * CHUNK + half
    col = cols_iota((chunks, tokens))
    for place in range(2):
        begin = chunk + place * half
        steps = exact(one((col >= begin) & (col < begin + half)).astype(bf16), parts, NT)
        kappa_ref[place * chunks : (place + 1) * chunks, :] = exact(thirds(jnp.exp(steps)), spread)
    through = jnp.broadcast_to(jnp.exp(offsets[-1]), (8, LANES)) * one(note_before == note_last)
    through_ref[...] = exact(thirds(through), spread)


def tiles(rows, channels, high=64, wide=LANES):
    return [
        (slice(r, r + high), slice(c, c + wide))
        for r in range(0, rows, high)
        for c in range(0, channels, wide)
    ]


def adjoint_kernel(
    lens_ref, start_ref, grad_ref, scale_ref, pre_ref, halo_ref, taps_ref, through_ref,
    hi_ref, lo_ref, slope_ref, rh_ref, rl_ref, gh_ref, gl_ref, send_ref,
    spread, spread_r, ext, *, heads
):
    rows, channels = grad_ref.shape
    step = pl.program_id(0)

    @pl.when(step == 0)
    def _():
        spread[...] = expander(heads, channels, 2)
        spread_r[...] = expander(heads, channels, 0)
        send_ref[...] = jnp.zeros_like(send_ref)
        send_ref[N : N + 8, :] = through_ref[...]
        ext[0:8, :] = halo_ref[8:16, channels:].astype(f32)

    @pl.when(step > 0)
    def _():
        ext[0:8, :] = ext[rows : rows + 8, :]

    ext[8:, :] = pre_ref[...].astype(f32)
    scale = scale_ref[...]
    wide = min(2 * LANES, channels)

    def spreads(c):
        over = slice(c, c + wide)
        return dot(scale, spread[:, over]), dot(scale, spread_r[:, over])

    def conv(link):
        for first in range(0, rows, 64):
            at, linked = slice(first, first + 64), link(first, 64)
            for c in range(0, 2 * N, LANES):
                over = slice(c, c + LANES)
                u = conv_tile(ext, taps_ref, 8 + first, 64, over, linked, -1)
                value, slope_ref[at, over] = silu_and_slope(u)
                hi_ref[at, over], lo_ref[at, over] = split(value)

    two_ways(start_ref[0] + step * rows, rows, -1, lens_ref, conv)
    ready = spreads(0)
    for c in range(0, channels, wide):
        entry, near = ready
        ready = spreads(c + wide) if c + wide < channels else None
        for at, inside in tiles(rows, wide):
            over = slice(c + inside.start, c + inside.stop)
            grad = grad_ref[at, over].astype(f32)
            gh_ref[at, over], gl_ref[at, over] = split(grad * entry[at, inside])
            rh_ref[at, over], rl_ref[at, over] = split(grad * near[at, inside])
    send_ref[0:N, :] += dot3_tn((hi_ref[:, N:], lo_ref[:, N:]), (gh_ref[...], gl_ref[...]))


def state_kernel(
    lens_ref, start_ref, pre_ref, halo_ref, taps_ref, scale_ref, hi_ref, lo_ref, through_ref, other_ref,
    slope_ref, qh_ref, ql_ref, xh_ref, xl_ref, own_ref, *refs, heads, count
):
    messages = refs[: count - 1]
    spread, spread_q, ext = refs[count - 1 :]
    rows, channels = pre_ref.shape
    step, steps = pl.program_id(0), pl.num_programs(0)

    @pl.when(step == 0)
    def _():
        spread[...] = expander(heads, channels, 3)
        spread_q[...] = expander(heads, channels, 1)
        own_ref[...] = jnp.zeros_like(own_ref)
        own_ref[N : N + 8, :] = through_ref[...]
        ext[0:8, :] = halo_ref[8:16, :channels].astype(f32)

    @pl.when(step > 0)
    def _():
        ext[0:8, :] = ext[rows : rows + 8, :]

    ext[8:, :] = pre_ref[...].astype(f32)
    scale = scale_ref[...]
    wide = min(2 * LANES, channels)

    def spreads(c):
        over = slice(c, c + wide)
        return dot(scale, spread[:, over]), dot(scale, spread_q[:, over])

    def body(link):
        ready = spreads(0)
        linked = [link(first, 64) for first in range(0, rows, 64)]
        for c in range(0, channels, wide):
            leave, near = ready
            ready = spreads(c + wide) if c + wide < channels else None
            for at, inside in tiles(rows, wide):
                over = slice(c + inside.start, c + inside.stop)
                u = conv_tile(ext, taps_ref, 8 + at.start, 64, over, linked[at.start // 64], -1)
                value, slope_ref[at, over] = silu_and_slope(u)
                xh_ref[at, over], xl_ref[at, over] = split(value * leave[at, inside])
                qh_ref[at, over], ql_ref[at, over] = split(value * near[at, inside])

    two_ways(start_ref[0] + step * rows, rows, -1, lens_ref, body)
    own_ref[0:N, :] += dot3_tn((hi_ref[:, :N], lo_ref[:, :N]), (xh_ref[...], xl_ref[...]))

    @pl.when(step == steps - 1)
    def _():
        for lag in range(1, count):
            ahead = start_ref[0] + lag * rows * steps < count * rows * steps
            for part in range(channels // LANES):
                over, at = slice(part * LANES, (part + 1) * LANES), N * part
                held = jnp.where(ahead, own_ref[:, over], other_ref[:, over])
                messages[lag - 1][at : at + N, :] = held[:N]
                messages[lag - 1][N * channels // LANES + part : N * channels // LANES + part + 1, :] = held[N : N + 1]


def local_kernel(
    lens_ref, start_ref, kappa_ref,
    fx_h, fx_l, fg_h, fg_l, f_hi, f_lo, bx_h, bx_l, bg_h, bg_l, b_hi, b_lo,
    scale_ref, dx_ref, dbc_ref, rate_ref, state, adjoint, summer, product, spread, *, heads
):
    step = pl.program_id(0)
    chunks = pl.num_programs(0)
    channels = dx_ref.shape[1]
    here, there = step, chunks - 1 - step

    @pl.when(step == 0)
    def _():
        summer[...] = head_summer(channels)
        spread[...] = expander(heads, channels, 1)
        state[...] = jnp.zeros_like(state)
        adjoint[...] = jnp.zeros_like(adjoint)
        dbc_ref[...] = jnp.zeros_like(dbc_ref)
        rate_ref[...] = jnp.zeros_like(rate_ref)

    square = (CHUNK, CHUNK)
    row, col = rows_iota(square), cols_iota(square)
    pick = lambda flag, parts: tuple(
        jnp.where(flag, part.astype(f32), 0.0).astype(bf16) for part in parts
    )
    beside = lambda left, right: tuple(jnp.concatenate(p, axis=1) for p in zip(left, right))
    below = lambda left, right: tuple(stack(*p) for p in zip(left, right))
    turned = lambda parts: stack(parts[0], parts[1], parts[0]).astype(f32).T.astype(bf16)

    def setting(chunk, hi_ref, lo_ref):
        first = start_ref[0] + chunk * CHUNK
        note_before = note_of(first - 1, lens_ref)
        note_last = note_of(first + CHUNK - 1, lens_ref)
        keep = jnp.where(note_before == note_last, 1.0, 0.0)
        note = note_of(first + rows_iota((CHUNK, LANES)), lens_ref)
        linked = note_of(first + row, lens_ref) == note_of(first + col, lens_ref)
        b_parts = (hi_ref[:, :N], lo_ref[:, :N])
        c_parts = (hi_ref[:, N:], lo_ref[:, N:])
        return keep, note == note_before, note == note_last, linked, b_parts, c_parts

    def walk(ref, left, turn, x_refs, keep, place, over):
        held = ref[:, over]
        held_parts = split(held)
        x_parts = (x_refs[0][:, over], x_refs[1][:, over])
        right = below(held_parts, x_parts)
        fresh = dot(turn, stack(x_parts[0], x_parts[0], x_parts[1]))
        moved = (held * keep + fresh) * kappa_ref[pl.ds(place, 1), over]
        ref[:, over] = moved * kappa_ref[pl.ds(chunks + place, 1), over]
        return dot3(left, right), right, held_parts

    rows_f = pl.ds(pl.multiple_of(here * CHUNK, CHUNK), CHUNK)
    rows_b = pl.ds(pl.multiple_of(there * CHUNK, CHUNK), CHUNK)
    f_keep, f_enters, f_leaves, f_linked, fb, fc = setting(here, f_hi, f_lo)
    b_keep, b_enters, b_leaves, b_linked, bb, bc = setting(there, b_hi, b_lo)
    f_scores = jnp.where(f_linked & (col < row), dot3(fc, fb, NT), 0.0)
    b_scores = jnp.where(b_linked & (row < col), dot3(bb, bc, NT), 0.0)
    f_left = beside(pick(f_enters, fc), split(f_scores))
    b_left = beside(pick(b_leaves, bb), split(b_scores))
    f_turn, b_turn = turned(pick(f_leaves, fb)), turned(pick(b_enters, bc))
    own = jnp.sum(whole_of(bb) * whole_of(bc), axis=1, keepdims=True)
    wide = min(2 * LANES, channels)
    inner = outer = 0.0
    for first in range(0, channels, wide):
        over = slice(first, first + wide)
        y, right, _ = walk(state, f_left, f_turn, (fx_h, fx_l), f_keep, here, over)
        inner = inner + dot3((fg_h[:, over], fg_l[:, over]), right, NT)
        product[0:CHUNK, over], product[CHUNK : 2 * CHUNK, over] = split(
            whole_of((fg_h[:, over], fg_l[:, over])) * y
        )
        before = jnp.maximum(there - 1, 0)
        dx, _, a_parts = walk(adjoint, b_left, b_turn, (bg_h, bg_l), b_keep, before, over)
        outer = outer + dot3((bx_h[:, over], bx_l[:, over]), a_parts, NT)
        near = dot(scale_ref[...], spread[:, over])
        dx_ref[:, over] = (dx + own * whole_of((bg_h[:, over], bg_l[:, over]))) * near
        product[2 * CHUNK : 3 * CHUNK, over], product[3 * CHUNK :, over] = split(
            whole_of((bx_h[:, over], bx_l[:, over])) * dx
        )
    d_scores = split(jnp.where(f_linked & (col <= row), inner[:, N:], 0.0))
    for_c = jnp.where(f_enters, inner[:, :N], 0.0) + dot3(d_scores, fb)
    for_b = dot3_tn(d_scores, fc)
    dbc_ref[rows_f, :] += jnp.concatenate([for_b, for_c], axis=1)
    dbc_ref[rows_b, :N] += jnp.where(b_leaves, outer, 0.0)
    rates = dot(product[...], summer[...])
    rate_ref[rows_f, :] += rates[:CHUNK] + rates[CHUNK : 2 * CHUNK]
    rate_ref[rows_b, :] -= rates[2 * CHUNK : 3 * CHUNK] + rates[3 * CHUNK :]


def joined(messages):
    parts = (messages[0].shape[0] - 8) // N
    tiles_of = []
    for part in range(parts):
        total = jnp.zeros((N, LANES), f32)
        for message in reversed(messages):
            through = message[N * parts + part : N * parts + part + 1, :]
            total = message[part * N : (part + 1) * N, :] + through * total
        tiles_of.append(total)
    return jnp.concatenate(tiles_of, axis=1)


def pull(high, low, both):
    most = dot(high, both[...], NT)
    return most[:, :N] + most[:, N:] + dot(low, both[0:N, :], NT)


def push(high, low, both, over=slice(None)):
    first = both[0:N, over]
    return dot(jnp.concatenate([high, low, high], axis=1), stack(first, first, both[N:, over]))


def entering_kernel(start_ref, *refs, count, heads, tokens):
    messages = refs[: count - 1]
    place = start_ref[0]
    forward = [
        jnp.where(place >= lag * tokens, messages[lag - 1][...], 0.0) for lag in range(1, count)
    ]
    backward = [
        jnp.where(place + lag * tokens < count * tokens, messages[count - 1 - lag][...], 0.0)
        for lag in range(1, count)
    ]
    (
        own_ref, gh_ref, gl_ref, xh_ref, xl_ref, hi_ref, lo_ref, scale_ref, dx_ref, dbc_ref,
        slope_ref, slope_bc_ref, s2_ref, a2_ref, end_ref, head_ref,
    ) = refs[count - 1 :]
    channels = gh_ref.shape[1]
    state, adjoint = joined(forward), joined(backward)
    s2_ref[0:N, :], s2_ref[N:, :] = split(state)
    a2_ref[0:N, :], a2_ref[N:, :] = split(adjoint)
    last = own_ref[0:N, :] + own_ref[N : N + 1, :] * state
    end_ref[...] = jnp.broadcast_to(jnp.sum(last * adjoint, axis=0, keepdims=True), end_ref.shape)
    for_c = pull(gh_ref[...], gl_ref[...], s2_ref)
    for_b = pull(xh_ref[...], xl_ref[...], a2_ref)
    shared = (dbc_ref[...] + jnp.concatenate([for_b, for_c], axis=1)) * slope_bc_ref[...]
    scale = scale_ref[...]
    dx = push(hi_ref[:, :N], lo_ref[:, :N], a2_ref) * dot(scale, expander(heads, channels, 3))
    dx = dx_ref[...] + dx
    head_ref[:, :channels] = (dx * slope_ref[...])[0:8, :]
    head_ref[:, channels:] = shared[0:8, :]


def shared_kernel(gh_ref, gl_ref, xh_ref, xl_ref, dbc_ref, slope_ref, s2_ref, a2_ref, out_ref):
    for_c = pull(gh_ref[...], gl_ref[...], s2_ref)
    for_b = pull(xh_ref[...], xl_ref[...], a2_ref)
    out_ref[...] = (dbc_ref[...] + jnp.concatenate([for_b, for_c], axis=1)) * slope_ref[...]


def arrange_kernel(
    lens_ref, start_ref, side_ref, shared_ref, halo_ref, taps_ref, keep_ref, give_ref, ext, total, *, sharers
):
    tokens = shared_ref.shape[0]
    ext[0:tokens, :] = shared_ref[...]
    ext[tokens:, :] = halo_ref[:, -2 * N :]
    size = tokens // sharers
    high = 64
    odd = side_ref[0] % 2 == 1

    for first in range(0, tokens, high):

        def body(link, at=slice(first, first + high)):
            linked = link(0, high)
            for c in range(0, 2 * N, LANES):
                over = slice(c, c + LANES)
                total[at, over] = conv_tile(ext, taps_ref, at.start, high, over, linked, 1)

        two_ways(start_ref[0] + first, high, 1, lens_ref, body)
    for pair in range(sharers // 2):
        even, uneven = (total[(2 * pair + i) * size : (2 * pair + i + 1) * size, :] for i in range(2))
        at = slice(pair * size, (pair + 1) * size)
        keep_ref[at, :] = jnp.where(odd, uneven, even)
        give_ref[at, :] = jnp.where(odd, even, uneven)


def final_kernel(
    lens_ref, start_ref, gh_ref, gl_ref, xh_ref, xl_ref, hi_ref, lo_ref, scale_ref,
    dx_ref, slope_ref, rate_ref, s2_ref, a2_ref, taps_ref, tail_ref, end_ref,
    out_ref, log_ref, carry, spread, summer, ext, product, *, heads
):
    step = pl.program_id(0)
    rows, channels = gh_ref.shape

    @pl.when(step == 0)
    def _():
        spread[...] = expander(heads, channels, 3)
        summer[...] = head_summer(channels)
        ext[rows:, :] = tail_ref[:, :channels]
        carry[...] = jnp.zeros_like(carry)

    @pl.when(step > 0)
    def _():
        ext[rows:, :] = ext[0:8, :]

    scale = scale_ref[...]
    wide = min(2 * LANES, channels)

    def products(c):
        over = slice(c, c + wide)
        return (
            push(hi_ref[:, N:], lo_ref[:, N:], s2_ref, over),
            push(hi_ref[:, :N], lo_ref[:, :N], a2_ref, over),
            dot(scale, spread[:, over]),
        )

    ready = products(0)
    for c in range(0, channels, wide):
        y, entered, leave = ready
        ready = products(c + wide) if c + wide < channels else None
        for at, inside in tiles(rows, wide):
            over = slice(c + inside.start, c + inside.stop)
            dx = entered[at, inside]
            rate = whole_of((gh_ref[at, over], gl_ref[at, over])) * y[at, inside]
            rate = rate - whole_of((xh_ref[at, over], xl_ref[at, over])) * dx
            product[at, over], product[rows + at.start : rows + at.stop, over] = split(rate)
            grad = dx_ref[at, over] + dx * leave[at, inside]
            ext[at, over] = grad * slope_ref[at, over]
    rates = dot(product[...], summer[...])
    rates = rate_ref[...] + rates[:rows] + rates[rows:]
    end_row = (rows_iota((rows, LANES)) == rows - 1) & (step == 0)
    beyond = exact(thirds(end_ref[...]), summer[...])[0:1, :]
    rates = rates + jnp.where(end_row, beyond, 0.0)
    later = rows_iota((rows, rows)) >= cols_iota((rows, rows))
    ones = jnp.ones((rows, LANES), f32)
    marks = jnp.concatenate([jnp.where(later, 1.0, 0.0), ones], axis=1).astype(bf16)
    sums = exact(thirds(rates), marks, TN)
    log = sums[:, :rows] + widen(carry[...], rows)
    log_ref[...] = log[0:heads, :]
    carry[...] += sums[:, rows:]
    first = start_ref[0] + (pl.num_programs(0) - 1 - step) * rows
    for r in range(0, rows, 64):

        def body(link, at=slice(r, r + 64)):
            linked = link(0, 64)
            for c in range(0, channels, LANES):
                over = slice(c, c + LANES)
                out_ref[at, over] = conv_tile(ext, taps_ref, at.start, 64, over, linked, 1)

        two_ways(first + r, 64, 1, lens_ref, body)


def shifted(value, axis, steps):
    count = lax.axis_size(axis)
    initial, last = (max(0, -steps), min(count, count - steps))
    return lax.ppermute(value, axis, [(source, source + steps) for source in range(initial, last)])


def merge_kernel(side_ref, kept_ref, came_ref, keep_ref, give_ref):
    odd = side_ref[0] == 1
    for pair in range(keep_ref.shape[0]):
        even, uneven = (kept_ref[2 * pair + i] + came_ref[2 * pair + i] for i in range(2))
        keep_ref[pair] = jnp.where(odd, uneven, even)
        give_ref[pair] = jnp.where(odd, even, uneven)


def pieces_kernel(place_ref, kept_ref, came_ref, *piece_refs):
    for i, piece_ref in enumerate(piece_refs):
        block = place_ref[0] ^ i
        piece_ref[...] = kept_ref[block] + came_ref[block]


def total_kernel(*refs):
    total = refs[0][...]
    for ref in refs[1:-1]:
        total = total + ref[...]
    refs[-1][...] = total


def head_scatter(keep, give, mine, params):
    count = lax.axis_size("head")
    swap = lambda value, bits: lax.ppermute(value, "head", [(i, i ^ bits) for i in range(count)])
    size, width = 2 * keep.shape[0] // count, keep.shape[1]
    blocks = lambda value: value.reshape(-1, size, width)
    smem = pl.BlockSpec(memory_space=pltpu.SMEM)
    vmem = pl.BlockSpec(memory_space=pltpu.VMEM)
    keep, give, bit = blocks(keep), blocks(give), 1
    while keep.shape[0] > 4:
        came = swap(give, bit)
        bit *= 2
        half = jax.ShapeDtypeStruct((keep.shape[0] // 2, size, width), f32)
        keep, give = pl.pallas_call(
            merge_kernel,
            out_shape=(half, half),
            in_specs=[smem, vmem, vmem],
            out_specs=(vmem, vmem),
            compiler_params=params,
        )((mine // bit) % 2, keep, came)
    came = swap(give, bit)
    bit *= 2
    left = keep.shape[0]
    block = jax.ShapeDtypeStruct((size, width), f32)
    pieces = pl.pallas_call(
        pieces_kernel,
        out_shape=(block,) * left,
        in_specs=[smem, vmem, vmem],
        out_specs=(vmem,) * left,
        compiler_params=params,
    )(mine // bit, keep, came)
    return pl.pallas_call(
        total_kernel,
        out_shape=block,
        in_specs=[vmem] * left,
        out_specs=vmem,
        compiler_params=params,
    )(pieces[0], *[swap(pieces[i], i * bit) for i in range(1, left)])


def local(pre_x, pre_bc, conv_x, conv_bc, log_decay, lengths, grad_out):
    tokens, channels = pre_x.shape
    heads = log_decay.shape[0]
    count = lax.axis_size("seq")
    sharers = lax.axis_size("head")
    chunks = tokens // CHUNK
    big = 256
    steps = tokens // big
    width = 2 * LANES
    start = (lax.axis_index("seq") * tokens).astype(jnp.int32).reshape(1)
    mine = lax.axis_index("head").astype(jnp.int32).reshape(1)
    shape = jax.ShapeDtypeStruct
    smem = pl.BlockSpec(memory_space=pltpu.SMEM)
    vmem = pl.BlockSpec(memory_space=pltpu.VMEM)
    params = pltpu.CompilerParams(vmem_limit_bytes=VMEM_LIMIT)
    by_rows = lambda rows, cols: pl.BlockSpec((rows, cols), lambda i: (i, 0))
    whole = lambda rows, cols: pl.BlockSpec((rows, cols), lambda *i: (0, 0))
    wide = tokens * channels
    cost = lambda work: pl.CostEstimate(flops=wide * work, bytes_accessed=wide * 16, transcendentals=0)
    grad_out = pltpu.with_memory_space_constraint(grad_out, pltpu.HBM)
    pre_x = pltpu.with_memory_space_constraint(pre_x, pltpu.HBM)
    pre_bc = pltpu.with_memory_space_constraint(pre_bc, pltpu.HBM)
    rows_f32, rows_bf16 = shape((tokens, channels), f32), shape((tokens, channels), bf16)
    bc_f32, bc_bf16 = shape((tokens, 2 * N), f32), shape((tokens, 2 * N), bf16)

    last_rows = lambda cols: pl.BlockSpec((16, cols), lambda i: (tokens // 16 - 1, 0))
    edge = pl.pallas_call(
        edge_kernel,
        grid=(1,),
        out_shape=shape((16, channels + 2 * N), bf16),
        in_specs=[last_rows(channels), last_rows(2 * N)],
        out_specs=whole(16, channels + 2 * N),
        compiler_params=params,
    )(pre_x, pre_bc)
    halo = shifted(edge, "seq", 1)

    scale, kappa, through = pl.pallas_call(
        scales_kernel,
        out_shape=(
            shape((tokens, width), bf16), shape((2 * chunks, channels), f32), shape((8, channels), f32),
        ),
        in_specs=[smem, smem, vmem],
        out_specs=(vmem,) * 3,
        scratch_shapes=[pltpu.VMEM((LANES, tokens), f32)],
        compiler_params=params,
        cost_estimate=cost(1000),
    )(lengths, start, log_decay)

    spread = pltpu.VMEM((width, channels), bf16)
    hi, lo, slope_bc, r_high, r_low, g_high, g_low, send_adjoint = pl.pallas_call(
        functools.partial(adjoint_kernel, heads=heads),
        grid=(steps,),
        out_shape=(bc_bf16, bc_bf16, bc_f32) + (rows_bf16,) * 4 + (shape((N + 8, channels), f32),),
        in_specs=[
            smem, smem, by_rows(big, channels), by_rows(big, width), by_rows(big, 2 * N),
            whole(16, channels + 2 * N), whole(K, 2 * N), whole(8, channels),
        ],
        out_specs=(by_rows(big, 2 * N),) * 3 + (by_rows(big, channels),) * 4 + (whole(N + 8, channels),),
        scratch_shapes=[spread, spread, pltpu.VMEM((big + 8, 2 * N), f32)],
        compiler_params=params,
        cost_estimate=cost(1000),
    )(lengths, start, grad_out, scale, pre_bc, halo, conv_bc, through)

    packed = (N * channels // LANES + 8, LANES)
    slope_x, q_high, q_low, x_high, x_low, own_state, *messages = pl.pallas_call(
        functools.partial(state_kernel, heads=heads, count=count),
        grid=(steps,),
        out_shape=(rows_f32,) + (rows_bf16,) * 4
        + (shape((N + 8, channels), f32),)
        + (shape(packed, f32),) * (count - 1),
        in_specs=[
            smem, smem, by_rows(big, channels), whole(16, channels + 2 * N), whole(K, channels),
            by_rows(big, width), by_rows(big, 2 * N), by_rows(big, 2 * N), whole(8, channels),
            whole(N + 8, channels),
        ],
        out_specs=(by_rows(big, channels),) * 5
        + (whole(N + 8, channels),)
        + (whole(*packed),) * (count - 1),
        scratch_shapes=[spread, spread, pltpu.VMEM((big + 8, channels), f32)],
        compiler_params=params,
        cost_estimate=cost(1000),
    )(lengths, start, pre_x, halo, conv_x, scale, hi, lo, through, send_adjoint)
    received = [
        lax.ppermute(message, "seq", [(i, (i + lag) % count) for i in range(count)])
        for lag, message in enumerate(messages, 1)
    ]

    from_end = lambda rows, cols: pl.BlockSpec((rows, cols), lambda i: (chunks - 1 - i, 0))
    both_ways = [
        place(CHUNK, size)
        for place in (by_rows, from_end)
        for size in (channels, channels, channels, channels, 2 * N, 2 * N)
    ]
    dx, dbc, rate = pl.pallas_call(
        functools.partial(local_kernel, heads=heads),
        grid=(chunks,),
        out_shape=(rows_f32, bc_f32, shape((tokens, LANES), f32)),
        in_specs=[smem, smem, whole(2 * chunks, channels)] + both_ways + [from_end(CHUNK, width)],
        out_specs=(from_end(CHUNK, channels), whole(tokens, 2 * N), whole(tokens, LANES)),
        scratch_shapes=[
            pltpu.VMEM((N, channels), f32), pltpu.VMEM((N, channels), f32),
            pltpu.VMEM((channels, LANES), bf16),
        ]
        + [pltpu.VMEM((4 * CHUNK, channels), bf16), spread],
        compiler_params=params,
        cost_estimate=cost(8000),
    )(lengths, start, kappa, *([q_high, q_low, r_high, r_low, hi, lo] * 2), scale)

    s2, a2, end, head = pl.pallas_call(
        functools.partial(entering_kernel, count=count, heads=heads, tokens=tokens),
        grid=(1,),
        out_shape=(
            shape((2 * N, channels), bf16), shape((2 * N, channels), bf16), shape((8, channels), f32),
            shape((8, channels + 2 * N), f32),
        ),
        in_specs=[smem]
        + [whole(*packed)] * (count - 1)
        + [whole(N + 8, channels)]
        + [whole(16, channels)] * 4
        + [whole(16, 2 * N)] * 2
        + [whole(16, width), whole(16, channels), whole(16, 2 * N), whole(16, channels), whole(16, 2 * N)],
        out_specs=(
            whole(2 * N, channels), whole(2 * N, channels), whole(8, channels),
            whole(8, channels + 2 * N),
        ),
        compiler_params=params,
        cost_estimate=cost(200),
    )(
        start, *received, own_state, g_high, g_low, x_high, x_low, hi, lo, scale, dx, dbc,
        slope_x, slope_bc,
    )
    after = shifted(head, "seq", -1)

    high = tokens
    shared = pl.pallas_call(
        shared_kernel,
        grid=(tokens // high,),
        out_shape=bc_f32,
        in_specs=[by_rows(high, channels)] * 4
        + [by_rows(high, 2 * N)] * 2
        + [whole(2 * N, channels)] * 2,
        out_specs=by_rows(high, 2 * N),
        compiler_params=params,
        cost_estimate=cost(1500),
    )(g_high, g_low, x_high, x_low, dbc, slope_bc, s2, a2)

    half = shape((tokens // 2, 2 * N), f32)
    keep, give = pl.pallas_call(
        functools.partial(arrange_kernel, sharers=sharers),
        out_shape=(half, half),
        in_specs=[smem, smem, smem, vmem, vmem, vmem],
        out_specs=(vmem, vmem),
        scratch_shapes=[pltpu.VMEM((tokens + 8, 2 * N), f32), pltpu.VMEM((tokens, 2 * N), f32)],
        compiler_params=params,
    )(lengths, start, mine, shared, after, conv_bc)
    grad_pre_bc = head_scatter(keep, give, mine, params)

    back = lambda rows, cols: pl.BlockSpec((rows, cols), lambda i: (steps - 1 - i, 0))
    grad_pre_x, grad_log = pl.pallas_call(
        functools.partial(final_kernel, heads=heads),
        grid=(steps,),
        out_shape=(rows_f32, shape((heads, tokens), f32)),
        in_specs=[smem, smem]
        + [back(big, channels)] * 4
        + [back(big, 2 * N)] * 2
        + [back(big, width)]
        + [back(big, channels)] * 2
        + [
            back(big, LANES), whole(2 * N, channels), whole(2 * N, channels),
            whole(K, channels), whole(8, channels + 2 * N), whole(8, channels),
        ],
        out_specs=(
            back(big, channels), pl.BlockSpec((heads, big), lambda i: (0, steps - 1 - i)),
        ),
        scratch_shapes=[
            pltpu.VMEM((LANES, LANES), f32), spread, pltpu.VMEM((channels, LANES), bf16),
            pltpu.VMEM((big + 8, channels), f32), pltpu.VMEM((2 * big, channels), bf16),
        ],
        compiler_params=params,
        cost_estimate=cost(3000),
    )(
        lengths, start, g_high, g_low, x_high, x_low, hi, lo, scale, dx, slope_x, rate, s2, a2,
        conv_x, after, end,
    )
    return (grad_pre_x, grad_pre_bc, grad_log)


def solution(mesh):
    placed = (
        P("seq", "head"),
        P("seq", None),
        P(None, "head"),
        P(),
        P("head", "seq"),
        P(),
        P("seq", "head"),
    )
    return jax.shard_map(
        local,
        mesh=mesh,
        in_specs=placed,
        out_specs=(P("seq", "head"), P(("seq", "head"), None), P("head", "seq")),
        check_vma=False,
    )
```
